32 devices in a mesh: ep: 16 (over z, x, core), tp: 2 (over y).
Axes of the slice: x: 2, y: 2, z: 4, core: 2. Of those that a mesh axis runs over, the one named last changes fastest.
Arguments:
- tokens: bfloat16 [8192, 1280], P(('ep', 'tp')), may hold values from -6 to 6
- cotangent: bfloat16 [8192, 1280], P(('ep', 'tp')), may hold values from -6 to 6
- segments: int32 [32, 256], P(('ep', 'tp')), may hold values from 0 to 3, never falling along the last dimension, each value on 1 to 128 neighbouring positions
- routes: int32 [8192, 7], P(('ep', 'tp')), may hold values from 0 to 15, all different within a row; in each aligned block of 256 rows (0 to 255, 256 to 511, ...) at most 128 rows name the same one
- gates: float32 [8192, 7], P(('ep', 'tp')), may hold values from 0.2 to 0.8
- qkv_weight: float32 [1280, 3840], P(('ep', 'tp')), may hold values from -0.15625 to 0.15625
- qkv_first: float32 [1280, 3840], P(('ep', 'tp')), may hold values from -0.00018310547 to 0.00018310547
- qkv_second: float32 [1280, 3840], P(('ep', 'tp')), may hold values from 3.5783887e-09 to 1.4178521e-08
- out_weight: float32 [1280, 1280], P(('ep', 'tp')), may hold values from -1 to 1
- out_first: float32 [1280, 1280], P(('ep', 'tp')), may hold values from -0.00018310547 to 0.00018310547
- out_second: float32 [1280, 1280], P(('ep', 'tp')), may hold values from 4.4561066e-10 to 1.7554359e-09
- shared_in: float32 [1280, 1792], P(('ep', 'tp')), may hold values from -0.15625 to 0.15625
- shared_in_first: float32 [1280, 1792], P(('ep', 'tp')), may hold values from -0.00018310547 to 0.00018310547
- shared_in_second: float32 [1280, 1792], P(('ep', 'tp')), may hold values from 3.5783887e-09 to 1.4178521e-08
- shared_out: float32 [896, 1280], P(('ep', 'tp')), may hold values from -0.1875 to 0.1875
- shared_out_first: float32 [896, 1280], P(('ep', 'tp')), may hold values from -0.00018310547 to 0.00018310547
- shared_out_second: float32 [896, 1280], P(('ep', 'tp')), may hold values from 7.1567774e-10 to 2.8357041e-09
- expert_in: float32 [16, 2, 896, 1280], P('ep', None, 'tp'), may hold values from -0.15625 to 0.15625
- expert_in_first: float32 [16, 2, 896, 1280], P('ep', None, 'tp'), may hold values from -5.340576e-05 to 5.340576e-05
- expert_in_second: float32 [16, 2, 896, 1280], P('ep', None, 'tp'), may hold values from 3.13109e-10 to 1.2406206e-09
- expert_out: float32 [16, 896, 1280], P('ep', 'tp'), may hold values from -0.6781754 to 0.6781754
- expert_out_first: float32 [16, 896, 1280], P('ep', 'tp'), may hold values from -5.340576e-05 to 5.340576e-05
- expert_out_second: float32 [16, 896, 1280], P('ep', 'tp'), may hold values from 3.13109e-10 to 1.2406206e-09
- norm_gains: float32 [2, 1280], P(None, ('ep', 'tp')), may hold values from 0.36 to 2.82
- gains_first: float32 [2, 1280], P(None, ('ep', 'tp')), may hold values from -0.0008544922 to 0.0008544922
- gains_second: float32 [2, 1280], P(None, ('ep', 'tp')), may hold values from 8.7771795e-08 to 3.5783887e-07
Outputs:
- block_out: bfloat16 [8192, 1280], P(('ep', 'tp'))
- tokens_grad: float32 [8192, 1280], P(('ep', 'tp'))
- grad_norm: float32 [], replicated
- qkv_new: float32 [1280, 3840], P(('ep', 'tp'))
- qkv_first_new: float32 [1280, 3840], P(('ep', 'tp'))
- qkv_second_new: float32 [1280, 3840], P(('ep', 'tp'))
- qkv_copy: bfloat16 [1280, 3840], P(('ep', 'tp'))
- out_new: float32 [1280, 1280], P(('ep', 'tp'))
- out_first_new: float32 [1280, 1280], P(('ep', 'tp'))
- out_second_new: float32 [1280, 1280], P(('ep', 'tp'))
- out_copy: bfloat16 [1280, 1280], P(('ep', 'tp'))
- shared_in_new: float32 [1280, 1792], P(('ep', 'tp'))
- shared_in_first_new: float32 [1280, 1792], P(('ep', 'tp'))
- shared_in_second_new: float32 [1280, 1792], P(('ep', 'tp'))
- shared_in_copy: bfloat16 [1280, 1792], P(('ep', 'tp'))
- shared_out_new: float32 [896, 1280], P(('ep', 'tp'))
- shared_out_first_new: float32 [896, 1280], P(('ep', 'tp'))
- shared_out_second_new: float32 [896, 1280], P(('ep', 'tp'))
- shared_out_copy: bfloat16 [896, 1280], P(('ep', 'tp'))
- expert_in_new: float32 [16, 2, 896, 1280], P('ep', None, 'tp')
- expert_in_first_new: float32 [16, 2, 896, 1280], P('ep', None, 'tp')
- expert_in_second_new: float32 [16, 2, 896, 1280], P('ep', None, 'tp')
- expert_in_copy: bfloat16 [16, 2, 896, 1280], P('ep', None, 'tp')
- expert_out_new: float32 [16, 896, 1280], P('ep', 'tp')
- expert_out_first_new: float32 [16, 896, 1280], P('ep', 'tp')
- expert_out_second_new: float32 [16, 896, 1280], P('ep', 'tp')
- expert_out_copy: bfloat16 [16, 896, 1280], P('ep', 'tp')
- gains_new: float32 [2, 1280], P(None, ('ep', 'tp'))
- gains_first_new: float32 [2, 1280], P(None, ('ep', 'tp'))
- gains_second_new: float32 [2, 1280], P(None, ('ep', 'tp'))
- gains_copy: bfloat16 [2, 1280], P(None, ('ep', 'tp'))
The draws below stay inside these ranges and needn't reach their ends.
Inputs may be any that keep to these rules, and one draw needn't show every extreme that they name: `routes`: each row names 7 different experts; among the 256 rows of one device no expert is named more than 128 times, a bound that some block reaches. `segments`: along each row the document number never falls; each document holds 1 to 128 tokens, one exactly 128.
All inputs are finite; a program needn't handle non-finite values.
Results may differ from the reference program's by a relative error of at most 0.017.
The reference program's roundings to bfloat16 on the way count: a program that leaves them out, or rounds other values in their place, can miss the bound.
Values may be sent and summed in bfloat16 or wider, within the bound.
A program may use at most 384 MiB of HBM per device.

```python
import math
import jax
import jax.numpy as jnp
import numpy as np
from jax import lax

D = 1280
HEADS = 10
HDIM = 128
FF = 896
TOPK = 7
TOK_DEV = 256
DOCS = 4
STEP = 10
SEQS = 32
TOKENS = 8192
EXPERTS = 16
CAP = 128
DOC_MOST = 128


def ramp_factor(length, lowest, spread):
    return lowest + spread * jnp.arange(length, dtype=jnp.float32) / (length - 1)


def draw_norm_gains(key, part):
    key = jax.random.fold_in(key, 11)
    rising = ramp_factor(D, 0.6, 1.2)
    jitter = jax.random.uniform(key, (2, D), jnp.float32, 0.8, 1.25)
    return rising[None, :] * jitter


def draw_expert_out(key, part):
    key = jax.random.fold_in(key, 12)
    lowest = 0.6
    spread = 1.2
    normal_part = jnp.clip(jax.random.normal(key, (EXPERTS, FF, D), jnp.float32), -4.0, 4.0) * FF ** (-0.5)
    by_expert = ramp_factor(EXPERTS, lowest, spread)[:, None, None]
    by_unit = ramp_factor(FF, lowest, spread)[None, :, None]
    return normal_part * by_expert * by_unit


def levels(own_key, extent, split, least, top_value):
    def one(dim, blocks):
        heights = jax.random.uniform(jax.random.fold_in(jax.random.fold_in(own_key, 6), dim), (blocks,), jnp.float32, least / len(split), top_value / len(split))
        return jnp.repeat(jnp.exp(heights), extent[dim] // blocks).reshape((-1,) + (1,) * (len(extent) - dim - 1))

    gain = one(*split[0])
    for cut in split[1:]:
        gain = gain * one(*cut)
    return gain


def length_profile(number_of, total, most, skew):
    weights = [(1 << 20) // math.isqrt(standing ** skew) + 1 for standing in range(2, number_of + 1)]
    surplus, holding = total - most - (number_of - 1), [1] * (number_of - 1)
    while surplus > 0:
        free = [i for i in range(number_of - 1) if holding[i] < most]
        whole, budget = sum([weights[i] for i in free]), surplus
        for i in free:
            addition = min(most - holding[i], max(1, budget * weights[i] // whole), surplus)
            holding[i] = holding[i] + addition
            surplus = surplus - addition
    return np.array([most] + holding)


def ragged(key, number_of, total, limit, slope):
    if number_of == 2:
        one = jax.random.randint(key, (), max(1, total - limit), min(limit, total - 1) + 1)
        return jnp.stack([one, total - one])
    tallies = jnp.asarray(length_profile(number_of, total, limit, slope), jnp.int32)
    pairs = (number_of - 1) // 2
    source_of, sink = tallies[1:1 + 2 * pairs:2], tallies[2:2 + 2 * pairs:2]
    margin = jnp.minimum(source_of - 1, limit - sink)
    shifted = jax.random.randint(jax.random.fold_in(key, 1), (pairs,), 0, 1 << 20) % (margin + 1)
    tallies = tallies.at[1:1 + 2 * pairs:2].set(source_of - shifted).at[2:2 + 2 * pairs:2].set(sink + shifted)
    return tallies[jax.random.permutation(jax.random.fold_in(key, 2), number_of)]


def routed_block(key, own, number, rows, count, top, bound, slope):
    order = jax.random.permutation(key, count)
    crowded, ordinary = shares(count, rows * top, bound, slope, True), shares(count, rows * top, bound, slope, False)
    places = jnp.arange(count)

    def named(sizes, turn):
        used = int((sizes > 0).sum())
        fixed = max(1, used // 4)
        shifted = fixed + (places - fixed + turn * (used - fixed)) % max(1, count - fixed)
        return jnp.zeros((count,), jnp.int32).at[order[jnp.where(places < fixed, places, shifted)]].set(jnp.asarray(sizes, jnp.int32))

    sizes = jnp.where(number % 4 == 0, named(crowded, number // 4), named(ordinary, number - number // 4 - 1))
    mixed = jax.random.permutation(jax.random.fold_in(own, 3), count)
    giver, receiver = mixed[0:count // 2 * 2:2], mixed[1:count // 2 * 2:2]
    slack = jnp.minimum(sizes[giver] - 1, bound - sizes[receiver]) // 2
    slack = jnp.where((giver == order[0]) | (receiver == order[0]) | (sizes[receiver] == 0), 0, jnp.maximum(slack, 0))
    shifted = jax.random.randint(jax.random.fold_in(own, 4), (count // 2,), 0, 1 << 20) % (slack + 1)
    sizes = sizes.at[giver].add(-shifted).at[receiver].add(shifted)
    items = jnp.searchsorted(jnp.cumsum(sizes), jnp.arange(rows * top), side="right").astype(jnp.int32)
    table = items.reshape(top, rows).T
    table = table[jax.random.permutation(jax.random.fold_in(own, 1), rows)]
    turn = jax.random.randint(jax.random.fold_in(own, 2), (rows, 1), 0, top)
    return jnp.take_along_axis(table, (jnp.arange(top)[None, :] + turn) % top, axis=1)


def shares(count, total, most, skew, full):
    portions = [(1 << 20) // math.isqrt(grade ** skew) + 1 for grade in range(1, count + 1)]
    largest = most if full else min(most, max(-(-total // count), total * portions[0] // sum(portions)))
    least = 1 if total - largest >= count - 1 else 0
    holding, spare = [largest] + [least] * (count - 1), total - largest - least * (count - 1)
    while spare > 0:
        candidates = [i for i in range(1, count) if holding[i] < largest] or [i for i in range(1, count) if holding[i] < most]
        mass, budget = sum([portions[i] for i in candidates]), spare
        for i in candidates:
            extra = min(most - holding[i], max(1, budget * portions[i] // mass), spare)
            holding[i] = holding[i] + extra
            spare = spare - extra
    return np.array(holding)


def noise(rng, extent, scale, most, shards=(), held_as=jnp.bfloat16):
    drawn = jax.random.normal(rng, extent, jnp.float32) * scale
    if len(shards) > 0:
        drawn = levels(rng, extent, shards, -0.22, 0.18) * drawn
    return jnp.clip(drawn, min=-most, max=most).astype(held_as)


def setup_inputs(seed: int = 0) -> dict:
    splits = jax.random.split(jax.random.key(seed), 27)
    tokens = noise(splits[0], (TOKENS, D), 1.0, 6.0, ((0, 32),))
    cotangent = noise(splits[1], (TOKENS, D), 1.0, 6.0, ((0, 32),))
    segments = jax.vmap(lambda own: jnp.searchsorted(jnp.cumsum(ragged(own, DOCS, TOK_DEV, DOC_MOST, 1)), jnp.arange(TOK_DEV), side="right"))(jax.random.split(splits[2], SEQS)).reshape((SEQS, TOK_DEV)).astype(jnp.int32)
    routes_keys = jax.random.split(jax.random.fold_in(splits[3], 1), TOKENS // TOK_DEV)
    routes_turns = jax.random.permutation(jax.random.fold_in(splits[3], 3), TOKENS // TOK_DEV)
    routes = jax.vmap(lambda own, number: routed_block(jax.random.fold_in(splits[3], 2), own, number, TOK_DEV, EXPERTS, TOPK, CAP, 1))(routes_keys, routes_turns).reshape((TOKENS, TOPK))
    gates = jnp.clip(jnp.exp(math.log(0.8) - 1.3862944 * jax.random.uniform(splits[4], (TOKENS, TOPK), jnp.float32) ** levels(splits[4], (TOKENS, TOPK), ((0, 32),), -0.2, 0.2)), 0.2, 0.8)
    qkv_weight = noise(splits[5], (D, 3 * D), D ** -0.5, 0.15625, ((0, 32),), jnp.float32)
    qkv_first = noise(splits[6], (D, 3 * D), (0.11 * (4 * D * D + 3 * D * FF + 0.6 * TOPK * D * FF) ** -0.5), 0.00018310547, ((0, 32),), jnp.float32)
    qkv_second = jnp.clip(jnp.exp(math.log(1.417852057983282e-08) - 1.3768156 * jax.random.uniform(splits[7], (D, 3 * D), jnp.float32) ** levels(splits[7], (D, 3 * D), ((0, 32),), -0.2, 0.2)), 3.5783886964679823e-09, 1.417852057983282e-08)
    out_weight = noise(splits[8], (D, D), (D * 8 // TOK_DEV) ** -0.5, 1.0, ((0, 32),), jnp.float32)
    out_first = noise(splits[9], (D, D), (0.11 * (4 * D * D + 3 * D * FF + 0.6 * TOPK * D * FF) ** -0.5), 0.00018310547, ((0, 32),), jnp.float32)
    out_second = jnp.clip(jnp.exp(math.log(1.7554359077465165e-09) - 1.3710269 * jax.random.uniform(splits[10], (D, D), jnp.float32) ** levels(splits[10], (D, D), ((0, 32),), -0.2, 0.2)), 4.4561065948300893e-10, 1.7554359077465165e-09)
    shared_in = noise(splits[11], (D, 2 * FF), D ** -0.5, 0.15625, ((0, 32),), jnp.float32)
    shared_in_first = noise(splits[12], (D, 2 * FF), (0.11 * (4 * D * D + 3 * D * FF + 0.6 * TOPK * D * FF) ** -0.5), 0.00018310547, ((0, 32),), jnp.float32)
    shared_in_second = jnp.clip(jnp.exp(math.log(1.417852057983282e-08) - 1.3768156 * jax.random.uniform(splits[13], (D, 2 * FF), jnp.float32) ** levels(splits[13], (D, 2 * FF), ((0, 32),), -0.2, 0.2)), 3.5783886964679823e-09, 1.417852057983282e-08)
    shared_out = noise(splits[14], (FF, D), FF ** -0.5, 0.1875, ((0, 32),), jnp.float32)
    shared_out_first = noise(splits[15], (FF, D), (0.11 * (4 * D * D + 3 * D * FF + 0.6 * TOPK * D * FF) ** -0.5), 0.00018310547, ((0, 32),), jnp.float32)
    shared_out_second = jnp.clip(jnp.exp(math.log(2.835704115966564e-09) - 1.3768156 * jax.random.uniform(splits[16], (FF, D), jnp.float32) ** levels(splits[16], (FF, D), ((0, 32),), -0.2, 0.2)), 7.156777392935965e-10, 2.835704115966564e-09)
    expert_in = noise(splits[17], (EXPERTS, 2, FF, D), D ** -0.5, 0.15625, ((0, 16), (2, 2)), jnp.float32)
    expert_in_first = noise(splits[18], (EXPERTS, 2, FF, D), (0.05 * (TOPK * EXPERTS ** -1) ** 0.5 * (4 * D * D + 3 * D * FF + 0.6 * TOPK * D * FF) ** -0.5), 5.340576171875e-05, ((0, 16), (2, 2)), jnp.float32)
    expert_in_second = jnp.clip(jnp.exp(math.log(1.240620606246523e-09) - 1.3768156 * jax.random.uniform(splits[19], (EXPERTS, 2, FF, D), jnp.float32) ** levels(splits[19], (EXPERTS, 2, FF, D), ((0, 16), (2, 2)), -0.2, 0.2)), 3.1310901094094845e-10, 1.240620606246523e-09)
    expert_out = draw_expert_out(jax.random.fold_in(splits[26], 71), 0)
    expert_out_first = noise(splits[21], (EXPERTS, FF, D), (0.05 * (TOPK * EXPERTS ** -1) ** 0.5 * (4 * D * D + 3 * D * FF + 0.6 * TOPK * D * FF) ** -0.5), 5.340576171875e-05, ((0, 16), (1, 2)), jnp.float32)
    expert_out_second = jnp.clip(jnp.exp(math.log(1.240620606246523e-09) - 1.3768156 * jax.random.uniform(splits[22], (EXPERTS, FF, D), jnp.float32) ** levels(splits[22], (EXPERTS, FF, D), ((0, 16), (1, 2)), -0.2, 0.2)), 3.1310901094094845e-10, 1.240620606246523e-09)
    norm_gains = draw_norm_gains(jax.random.fold_in(splits[26], 71), 0)
    gains_first = noise(splits[24], (2, D), (0.55 * (4 * D * D + 3 * D * FF + 0.6 * TOPK * D * FF) ** -0.5), 0.0008544922, ((1, 32),), jnp.float32)
    gains_second = jnp.clip(jnp.exp(math.log(3.5783887142315507e-07) - 1.4053426 * jax.random.uniform(splits[25], (2, D), jnp.float32) ** levels(splits[25], (2, D), ((1, 32),), -0.2, 0.2)), 8.777179516528122e-08, 3.5783887142315507e-07)
    return {"tokens": tokens, "cotangent": cotangent, "segments": segments, "routes": routes, "gates": gates, "qkv_weight": qkv_weight, "qkv_first": qkv_first, "qkv_second": qkv_second, "out_weight": out_weight, "out_first": out_first, "out_second": out_second, "shared_in": shared_in, "shared_in_first": shared_in_first, "shared_in_second": shared_in_second, "shared_out": shared_out, "shared_out_first": shared_out_first, "shared_out_second": shared_out_second, "expert_in": expert_in, "expert_in_first": expert_in_first, "expert_in_second": expert_in_second, "expert_out": expert_out, "expert_out_first": expert_out_first, "expert_out_second": expert_out_second, "norm_gains": norm_gains, "gains_first": gains_first, "gains_second": gains_second}


PRECISE = lax.Precision.HIGHEST
NEG_BIG = -1000000000.0
NORM_EPS = 1e-06
ROPE_BASE = 10000.0
CLIP_LEVEL = 1.0
BETA_ONE = 0.9
BETA_TWO = 0.95
ADAM_EPS = 1e-08
WEIGHT_DECAY = 0.1
MATRIX_RATE = 0.05
GAIN_RATE = 0.5

@jax.custom_vjp
def low(v):
    return lax.optimization_barrier(v.astype(jnp.bfloat16)).astype(jnp.float32)

@jax.custom_vjp
def low_back(v):
    return v

def low_keep(v):
    return (low(v), None)

def low_pass(kept, grad):
    return (grad,)

def back_keep(v):
    return (v, None)

def back_low(kept, grad):
    return (low(grad),)
low.defvjp(low_keep, low_pass)
low_back.defvjp(back_keep, back_low)

def normalize(values):
    return values * lax.rsqrt(lax.optimization_barrier(jnp.mean(values * values, axis=-1, keepdims=True)) + NORM_EPS)

def rope_tables(length):
    places = jnp.arange(length, dtype=jnp.float32)
    frequencies = ROPE_BASE ** (-jnp.arange(HDIM // 2, dtype=jnp.float32) * (2.0 / HDIM))
    angles = places[:, None] * frequencies[None, :]
    return (jnp.cos(angles), jnp.sin(angles))

def rotate(values, cosine, sine_table):
    middle = values.shape[-1] // 2
    former = values[..., :middle]
    latter = values[..., middle:]
    return jnp.concatenate([former * cosine - latter * sine_table, latter * cosine + former * sine_table], axis=-1)

def attend(queries, keys_in, values_in, segment_row):
    scores = jnp.einsum('shw,thw->hst', queries, keys_in, precision=PRECISE) * HDIM ** (-0.5)
    scores = low_back(scores)
    places = jnp.arange(segment_row.shape[0])
    allowed = (places[:, None] >= places[None, :]) & (segment_row[:, None] == segment_row[None, :])
    scores = jnp.where(allowed[None], scores, NEG_BIG)
    highest = lax.optimization_barrier(jnp.max(scores, axis=-1, keepdims=True))
    weights = jnp.exp(scores - highest)
    probabilities = weights / lax.optimization_barrier(jnp.sum(weights, axis=-1, keepdims=True))
    return jnp.einsum('hst,thw->shw', low(probabilities), values_in, precision=PRECISE)

def forward(tokens, qkv_weight, out_weight, shared_in, shared_out, expert_in, expert_out, norm_gains, segments, mixing):
    tok_count = tokens.shape[0]
    gains_low = low(norm_gains)
    normed_one = low(normalize(tokens) * gains_low[0])
    projected = low_back(jnp.dot(normed_one, low(qkv_weight), precision=PRECISE))
    shaped = projected.reshape(tok_count // TOK_DEV, TOK_DEV, 3, HEADS, HDIM)
    cosine, sine_table = rope_tables(TOK_DEV)
    cosine = cosine[:, None, :]
    sine_table = sine_table[:, None, :]
    queries = low(rotate(shaped[:, :, 0], cosine, sine_table))
    keys_all = low(rotate(shaped[:, :, 1], cosine, sine_table))
    values_all = low(shaped[:, :, 2])
    checked = jax.checkpoint(attend)
    attended = lax.map(lambda packed: checked(packed[0], packed[1], packed[2], packed[3]), (queries, keys_all, values_all, segments))
    attended = low(low_back(attended.reshape(tok_count, D)))
    branch = low_back(jnp.dot(attended, low(out_weight), precision=PRECISE))
    hidden = tokens + branch
    normed_two = low(normalize(hidden) * gains_low[1])
    shared_pre = low_back(jnp.dot(normed_two, low(shared_in), precision=PRECISE))
    shared_act = low(jax.nn.silu(shared_pre[:, :FF]) * shared_pre[:, FF:])
    shared_res = low_back(jnp.dot(shared_act, low(shared_out), precision=PRECISE))

    def expert_step(running, packed):
        weights_in, weights_out, weighting = packed
        inputs = low_back(normed_two)
        gate_pre = low_back(jnp.dot(inputs, low(weights_in[0]).T, precision=PRECISE))
        up_pre = low_back(jnp.dot(inputs, low(weights_in[1]).T, precision=PRECISE))
        active = low(jax.nn.silu(gate_pre) * up_pre)
        result = low(low_back(jnp.dot(active, low(weights_out), precision=PRECISE)))
        return (running + weighting[:, None] * result, None)
    initial = jnp.zeros((tok_count, D), jnp.float32)
    routed, unused = lax.scan(jax.checkpoint(expert_step), initial, (expert_in, expert_out, mixing.T))
    return hidden + shared_res + routed

def adam_update(weight, gradient, first, second, clip_scale, rate, decay):
    clipped = gradient * clip_scale
    first_new = BETA_ONE * first + (1.0 - BETA_ONE) * clipped
    second_new = BETA_TWO * second + (1.0 - BETA_TWO) * clipped * clipped
    corr_one = 1.0 - BETA_ONE ** STEP
    corr_two = 1.0 - BETA_TWO ** STEP
    stepped = first_new / corr_one / (jnp.sqrt(second_new / corr_two) + ADAM_EPS)
    weight_new = weight - rate * (stepped + decay * weight)
    return (weight_new, first_new, second_new, weight_new.astype(jnp.bfloat16))

def reference(tokens, cotangent, segments, routes, gates, qkv_weight, qkv_first, qkv_second, out_weight, out_first, out_second, shared_in, shared_in_first, shared_in_second, shared_out, shared_out_first, shared_out_second, expert_in, expert_in_first, expert_in_second, expert_out, expert_out_first, expert_out_second, norm_gains, gains_first, gains_second):
    experts_iota = jnp.arange(EXPERTS, dtype=jnp.int32)
    chosen = (routes[:, :, None] == experts_iota[None, None, :]).astype(jnp.float32)
    mixing = lax.optimization_barrier(jnp.sum(gates[:, :, None] * chosen, axis=1))

    def wrapped(tok_float, qkv_arg, out_arg, shin_arg, shout_arg, exin_arg, exout_arg, gains_arg):
        return forward(tok_float, qkv_arg, out_arg, shin_arg, shout_arg, exin_arg, exout_arg, gains_arg, segments, mixing)
    output, pullback = jax.vjp(wrapped, tokens.astype(jnp.float32), qkv_weight, out_weight, shared_in, shared_out, expert_in, expert_out, norm_gains)
    tokens_grad, qkv_grad, out_grad, shin_grad, shout_grad, exin_grad, exout_grad, gains_grad = pullback(cotangent.astype(jnp.float32))
    squares = jnp.sum(qkv_grad * qkv_grad) + jnp.sum(out_grad * out_grad) + jnp.sum(shin_grad * shin_grad)
    squares = squares + jnp.sum(shout_grad * shout_grad) + jnp.sum(exin_grad * exin_grad)
    squares = squares + jnp.sum(exout_grad * exout_grad) + jnp.sum(gains_grad * gains_grad)
    grad_norm = jnp.sqrt(squares)
    clip_scale = jnp.minimum(1.0, CLIP_LEVEL / (grad_norm + 1e-06))
    qkv_new, qkv_first_new, qkv_second_new, qkv_copy = adam_update(qkv_weight, qkv_grad, qkv_first, qkv_second, clip_scale, MATRIX_RATE, WEIGHT_DECAY)
    out_new, out_first_new, out_second_new, out_copy = adam_update(out_weight, out_grad, out_first, out_second, clip_scale, MATRIX_RATE, WEIGHT_DECAY)
    shin_new, shin_first_new, shin_second_new, shin_copy = adam_update(shared_in, shin_grad, shared_in_first, shared_in_second, clip_scale, MATRIX_RATE, WEIGHT_DECAY)
    shout_new, shout_first_new, shout_second_new, shout_copy = adam_update(shared_out, shout_grad, shared_out_first, shared_out_second, clip_scale, MATRIX_RATE, WEIGHT_DECAY)
    exin_new, exin_first_new, exin_second_new, exin_copy = adam_update(expert_in, exin_grad, expert_in_first, expert_in_second, clip_scale, MATRIX_RATE, WEIGHT_DECAY)
    exout_new, exout_first_new, exout_second_new, exout_copy = adam_update(expert_out, exout_grad, expert_out_first, expert_out_second, clip_scale, MATRIX_RATE, WEIGHT_DECAY)
    gains_new, gains_first_new, gains_second_new, gains_copy = adam_update(norm_gains, gains_grad, gains_first, gains_second, clip_scale, GAIN_RATE, 0.0)
    return (output.astype(jnp.bfloat16), tokens_grad, grad_norm, qkv_new, qkv_first_new, qkv_second_new, qkv_copy, out_new, out_first_new, out_second_new, out_copy, shin_new, shin_first_new, shin_second_new, shin_copy, shout_new, shout_first_new, shout_second_new, shout_copy, exin_new, exin_first_new, exin_second_new, exin_copy, exout_new, exout_first_new, exout_second_new, exout_copy, gains_new, gains_first_new, gains_second_new, gains_copy)
```

```python
import functools
import jax
import jax.numpy as jnp
from jax import lax
from jax.experimental import pallas as pl
from jax.experimental.pallas import tpu as pltpu
from jax.sharding import PartitionSpec as P

HEADS = 10
HDIM = 128
FF = 896
TOPK = 7
STEP = 10


MESH = pl.DeviceIdType.MESH
VMEM_MOST = 60 * 1024 * 1024
NEG_BIG = -1000000000.0
NORM_EPS = 1e-06
ROPE_BASE = 10000.0
CLIP_LEVEL = 1.0
BETA_ONE = 0.9
BETA_TWO = 0.95
ADAM_EPS = 1e-08
WEIGHT_DECAY = 0.1
MATRIX_RATE = 0.05
GAIN_RATE = 0.5


class Place:
    def __init__(self, ep_count, tp_count):
        chips = ep_count // 2
        nb = 1
        while nb * nb * 4 <= chips:
            nb *= 2
        self.nb, self.na, self.nt = nb, chips // nb, tp_count
        self.ep_count = ep_count
        e = lax.axis_index("ep")
        self.t = lax.axis_index("tp")
        self.core = lax.rem(e, 2)
        self.b = lax.rem(e // 2, nb)
        self.a = e // (2 * nb)

    def dims(self, whole):
        if not whole:
            return (("a", self.na), ("b", self.nb))
        if self.nb == self.nt:
            return (("a", self.na), ("u", self.nb), ("v", self.nt))
        return (("a", self.na), ("b", self.nb), ("t", self.nt))

    def own(self, name):
        even = self.core == 0
        if name == "u":
            return jnp.where(even, self.b, self.t)
        if name == "v":
            return jnp.where(even, self.t, self.b)
        return getattr(self, name)

    def chip(self, at):
        a = at.get("a", self.a)
        b, t = at.get("b", self.b), at.get("t", self.t)
        if "u" in at:
            even = self.core == 0
            b = jnp.where(even, at["u"], at["v"])
            t = jnp.where(even, at["v"], at["u"])
        return a, b, t

    def device(self, at, core):
        a, b, t = self.chip(at)
        return ((a * self.nb + b) * 2 + core, t)

    def index(self, at, core, whole):
        e, t = self.device(at, core)
        return e * self.nt + t if whole else e

    def slot(self, at, whole):
        a, b, t = self.chip(at)
        chip = a * self.nb + b
        return chip * self.nt + t if whole else chip


def shifts(extent):
    if extent == 2:
        return [0, 1]
    found = [0]
    for step in range(1, extent):
        found += [step, -step]
    return found


def moved(own, shift, extent):
    if shift == 0:
        return own, None
    if extent == 2:
        return 1 - own, None
    there = own + shift
    return there, (there >= 0) & (there < extent)


def both(one, other):
    if one is None:
        return other
    return one if other is None else one & other


def guarded(condition, body):
    if condition is None:
        body()
    else:
        pl.when(condition)(body)


def sides(extent):
    return [1] if extent == 2 else [1, -1]


def greet(place, whole):
    barrier = pltpu.get_barrier_semaphore()
    here = {name: place.own(name) for name, _ in place.dims(whole)}
    pl.semaphore_signal(barrier, inc=1, device_id=place.device(here, 1 - place.core), device_id_type=MESH)
    count = jnp.int32(1)
    for name, extent in place.dims(whole):
        for side in sides(extent):
            there, on = moved(here[name], side, extent)
            target = place.device({**here, name: there}, place.core)

            def signal(target=target):
                pl.semaphore_signal(barrier, inc=1, device_id=target, device_id_type=MESH)

            guarded(on, signal)
            count = count + (1 if on is None else on.astype(jnp.int32))
    pl.semaphore_wait(barrier, count)


def relative_blocks(dims):
    blocks = [()]
    for _, extent in dims:
        blocks = [block + (shift,) for block in blocks for shift in shifts(extent)]
    return blocks


def gather_events(place, whole, pairs, send_sems, recv_sems):
    dims = place.dims(whole)
    here = {name: place.own(name) for name, _ in dims}
    counter = [0]
    ends = []
    starts = []

    def copies(at, target, core_of_block, own):
        index = place.index(at, core_of_block, whole)
        number = counter[0]
        counter[0] += 1
        made = []
        for k, (block, gathered) in enumerate(pairs):
            made.append(
                pltpu.make_async_remote_copy(
                    src_ref=block if own else gathered.at[index],
                    dst_ref=gathered.at[index],
                    send_sem=send_sems.at[k, number],
                    recv_sem=recv_sems.at[k, index],
                    device_id=target,
                    device_id_type=MESH,
                )
            )
        return made

    def send(at, on, target, own, todo):
        made = copies(at, target, place.core, own)

        def start(made=made):
            for copy in made:
                copy.start()

        def finish(made=made):
            for copy in made:
                copy.wait_send()

        todo.append((on, start))
        ends.append((on, finish))

    steps = []
    for block in relative_blocks(dims):
        at, valid = dict(here), None
        for (name, extent), shift in zip(dims, block):
            at[name], on = moved(here[name], shift, extent)
            valid = both(valid, on)
        last = max([k for k, shift in enumerate(block) if shift], default=-1)
        own = last < 0
        todo = []
        for k in range(len(dims) - 1, -1, -1):
            name, extent = dims[k]
            if k < last:
                continue
            if k == last:
                if extent == 2:
                    continue
                ways = [-1 if block[k] > 0 else 1]
            else:
                ways = sides(extent)
            for way in ways:
                there, on = moved(here[name], way, extent)
                target = place.device({**here, name: there}, place.core)
                send(at, both(valid, on), target, own, todo)
        send(at, valid, place.device(here, 1 - place.core), own, todo)
        index = place.index(at, place.core, whole)

        def step(index=index, valid=valid, todo=todo, own=own):
            def body():
                if not own:
                    for k, (_, gathered) in enumerate(pairs):
                        pltpu.make_async_copy(gathered.at[index], gathered.at[index], recv_sems.at[k, index]).wait()

            guarded(valid, body)
            for on, start in todo:
                guarded(on, start)

        key = abs(block[0]) + sum(1.0 for s in block[1:] if s) + 0.1 * last
        steps.append((key, step))
        other = place.index(at, 1 - place.core, whole)

        def arrived(other=other):
            for k, (_, gathered) in enumerate(pairs):
                pltpu.make_async_copy(gathered.at[other], gathered.at[other], recv_sems.at[k, other]).wait()

        ends.append((valid, arrived))
    return steps, ends, counter[0]


def count_gather_sends(dims):
    total = 0
    for block in relative_blocks(dims):
        last = max([k for k, shift in enumerate(block) if shift], default=-1)
        for k, (_, extent) in enumerate(dims):
            if k > last:
                total += len(sides(extent))
            elif k == last and extent > 2:
                total += 1
        total += 1
    return total


def gather_kernel(ep_count, tp_count, groups, *refs):
    count = sum(n for _, n in groups)
    blocks, gathered, scratch = refs[:count], refs[count : 2 * count], refs[2 * count :]
    place = Place(ep_count, tp_count)
    greet(place, any(whole for whole, _ in groups))
    steps, ends, first = [], [], 0
    locals_ = []
    for g, (whole, n) in enumerate(groups):
        send_sems, recv_sems, own_sems = scratch[3 * g : 3 * g + 3]
        pairs = list(zip(blocks[first : first + n], gathered[first : first + n]))
        first += n
        more, finish, _ = gather_events(place, whole, pairs, send_sems, recv_sems)
        steps += more
        ends += finish
        here = {name: place.own(name) for name, _ in place.dims(whole)}
        mine = place.index(here, place.core, whole)
        for k, (block, out) in enumerate(pairs):
            locals_.append(pltpu.make_async_copy(block, out.at[mine], own_sems.at[k]))
    order = sorted(range(len(steps)), key=lambda i: steps[i][0])
    steps[order[0]][1]()
    for copy in locals_:
        copy.start()
    for i in order[1:]:
        steps[i][1]()
    for on, finish in ends:
        guarded(on, finish)
    for copy in locals_:
        copy.wait()


def gather(ep_count, tp_count, collective_id, name, whole_blocks, ep_blocks):
    groups, arrays, shapes, scratch = [], [], [], []
    place = Place(ep_count, tp_count)
    for whole, blocks in ((True, whole_blocks), (False, ep_blocks)):
        if not blocks:
            continue
        groups.append((whole, len(blocks)))
        total = ep_count * tp_count if whole else ep_count
        for block in blocks:
            arrays.append(block)
            shapes.append(jax.ShapeDtypeStruct((total,) + block.shape, block.dtype))
        sends = count_gather_sends(place.dims(whole))
        scratch += [
            pltpu.SemaphoreType.DMA((len(blocks), sends)),
            pltpu.SemaphoreType.DMA((len(blocks), total)),
            pltpu.SemaphoreType.DMA((len(blocks),)),
        ]
    return pl.pallas_call(
        functools.partial(gather_kernel, ep_count, tp_count, tuple(groups)),
        out_shape=tuple(shapes),
        in_specs=[pl.BlockSpec(memory_space=pl.ANY)] * len(arrays),
        out_specs=tuple([pl.BlockSpec(memory_space=pl.ANY)] * len(arrays)),
        scratch_shapes=scratch,
        compiler_params=pltpu.CompilerParams(collective_id=collective_id, has_side_effects=True),
        name=name,
    )(*arrays)


def add_into(target, sources, dtype):
    rows, columns = target.shape
    piece = 128
    while columns % (piece * 2) == 0 and rows * piece * 2 <= 40 * 1024:
        piece *= 2

    def body(i, carry):
        window = pl.ds(pl.multiple_of(i * piece, piece), piece)
        total = sources[0][:, window].astype(jnp.float32)
        for source in sources[1:]:
            total = total + source[:, window].astype(jnp.float32)
        target[:, window] = total.astype(dtype)
        return carry

    lax.fori_loop(0, columns // piece, body, 0)


def scatter_kernel(ep_count, tp_count, whole, count, *refs):
    partials, outs = refs[:count], refs[count : 2 * count]
    scratch = refs[2 * count :]
    place = Place(ep_count, tp_count)
    greet(place, whole)
    dims = place.dims(whole)
    here = {name: place.own(name) for name, _ in dims}
    owns = scratch[:count]
    sibs = scratch[count : 2 * count]
    lands = [scratch[2 * count + k * count : 2 * count + (k + 1) * count] for k in range(len(dims))]
    sems = scratch[2 * count + len(dims) * count :]
    own_sem, sib_send, sib_recv, line_send = sems[:4]
    line_recv, accs = sems[4 : 4 + len(dims)], sems[4 + len(dims) :]
    order = sorted(relative_blocks(dims), key=lambda block: -sum(abs(s) for s in block))
    order = sorted(order, key=lambda block: -max([k for k, s in enumerate(block) if s], default=-1))
    info = {}
    ends = []
    for block in order:
        at, valid = dict(here), None
        for (name, extent), shift in zip(dims, block):
            at[name], on = moved(here[name], shift, extent)
            valid = both(valid, on)
        slot = place.slot(at, whole)
        info[block] = (at, valid, slot)
        local = [
            pltpu.make_async_copy(
                partials[k].at[place.index(at, place.core, whole)], owns[k].at[slot], own_sem.at[k, slot]
            )
            for k in range(count)
        ]
        across = [
            pltpu.make_async_remote_copy(
                src_ref=partials[k].at[place.index(at, 1 - place.core, whole)],
                dst_ref=sibs[k].at[slot],
                send_sem=sib_send.at[k, slot],
                recv_sem=sib_recv.at[k, slot],
                device_id=place.device(here, 1 - place.core),
                device_id_type=MESH,
            )
            for k in range(count)
        ]

        def start(local=local, across=across):
            for copy in local + across:
                copy.start()

        def finish(across=across):
            for copy in across:
                copy.wait_send()

        guarded(valid, start)
        ends.append((valid, finish))
        info[block] += (local, across)

    def land_slot(level, at, shift, side):
        name, extent = dims[level]
        inner = 0
        for earlier, wide in dims[:level]:
            inner = inner * wide + at[earlier]
        wide = 1
        for _, e in dims[:level]:
            wide = wide * e
        if extent == 2:
            return inner
        place_on = at[name] if (shift != 0 or side < 0) else extent
        return place_on * wide + inner

    number = 0
    for block in order:
        at, valid, slot, local, across = info[block]
        last = max([k for k, shift in enumerate(block) if shift], default=-1)
        waits = []
        extra = []
        for level in range(len(dims) - 1, -1, -1):
            name, extent = dims[level]
            if level < last:
                break
            if level == last:
                if extent == 2:
                    continue
                froms = [-1 if block[level] > 0 else 1]
            elif extent == 2:
                froms = [1]
            else:
                froms = [-1, 1]
            for side in froms:
                _, on = moved(here[name], side, extent)
                spot = land_slot(level, at, block[level], side)
                extra.append((level, spot, on))

        def arrive(local=local, across=across):
            for copy in local:
                copy.wait()
            for copy in across:
                copy.wait_recv()

        guarded(valid, arrive)
        for k in range(count):
            sure = [owns[k].at[slot], sibs[k].at[slot]]
            maybe = []
            for level, spot, on in extra:
                ref = lands[level][k].at[spot]

                def wait(ref=ref, k=k, level=level, spot=spot):
                    pltpu.make_async_copy(ref, ref, line_recv[level].at[k, spot]).wait()

                guarded(both(valid, on), wait)
                if on is None:
                    sure.append(ref)
                else:
                    maybe.append((ref, on))
            if last >= 0:
                target, dtype = owns[k].at[slot], owns[k].dtype
            else:
                target, dtype = outs[k], outs[k].dtype

            def add(sure=sure, maybe=maybe, target=target, dtype=dtype, k=k):
                if not maybe:
                    add_into(target, sure, dtype)
                elif len(maybe) == 1:
                    (ref, on), = maybe
                    pl.when(on)(lambda: add_into(target, sure + [ref], dtype))
                    pl.when(jnp.logical_not(on))(lambda: add_into(target, sure, dtype))
                elif len(maybe) > 2:
                    acc = accs[k]
                    add_into(acc, sure, jnp.float32)
                    for ref, on in maybe:
                        pl.when(on)(functools.partial(add_into, acc, [acc, ref], jnp.float32))
                    add_into(target, [acc], dtype)
                else:
                    (low, on_low), (high, on_high) = maybe
                    pl.when(on_low & on_high)(lambda: add_into(target, sure + [low, high], dtype))
                    pl.when(on_low & jnp.logical_not(on_high))(lambda: add_into(target, sure + [low], dtype))
                    pl.when(on_high & jnp.logical_not(on_low))(lambda: add_into(target, sure + [high], dtype))

            guarded(valid, add)
        if last >= 0:
            name, extent = dims[last]
            way = 1 if block[last] > 0 else -1
            there, _ = moved(here[name], way, extent)
            arriving = 0 if extent == 2 else block[last] - way
            spot = land_slot(last, at, arriving, -way)
            made = [
                pltpu.make_async_remote_copy(
                    src_ref=owns[k].at[slot],
                    dst_ref=lands[last][k].at[spot],
                    send_sem=line_send.at[k, number],
                    recv_sem=line_recv[last].at[k, spot],
                    device_id=place.device({**here, name: there}, place.core),
                    device_id_type=MESH,
                )
                for k in range(count)
            ]
            number += 1

            def start(made=made):
                for copy in made:
                    copy.start()

            def finish(made=made):
                for copy in made:
                    copy.wait_send()

            guarded(valid, start)
            ends.append((valid, finish))
    for on, finish in ends:
        guarded(on, finish)


def scatter_add(ep_count, tp_count, collective_id, name, whole, partials):
    place = Place(ep_count, tp_count)
    dims = place.dims(whole)
    count = len(partials)
    slots = 1
    for _, extent in dims:
        slots *= extent
    blocks = [p.shape[1:] for p in partials]
    kinds = [p.dtype for p in partials]
    scratch = []
    for _ in range(2):
        scratch += [pltpu.VMEM((slots,) + b, d) for b, d in zip(blocks, kinds)]
    land_counts = []
    wide = 1
    for _, extent in dims:
        land_counts.append(wide if extent == 2 else (extent + 1) * wide)
        wide *= extent
    for lands in land_counts:
        scratch += [pltpu.VMEM((lands,) + b, d) for b, d in zip(blocks, kinds)]
    sends = sum(1 for block in relative_blocks(dims) if any(block))
    scratch += [pltpu.SemaphoreType.DMA((count, slots))] * 3 + [pltpu.SemaphoreType.DMA((count, sends))]
    scratch += [pltpu.SemaphoreType.DMA((count, lands)) for lands in land_counts]
    if sum(extent > 2 for _, extent in dims) > 1:
        scratch += [pltpu.VMEM(b, jnp.float32) for b in blocks]
    return pl.pallas_call(
        functools.partial(scatter_kernel, ep_count, tp_count, whole, count),
        out_shape=tuple(jax.ShapeDtypeStruct(b, jnp.float32) for b in blocks),
        in_specs=[pl.BlockSpec(memory_space=pl.ANY)] * count,
        out_specs=tuple([pl.BlockSpec(memory_space=pltpu.VMEM)] * count),
        scratch_shapes=scratch,
        compiler_params=pltpu.CompilerParams(
            collective_id=collective_id, has_side_effects=True, vmem_limit_bytes=VMEM_MOST
        ),
        name=name,
    )(*partials)


def expert_kernel(parts, per_step, cap, *refs):
    normed, cot, info = refs[:3]
    ins, outs_w = refs[3 : 3 + parts], refs[3 + parts : 3 + 2 * parts]
    result_ref, input_ref, own_grad = refs[3 + 2 * parts : 6 + 2 * parts]
    sent = refs[6 + 2 * parts : 5 + 3 * parts]
    scratch = refs[5 + 3 * parts :]
    rows_x, rows_g, gate_col, result_acc, input_acc = scratch[:5]
    sums = (own_grad,) + tuple(scratch[5:])
    step = pl.program_id(0)
    tok = normed.shape[1]
    width = normed.shape[2]
    chunk = 256

    @pl.when(step == 0)
    def _():
        for total in sums:
            total[...] = jnp.zeros_like(total)

    slots = lax.broadcasted_iota(jnp.int32, (cap, tok), 0).astype(jnp.float32)
    for s in range(per_step):
        hit = slots == info[s, 0:1, :]
        picks = jnp.where(hit, 1.0, 0.0).astype(jnp.bfloat16)
        gates = jnp.sum(jnp.where(hit, info[s, 1:2, :], 0.0), axis=1, keepdims=True)
        window = pl.ds(s * cap, cap)
        gate_col[window, :] = jnp.broadcast_to(gates, (cap, 128))
        rows_x[window, :] = jnp.dot(picks, normed[s], preferred_element_type=jnp.float32).astype(
            jnp.bfloat16
        )
        taken = jnp.dot(picks, cot[s], preferred_element_type=jnp.float32)
        rows_g[window, :] = (gates * taken).astype(jnp.bfloat16)
    across = (((1,), (1,)), ((), ()))
    down = (((0,), (0,)), ((), ()))

    def mul(left, right, dims):
        return lax.dot_general(left, right, dims, preferred_element_type=jnp.float32)

    straight = (((1,), (0,)), ((), ()))
    for p in range(parts):
        gate_pre = mul(rows_x[...], ins[p][0], across)
        up_pre = mul(rows_x[...], ins[p][1], across)
        sigmoid = jax.nn.sigmoid(gate_pre)
        active = (gate_pre * sigmoid * up_pre).astype(jnp.bfloat16)
        grad_act = mul(rows_g[...], outs_w[p][...], across)
        grad_up = (grad_act * gate_pre * sigmoid).astype(jnp.bfloat16)
        grad_gate = (grad_act * up_pre * sigmoid * (1.0 + gate_pre * (1.0 - sigmoid))).astype(
            jnp.bfloat16
        )
        for first in range(0, width, chunk):
            window = slice(first, first + chunk)
            result = mul(active, outs_w[p][:, window], straight)
            back = mul(grad_gate, ins[p][0, :, window], straight) + mul(
                grad_up, ins[p][1, :, window], straight
            )
            if p == 0:
                result_acc[:, window] = result
                input_acc[:, window] = back
            else:
                result_acc[:, window] += result
                input_acc[:, window] += back
            sums[p][0, :, window] += mul(grad_gate, rows_x[:, window], down)
            sums[p][1, :, window] += mul(grad_up, rows_x[:, window], down)
            sums[p][2, :, window] += mul(active, rows_g[:, window], down)
    for s in range(per_step):
        hit = slots == info[s, 0:1, :]
        picks = jnp.where(hit, 1.0, 0.0).astype(jnp.bfloat16)
        window = pl.ds(s * cap, cap)
        rounded = result_acc[window, :].astype(jnp.bfloat16).astype(jnp.float32)
        weighted = (gate_col[window, 0:1] * rounded).astype(jnp.bfloat16)
        result_ref[s] = mul(picks, weighted, down).astype(jnp.bfloat16)
        input_ref[s] = mul(picks, input_acc[window, :].astype(jnp.bfloat16), down).astype(
            jnp.bfloat16
        )

    @pl.when(step == pl.num_programs(0) - 1)
    def _():
        for p in range(1, parts):
            sent[p - 1][...] = sums[p][...].astype(jnp.bfloat16)


def expert_pass(normed_all, cot_all, info, ins, outs_w, cap):
    ep_count, tok, width = normed_all.shape
    parts = len(ins)
    hidden = ins[0].shape[1]
    per_step = max(1, min(ep_count, 256 // cap))
    rows = per_step * cap
    token_spec = pl.BlockSpec((per_step, tok, width), lambda i: (i, 0, 0))
    once = pl.Buffered(1)
    in_specs = [token_spec, token_spec, pl.BlockSpec((per_step, 2, tok), lambda i: (i, 0, 0))]
    in_specs += [
        pl.BlockSpec((2, hidden, width), lambda i: (0, 0, 0), pipeline_mode=once)
    ] * parts
    in_specs += [pl.BlockSpec((hidden, width), lambda i: (0, 0), pipeline_mode=once)] * parts
    grad_spec = pl.BlockSpec((3, hidden, width), lambda i: (0, 0, 0), pipeline_mode=once)
    token_shape = jax.ShapeDtypeStruct((ep_count, tok, width), jnp.bfloat16)
    out_shape = [token_shape, token_shape, jax.ShapeDtypeStruct((3, hidden, width), jnp.float32)]
    out_shape += [jax.ShapeDtypeStruct((3, hidden, width), jnp.bfloat16)] * (parts - 1)
    scratch = [
        pltpu.VMEM((rows, width), jnp.bfloat16),
        pltpu.VMEM((rows, width), jnp.bfloat16),
        pltpu.VMEM((rows, 128), jnp.float32),
        pltpu.VMEM((rows, width), jnp.float32),
        pltpu.VMEM((rows, width), jnp.float32),
    ] + [pltpu.VMEM((3, hidden, width), jnp.float32)] * (parts - 1)
    found = pl.pallas_call(
        functools.partial(expert_kernel, parts, per_step, cap),
        grid=(ep_count // per_step,),
        in_specs=in_specs,
        out_specs=[token_spec, token_spec] + [grad_spec] * parts,
        out_shape=out_shape,
        scratch_shapes=scratch,
        compiler_params=pltpu.CompilerParams(
            dimension_semantics=("arbitrary",), vmem_limit_bytes=VMEM_MOST
        ),
        cost_estimate=pl.CostEstimate(
            flops=18 * ep_count * cap * parts * hidden * width,
            bytes_accessed=8 * ep_count * tok * width + 30 * parts * hidden * width,
            transcendentals=ep_count * cap * parts * hidden,
        ),
        name="expert_pass",
    )(normed_all, cot_all, info, *ins, *outs_w)
    return found[0], found[1], found[2], found[3:]


def rope_tables(length):
    places = jnp.arange(length, dtype=jnp.float32)
    frequencies = ROPE_BASE ** (-jnp.arange(HDIM // 2, dtype=jnp.float32) * (2.0 / HDIM))
    angles = places[:, None] * frequencies[None, :]
    return (jnp.cos(angles)[:, None, :], jnp.sin(angles)[:, None, :])


def rotate(values, cosine, sine_table):
    middle = values.shape[-1] // 2
    former = values[..., :middle]
    latter = values[..., middle:]
    return jnp.concatenate(
        [former * cosine - latter * sine_table, latter * cosine + former * sine_table], axis=-1
    )


def unrotate(values, cosine, sine_table):
    middle = values.shape[-1] // 2
    former = values[..., :middle]
    latter = values[..., middle:]
    return jnp.concatenate(
        [former * cosine + latter * sine_table, latter * cosine - former * sine_table], axis=-1
    )


def norm_back(grad_normed, unit_values, factor, gain_values):
    grad_unit = grad_normed * gain_values
    gain_grad = jnp.sum(grad_normed * unit_values, axis=0)
    passed = factor * (
        grad_unit - unit_values * jnp.mean(grad_unit * unit_values, axis=-1, keepdims=True)
    )
    return (passed, gain_grad)


def swiglu_back(grad_act, gate_pre, up_pre):
    sigmoid_gate = jax.nn.sigmoid(gate_pre)
    grad_up = grad_act * gate_pre * sigmoid_gate
    grad_gate = grad_act * up_pre * sigmoid_gate * (1.0 + gate_pre * (1.0 - sigmoid_gate))
    return (grad_gate.astype(jnp.bfloat16), grad_up.astype(jnp.bfloat16))


def adam_update(weight, gradient, first, second, clip_scale, rate, decay):
    clipped = gradient * clip_scale
    first_new = BETA_ONE * first + (1.0 - BETA_ONE) * clipped
    second_new = BETA_TWO * second + (1.0 - BETA_TWO) * clipped * clipped
    corr_one = 1.0 - BETA_ONE**STEP
    corr_two = 1.0 - BETA_TWO**STEP
    stepped = first_new / corr_one / (jnp.sqrt(second_new / corr_two) + ADAM_EPS)
    weight_new = weight - rate * (stepped + decay * weight)
    return (weight_new, first_new, second_new, weight_new.astype(jnp.bfloat16))


def per_device(
    tokens,
    cotangent,
    segments,
    routes,
    gates,
    qkv_weight,
    qkv_first,
    qkv_second,
    out_weight,
    out_first,
    out_second,
    shared_in,
    shared_in_first,
    shared_in_second,
    shared_out,
    shared_out_first,
    shared_out_second,
    expert_in,
    expert_in_first,
    expert_in_second,
    expert_out,
    expert_out_first,
    expert_out_second,
    norm_gains,
    gains_first,
    gains_second,
):
    tok_count = tokens.shape[0]
    width = tokens.shape[1]
    ep_count = lax.axis_size("ep")
    tp_count = lax.axis_size("tp")
    capacity = tok_count * 8 // ep_count
    low = jnp.bfloat16
    ep_ring = [
        [((i + shift) % tp_count, i) for i in range(tp_count)] for shift in range(1, tp_count)
    ]
    in_own, out_own = expert_in[0].astype(low), expert_out[0].astype(low)
    ins_low = [in_own] + [lax.ppermute(in_own, "tp", ring) for ring in ep_ring]
    outs_low = [out_own] + [lax.ppermute(out_own, "tp", ring) for ring in ep_ring]
    cot_all = lax.all_gather(cotangent, "ep", axis=0)
    gain_columns = jnp.pad(norm_gains.T.astype(low), ((0, 0), (0, 126)))
    qkv_low, out_low, gains_low = gather(
        ep_count,
        tp_count,
        1,
        "gather_attention",
        [qkv_weight.astype(low), out_weight.astype(low), gain_columns],
        [],
    )
    qkv_low = qkv_low.reshape(width, 3 * width)
    out_low = out_low.reshape(width, width)
    gains_low = gains_low.reshape(width, 128)
    gain_one = gains_low[:, 0].astype(jnp.float32)
    gain_two = gains_low[:, 1].astype(jnp.float32)
    expert_ids = jnp.arange(ep_count, dtype=jnp.int32)
    chosen = routes[:, :, None] == expert_ids[None, None, :]
    onehot = jnp.sum(chosen.astype(jnp.float32), axis=1)
    gate_of = jnp.sum(jnp.where(chosen, gates[:, :, None], 0.0), axis=1)
    earlier = jnp.tril(jnp.ones((tok_count, tok_count), low), -1)
    rank = jnp.dot(earlier, onehot.astype(low), preferred_element_type=jnp.float32)
    slot_of = jnp.where(onehot > 0.0, rank, -1.0)
    info_own = jnp.concatenate([slot_of, gate_of], axis=1).T
    tok_float = tokens.astype(jnp.float32)
    factor_one = lax.rsqrt(jnp.mean(tok_float * tok_float, axis=-1, keepdims=True) + NORM_EPS)
    unit_one = tok_float * factor_one
    normed_one = (unit_one * gain_one).astype(jnp.bfloat16)
    projected = jnp.dot(normed_one, qkv_low, preferred_element_type=jnp.float32).reshape(
        tok_count, 3, HEADS, HDIM
    )
    cosine, sine_table = rope_tables(tok_count)
    queries = rotate(projected[:, 0], cosine, sine_table).astype(jnp.bfloat16)
    keys_low = rotate(projected[:, 1], cosine, sine_table).astype(jnp.bfloat16)
    values_low = projected[:, 2].astype(jnp.bfloat16)
    places = jnp.arange(tok_count)
    segment_row = segments[0]
    allowed = (places[:, None] >= places[None, :]) & (segment_row[:, None] == segment_row[None, :])
    score_scale = HDIM ** (-0.5)

    def masked_scores():
        raw = (
            jnp.einsum("shw,thw->hst", queries, keys_low, preferred_element_type=jnp.float32)
            * score_scale
        )
        return jnp.where(allowed[None], raw, NEG_BIG)

    scores = masked_scores()
    highest = jnp.max(scores, axis=-1, keepdims=True)
    log_total = highest + jnp.log(jnp.sum(jnp.exp(scores - highest), axis=-1, keepdims=True))
    probs_low = jnp.exp(scores - log_total).astype(jnp.bfloat16)
    attended = (
        jnp.einsum("hst,thw->shw", probs_low, values_low, preferred_element_type=jnp.float32)
        .reshape(tok_count, width)
        .astype(jnp.bfloat16)
    )
    hidden = tok_float + jnp.dot(attended, out_low, preferred_element_type=jnp.float32)
    factor_two = lax.rsqrt(jnp.mean(hidden * hidden, axis=-1, keepdims=True) + NORM_EPS)
    unit_two = hidden * factor_two
    normed_two = (unit_two * gain_two).astype(jnp.bfloat16)
    shin_low, shout_low, normed_all, info_all = gather(
        ep_count,
        tp_count,
        2,
        "gather_tokens",
        [shared_in.astype(low), shared_out.astype(low)],
        [normed_two, info_own],
    )
    shin_low = shin_low.reshape(width, 2 * FF)
    shout_low = shout_low.reshape(FF, width)
    info = lax.dynamic_index_in_dim(
        info_all.reshape(ep_count, 2, ep_count, tok_count), lax.axis_index("ep"), axis=2, keepdims=False
    )
    result_part, input_part, own_grad, sent_grads = expert_pass(
        normed_all, cot_all, info, ins_low, outs_low, capacity
    )
    for shift, sent in enumerate(sent_grads, 1):
        ring = [(i, (i + shift) % tp_count) for i in range(tp_count)]
        own_grad = own_grad + lax.ppermute(sent, "tp", ring).astype(jnp.float32)
    routed = lax.psum_scatter(
        result_part, "ep", scatter_dimension=0, tiled=True
    )[0].astype(jnp.float32)
    (routed_grad,) = scatter_add(ep_count, tp_count, 3, "scatter_inputs", False, [input_part])
    shared_pre = jnp.dot(normed_two, shin_low, preferred_element_type=jnp.float32)
    shared_act = (jax.nn.silu(shared_pre[:, :FF]) * shared_pre[:, FF:]).astype(jnp.bfloat16)
    shared_res = jnp.dot(shared_act, shout_low, preferred_element_type=jnp.float32)
    block_out = (hidden + shared_res + routed).astype(jnp.bfloat16)
    grad_top = cotangent.astype(jnp.float32)
    grad_low = grad_top.astype(jnp.bfloat16)
    shout_grad = jnp.einsum("tf,td->fd", shared_act, grad_low, preferred_element_type=jnp.float32)
    grad_shared_act = jnp.einsum(
        "td,fd->tf", grad_low, shout_low, preferred_element_type=jnp.float32
    )
    grad_sh_gate, grad_sh_up = swiglu_back(grad_shared_act, shared_pre[:, :FF], shared_pre[:, FF:])
    grad_shared_pre = jnp.concatenate([grad_sh_gate, grad_sh_up], axis=1)
    shin_grad = jnp.einsum(
        "td,tf->df", normed_two, grad_shared_pre, preferred_element_type=jnp.float32
    )
    grad_normed_two = routed_grad + jnp.einsum(
        "tf,df->td", grad_shared_pre, shin_low, preferred_element_type=jnp.float32
    )
    passed_two, gain_two_grad = norm_back(grad_normed_two, unit_two, factor_two, gain_two)
    grad_hidden = grad_top + passed_two
    grad_branch = grad_hidden.astype(jnp.bfloat16)
    out_grad = jnp.einsum("td,te->de", attended, grad_branch, preferred_element_type=jnp.float32)
    grad_attended = (
        jnp.einsum("te,de->td", grad_branch, out_low, preferred_element_type=jnp.float32)
        .astype(jnp.bfloat16)
        .reshape(tok_count, HEADS, HDIM)
    )
    probabilities = jnp.exp(masked_scores() - log_total)
    grad_probs = jnp.einsum(
        "shw,thw->hst", grad_attended, values_low, preferred_element_type=jnp.float32
    )
    grad_values = jnp.einsum(
        "hst,shw->thw",
        probabilities.astype(jnp.bfloat16),
        grad_attended,
        preferred_element_type=jnp.float32,
    )
    row_dot = jnp.sum(probabilities * grad_probs, axis=-1, keepdims=True)
    grad_scores = (probabilities * (grad_probs - row_dot)).astype(jnp.bfloat16)
    grad_queries = (
        jnp.einsum("hst,thw->shw", grad_scores, keys_low, preferred_element_type=jnp.float32)
        * score_scale
    )
    grad_keys = (
        jnp.einsum("hst,shw->thw", grad_scores, queries, preferred_element_type=jnp.float32)
        * score_scale
    )
    grad_proj = jnp.stack(
        [
            unrotate(grad_queries, cosine, sine_table),
            unrotate(grad_keys, cosine, sine_table),
            grad_values,
        ],
        axis=1,
    )
    grad_proj = grad_proj.reshape(tok_count, 3 * width).astype(jnp.bfloat16)
    qkv_grad = jnp.einsum("td,te->de", normed_one, grad_proj, preferred_element_type=jnp.float32)
    grad_normed_one = jnp.einsum(
        "te,de->td", grad_proj, qkv_low, preferred_element_type=jnp.float32
    )
    passed_one, gain_one_grad = norm_back(grad_normed_one, unit_one, factor_one, gain_one)
    tokens_grad = grad_hidden + passed_one
    gain_rows = jnp.pad(jnp.stack([gain_one_grad, gain_two_grad], axis=1), ((0, 0), (0, 126)))
    devices = ep_count * tp_count
    dense_grads = scatter_add(
        ep_count,
        tp_count,
        4,
        "scatter_weights",
        True,
        [
            grad.astype(low).reshape(devices, -1, grad.shape[1])
            for grad in (qkv_grad, out_grad, gain_rows, shin_grad, shout_grad)
        ],
    )
    qkv_part, out_part, gains_part, shin_part, shout_part = dense_grads
    gains_part = gains_part[:, :2].T
    exin_part, exout_part = own_grad[None, :2], own_grad[2:]
    squares = (
        jnp.sum(qkv_part * qkv_part) + jnp.sum(out_part * out_part) + jnp.sum(shin_part * shin_part)
    )
    squares = squares + jnp.sum(shout_part * shout_part) + jnp.sum(exin_part * exin_part)
    squares = squares + jnp.sum(exout_part * exout_part) + jnp.sum(gains_part * gains_part)
    grad_norm = jnp.sqrt(lax.psum(squares, ("ep", "tp")))
    clip_scale = jnp.minimum(1.0, CLIP_LEVEL / (grad_norm + 1e-06))
    qkv_new, qkv_first_new, qkv_second_new, qkv_copy = adam_update(
        qkv_weight, qkv_part, qkv_first, qkv_second, clip_scale, MATRIX_RATE, WEIGHT_DECAY
    )
    out_new, out_first_new, out_second_new, out_copy = adam_update(
        out_weight, out_part, out_first, out_second, clip_scale, MATRIX_RATE, WEIGHT_DECAY
    )
    shin_new, shin_first_new, shin_second_new, shin_copy = adam_update(
        shared_in,
        shin_part,
        shared_in_first,
        shared_in_second,
        clip_scale,
        MATRIX_RATE,
        WEIGHT_DECAY,
    )
    shout_new, shout_first_new, shout_second_new, shout_copy = adam_update(
        shared_out,
        shout_part,
        shared_out_first,
        shared_out_second,
        clip_scale,
        MATRIX_RATE,
        WEIGHT_DECAY,
    )
    exin_new, exin_first_new, exin_second_new, exin_copy = adam_update(
        expert_in,
        exin_part,
        expert_in_first,
        expert_in_second,
        clip_scale,
        MATRIX_RATE,
        WEIGHT_DECAY,
    )
    exout_new, exout_first_new, exout_second_new, exout_copy = adam_update(
        expert_out,
        exout_part,
        expert_out_first,
        expert_out_second,
        clip_scale,
        MATRIX_RATE,
        WEIGHT_DECAY,
    )
    gains_new, gains_first_new, gains_second_new, gains_copy = adam_update(
        norm_gains, gains_part, gains_first, gains_second, clip_scale, GAIN_RATE, 0.0
    )
    return (
        block_out,
        tokens_grad,
        grad_norm,
        qkv_new,
        qkv_first_new,
        qkv_second_new,
        qkv_copy,
        out_new,
        out_first_new,
        out_second_new,
        out_copy,
        shin_new,
        shin_first_new,
        shin_second_new,
        shin_copy,
        shout_new,
        shout_first_new,
        shout_second_new,
        shout_copy,
        exin_new,
        exin_first_new,
        exin_second_new,
        exin_copy,
        exout_new,
        exout_first_new,
        exout_second_new,
        exout_copy,
        gains_new,
        gains_first_new,
        gains_second_new,
        gains_copy,
    )


def solution(mesh):
    placed = (
        P(("ep", "tp"), None),
        P(("ep", "tp"), None),
        P(("ep", "tp"), None),
        P(("ep", "tp"), None),
        P(("ep", "tp"), None),
        P(("ep", "tp"), None),
        P(("ep", "tp"), None),
        P(("ep", "tp"), None),
        P(("ep", "tp"), None),
        P(("ep", "tp"), None),
        P(("ep", "tp"), None),
        P(("ep", "tp"), None),
        P(("ep", "tp"), None),
        P(("ep", "tp"), None),
        P(("ep", "tp"), None),
        P(("ep", "tp"), None),
        P(("ep", "tp"), None),
        P("ep", None, "tp", None),
        P("ep", None, "tp", None),
        P("ep", None, "tp", None),
        P("ep", "tp", None),
        P("ep", "tp", None),
        P("ep", "tp", None),
        P(None, ("ep", "tp")),
        P(None, ("ep", "tp")),
        P(None, ("ep", "tp")),
    )
    return jax.shard_map(
        per_device,
        mesh=mesh,
        in_specs=placed,
        out_specs=(
            P(("ep", "tp"), None),
            P(("ep", "tp"), None),
            P(),
            P(("ep", "tp"), None),
            P(("ep", "tp"), None),
            P(("ep", "tp"), None),
            P(("ep", "tp"), None),
            P(("ep", "tp"), None),
            P(("ep", "tp"), None),
            P(("ep", "tp"), None),
            P(("ep", "tp"), None),
            P(("ep", "tp"), None),
            P(("ep", "tp"), None),
            P(("ep", "tp"), None),
            P(("ep", "tp"), None),
            P(("ep", "tp"), None),
            P(("ep", "tp"), None),
            P(("ep", "tp"), None),
            P(("ep", "tp"), None),
            P("ep", None, "tp", None),
            P("ep", None, "tp", None),
            P("ep", None, "tp", None),
            P("ep", None, "tp", None),
            P("ep", "tp", None),
            P("ep", "tp", None),
            P("ep", "tp", None),
            P("ep", "tp", None),
            P(None, ("ep", "tp")),
            P(None, ("ep", "tp")),
            P(None, ("ep", "tp")),
            P(None, ("ep", "tp")),
        ),
        check_vma=False,
    )
```

```python
import functools
import jax
import jax.numpy as jnp
import numpy as np
from jax import lax
from jax.experimental import pallas as pl
from jax.experimental.pallas import tpu as pltpu
from jax.sharding import PartitionSpec as P

HEADS = 10
HDIM = 128
FF = 896
TOPK = 7
STEP = 10


MESH = pl.DeviceIdType.MESH
VMEM_MOST = 60 * 1024 * 1024
NEG_BIG = -1000000000.0
NORM_EPS = 1e-06
ROPE_BASE = 10000.0
CLIP_LEVEL = 1.0
BETA_ONE = 0.9
BETA_TWO = 0.95
ADAM_EPS = 1e-08
WEIGHT_DECAY = 0.1
MATRIX_RATE = 0.05
GAIN_RATE = 0.5


class Place:
    def __init__(self, ep_count, tp_count):
        chips = ep_count // 2
        nb = 1
        while nb * nb * 4 <= chips:
            nb *= 2
        self.nb, self.na, self.nt = nb, chips // nb, tp_count
        self.ep_count = ep_count
        self.wrap = chips * tp_count >= 64
        e = lax.axis_index("ep")
        self.t = lax.axis_index("tp")
        self.core = lax.rem(e, 2)
        self.b = lax.rem(e // 2, nb)
        self.a = e // (2 * nb)

    def dims(self, order):
        if "u" in order and self.nb != self.nt:
            order = "abt"
        extents = {"a": self.na, "b": self.nb, "t": self.nt, "u": self.nb, "v": self.nt}
        return tuple((name, shifts(extents[name], self.wrap)) for name in order)

    def extent(self, name):
        return {"a": self.na, "b": self.nb, "t": self.nt, "u": self.nb, "v": self.nt}[name]

    def moved(self, name, shift):
        own, extent = self.own(name), self.extent(name)
        if shift == 0:
            return own, None
        if extent == 2:
            return 1 - own, None
        if self.wrap:
            return lax.rem(own + shift + extent, extent), None
        there = own + shift
        return there, (there >= 0) & (there < extent)

    def own(self, name):
        even = self.core == 0
        if name == "u":
            return jnp.where(even, self.b, self.t)
        if name == "v":
            return jnp.where(even, self.t, self.b)
        return getattr(self, name)

    def chip(self, at):
        a = at.get("a", self.a)
        b, t = at.get("b", self.b), at.get("t", self.t)
        if "u" in at:
            even = self.core == 0
            b = jnp.where(even, at["u"], at["v"])
            t = jnp.where(even, at["v"], at["u"])
        return a, b, t

    def device(self, at, core):
        a, b, t = self.chip(at)
        return ((a * self.nb + b) * 2 + core, t)

    def index(self, at, core, whole):
        e, t = self.device(at, core)
        return e * self.nt + t if whole else e

    def slot(self, at, whole):
        a, b, t = self.chip(at)
        chip = a * self.nb + b
        return chip * self.nt + t if whole else chip


def shifts(extent, wrap):
    if extent == 1:
        return (0,)
    if extent == 2:
        return (0, 1)
    found = [0]
    for step in range(1, extent // 2 + 1 if wrap else extent):
        found += [step, -step]
    return tuple(found[:extent] if wrap else found)


def ways(spread):
    return (1,) if len(spread) == 2 else (1, -1) if len(spread) > 2 else ()


def onward(spread, shift):
    way = -1 if shift > 0 else 1
    return way if len(spread) > 2 and shift - way in spread else 0


def both(one, other):
    if one is None:
        return other
    return one if other is None else one & other


def guarded(condition, body):
    if condition is None:
        body()
    else:
        pl.when(condition)(body)


def greet(place, order):
    barrier = pltpu.get_barrier_semaphore()
    here = {name: place.own(name) for name, _ in place.dims(order)}
    pl.semaphore_signal(barrier, inc=1, device_id=place.device(here, 1 - place.core), device_id_type=MESH)
    count = jnp.int32(1)
    for name, spread in place.dims(order):
        for way in ways(spread):
            there, on = place.moved(name, way)
            target = place.device({**here, name: there}, place.core)

            def signal(target=target):
                pl.semaphore_signal(barrier, inc=1, device_id=target, device_id_type=MESH)

            guarded(on, signal)
            count = count + (1 if on is None else on.astype(jnp.int32))
    if len(order) > 2:
        for s in range(2, place.nt - 1):
            target = place.device({"t": lax.rem(place.t + s, place.nt)}, place.core)
            pl.semaphore_signal(barrier, inc=1, device_id=target, device_id_type=MESH)
            count = count + 1
    pl.semaphore_wait(barrier, count)


def relative_blocks(dims):
    blocks = [()]
    for _, spread in dims:
        blocks = [block + (shift,) for block in blocks for shift in spread]
    return blocks


def gather_events(place, order, pairs, send_sems, recv_sems):
    dims = place.dims(order)
    whole = len(dims) > 2
    here = {name: place.own(name) for name, _ in dims}
    counter = [0]
    ends = []

    def copies(at, target, core_of_block, own):
        index = place.index(at, core_of_block, whole)
        number = counter[0]
        counter[0] += 1
        made = []
        for k, (block, gathered) in enumerate(pairs):
            made.append(
                pltpu.make_async_remote_copy(
                    src_ref=block if own else gathered.at[index],
                    dst_ref=gathered.at[index],
                    send_sem=send_sems.at[k, number],
                    recv_sem=recv_sems.at[k, index],
                    device_id=target,
                    device_id_type=MESH,
                )
            )
        return made

    def send(at, on, target, own, todo):
        made = copies(at, target, place.core, own)

        def start(made=made):
            for copy in made:
                copy.start()

        def finish(made=made):
            for copy in made:
                copy.wait_send()

        todo.append((on, start))
        ends.append((on, finish))

    steps = []
    times = arrival_times(dims)
    for block in relative_blocks(dims):
        at, valid = dict(here), None
        for (name, _), shift in zip(dims, block):
            at[name], on = place.moved(name, shift)
            valid = both(valid, on)
        last = max([k for k, shift in enumerate(block) if shift], default=-1)
        own = last < 0
        todo = []
        for k in range(len(dims) - 1, -1, -1):
            name, spread = dims[k]
            if k < last:
                continue
            if k == last:
                way = onward(spread, block[k])
                sent = [way] if way else []
            else:
                sent = ways(spread)
            for way in sent:
                there, on = place.moved(name, way)
                target = place.device({**here, name: there}, place.core)
                send(at, both(valid, on), target, own, todo)
        send(at, valid, place.device(here, 1 - place.core), own, todo)
        index = place.index(at, place.core, whole)

        def step(index=index, valid=valid, todo=todo, own=own):
            def body():
                if not own:
                    for k, (_, gathered) in enumerate(pairs):
                        pltpu.make_async_copy(gathered.at[index], gathered.at[index], recv_sems.at[k, index]).wait()

            guarded(valid, body)
            for on, start in todo:
                guarded(on, start)

        steps.append((times[block], step))
        other = place.index(at, 1 - place.core, whole)

        def arrived(other=other):
            for k, (_, gathered) in enumerate(pairs):
                pltpu.make_async_copy(gathered.at[other], gathered.at[other], recv_sems.at[k, other]).wait()

        ends.append((valid, arrived))
    return steps, ends, counter[0]


def arrival_times(dims):
    times = {(): 0}
    for _, spread in dims:
        earlier = sorted(times, key=lambda block: times[block])
        found = {block + (0,): times[block] for block in earlier}
        for shift in spread:
            for i, block in enumerate(earlier):
                if shift:
                    far = abs(shift)
                    found[block + (shift,)] = max(times[block] + far, (far - 1) * len(earlier) + i + 1)
        times = found
    return times


def count_gather_sends(dims):
    total = 0
    for block in relative_blocks(dims):
        last = max([k for k, shift in enumerate(block) if shift], default=-1)
        for k, (_, spread) in enumerate(dims):
            if k > last:
                total += len(ways(spread))
            elif k == last and onward(spread, block[k]):
                total += 1
        total += 1
    return total


def exchange_copies(place, blocks, others, send_sems, recv_sems):
    copies = []
    for s in range(1, place.nt):
        back = blocks[0].shape == others[0].shape
        there = lax.rem(place.t + (s if back else place.nt - s), place.nt)
        target = place.device({"t": there}, place.core)
        for k, (block, other) in enumerate(zip(blocks, others)):
            copies.append(
                pltpu.make_async_remote_copy(
                    src_ref=block.at[s - 1] if back else block,
                    dst_ref=other.at[s - 1],
                    send_sem=send_sems.at[k, s - 1],
                    recv_sem=recv_sems.at[k, s - 1],
                    device_id=target,
                    device_id_type=MESH,
                )
            )
    return copies


def gather_kernel(ep_count, tp_count, groups, *refs):
    count = sum(n for _, n in groups)
    blocks, gathered, scratch = refs[:count], refs[count : 2 * count], refs[2 * count :]
    place = Place(ep_count, tp_count)
    greet(place, max((order for order, _ in groups), key=len))
    steps, ends, first = [], [], 0
    local, swaps = [], []
    for order, n in groups:
        mine_in, mine_out = blocks[first : first + n], gathered[first : first + n]
        first += n
        if order == "t":
            swaps += exchange_copies(place, mine_in, mine_out, scratch[0], scratch[1])
            scratch = scratch[2:]
            continue
        send_sems, recv_sems, own_sems = scratch[:3]
        scratch = scratch[3:]
        pairs = list(zip(mine_in, mine_out))
        more, finish, _ = gather_events(place, order, pairs, send_sems, recv_sems)
        size = sum(block.shape[0] * block.shape[1] * (4 if block.dtype == jnp.float32 else 2) for block in mine_in)
        steps += [(key * size, len(steps) + i, step) for i, (key, step) in enumerate(more)]
        ends += finish
        here = {name: place.own(name) for name, _ in place.dims(order)}
        mine = place.index(here, place.core, len(order) > 2)
        for k, (block, out) in enumerate(pairs):
            local.append(pltpu.make_async_copy(block, out.at[mine], own_sems.at[k]))
    steps.sort(key=lambda entry: entry[:2])
    lead = sum(1 for key, _, _ in steps if key == 0)
    for _, _, step in steps[:lead]:
        step()
    for copy in swaps + local:
        copy.start()
    for _, _, step in steps[lead:]:
        step()
    for on, finish in ends:
        guarded(on, finish)
    for copy in swaps + local:
        copy.wait()


def gather(ep_count, tp_count, collective_id, name, groups):
    arrays, shapes, scratch = [], [], []
    place = Place(ep_count, tp_count)
    for order, blocks in groups:
        total = ep_count * tp_count if len(order) > 2 else ep_count if order != "t" else tp_count - 1
        for block in blocks:
            arrays.append(block)
            shapes.append(jax.ShapeDtypeStruct((total,) + block.shape, block.dtype))
        if order == "t":
            scratch += [pltpu.SemaphoreType.DMA((len(blocks), total))] * 2
            continue
        sends = count_gather_sends(place.dims(order))
        scratch += [
            pltpu.SemaphoreType.DMA((len(blocks), sends)),
            pltpu.SemaphoreType.DMA((len(blocks), total)),
            pltpu.SemaphoreType.DMA((len(blocks),)),
        ]
    return pl.pallas_call(
        functools.partial(
            gather_kernel, ep_count, tp_count, tuple((order, len(blocks)) for order, blocks in groups)
        ),
        out_shape=tuple(shapes),
        in_specs=[pl.BlockSpec(memory_space=pl.ANY)] * len(arrays),
        out_specs=tuple([pl.BlockSpec(memory_space=pl.ANY)] * len(arrays)),
        scratch_shapes=scratch,
        compiler_params=pltpu.CompilerParams(collective_id=collective_id, has_side_effects=True),
        name=name,
    )(*arrays)


def add_into(target, sources, dtype):
    rows, columns = target.shape
    piece = 128
    while columns % (piece * 2) == 0 and rows * piece * 2 <= 40 * 1024:
        piece *= 2

    def body(i, carry):
        window = pl.ds(pl.multiple_of(i * piece, piece), piece)
        total = sources[0][:, window].astype(jnp.float32)
        for source in sources[1:]:
            total = total + source[:, window].astype(jnp.float32)
        target[:, window] = total.astype(dtype)
        return carry

    lax.fori_loop(0, columns // piece, body, 0)


def norm_kernel(ep_count, tp_count, count, *refs):
    parts, extra, out = refs[:count], refs[count], refs[count + 1]
    tile, tiles, send, recv = refs[count + 2 :]
    devices = ep_count * tp_count
    me = lax.axis_index("ep") * tp_count + lax.axis_index("tp")

    def place(i):
        other = lax.rem(me + i, devices)
        return other, (other // tp_count, lax.rem(other, tp_count))

    barrier = pltpu.get_barrier_semaphore()

    def signal(i, carry):
        pl.semaphore_signal(barrier, inc=1, device_id=place(i)[1], device_id_type=MESH)
        return carry

    lax.fori_loop(1, devices, signal, 0)
    tile[...] = jnp.zeros_like(tile)
    for first in range(0, extra.shape[1], 128):
        tile[0:1, :] += extra[:, first : first + 128]
    for part in parts:

        def add(i, carry, part=part):
            piece = part[:, pl.ds(pl.multiple_of(i * 128, 128), 128)]
            tile[0:1, :] += jnp.sum(piece * piece, axis=0, keepdims=True)
            return carry

        lax.fori_loop(0, part.shape[1] // 128, add, 0)
    pl.semaphore_wait(barrier, devices - 1)

    def share(i, carry):
        pltpu.make_async_remote_copy(
            src_ref=tile,
            dst_ref=tiles.at[me],
            send_sem=send.at[i],
            recv_sem=recv.at[me],
            device_id=place(i)[1],
            device_id_type=MESH,
        ).start()
        return carry

    lax.fori_loop(1, devices, share, 0)
    out[...] = tile[...]

    def collect(i, carry):
        other = place(i)[0]
        pltpu.make_async_copy(tiles.at[other], tiles.at[other], recv.at[other]).wait()
        out[...] += tiles[other]
        return carry

    lax.fori_loop(1, devices, collect, 0)

    def sent(i, carry):
        pltpu.make_async_copy(tile, tile, send.at[i]).wait()
        return carry

    lax.fori_loop(1, devices, sent, 0)


def sum_of_squares(ep_count, tp_count, collective_id, parts, extra):
    devices = ep_count * tp_count
    inside = pl.BlockSpec(memory_space=pltpu.VMEM)
    total = pl.pallas_call(
        functools.partial(norm_kernel, ep_count, tp_count, len(parts)),
        out_shape=jax.ShapeDtypeStruct((8, 128), jnp.float32),
        in_specs=[inside] * (len(parts) + 1),
        out_specs=inside,
        scratch_shapes=[
            pltpu.VMEM((8, 128), jnp.float32),
            pltpu.VMEM((devices, 8, 128), jnp.float32),
            pltpu.SemaphoreType.DMA((devices,)),
            pltpu.SemaphoreType.DMA((devices,)),
        ],
        compiler_params=pltpu.CompilerParams(collective_id=collective_id, has_side_effects=True),
        name="sum_of_squares",
    )(*parts, extra)
    return jnp.sum(total)


def scatter_events(place, order, partials, outs, refs):
    count = len(partials)
    dims = place.dims(order)
    whole = len(dims) > 2
    here = {name: place.own(name) for name, _ in dims}
    owns, sibs = refs[:count], refs[count : 2 * count]
    lands = [refs[(2 + k) * count : (3 + k) * count] for k in range(len(dims))]
    sems = refs[(2 + len(dims)) * count :]
    own_sem, sib_send, sib_recv, line_send = sems[:4]
    line_recv = sems[4:]
    blocks = sorted(relative_blocks(dims), key=lambda block: -sum(abs(s) for s in block))
    blocks = sorted(blocks, key=lambda block: -max([k for k, s in enumerate(block) if s], default=-1))
    info = {}
    starts, steps, ends = [], [], []
    for block in blocks:
        at, valid = dict(here), None
        for (name, _), shift in zip(dims, block):
            at[name], on = place.moved(name, shift)
            valid = both(valid, on)
        slot = place.slot(at, whole)
        local = [
            pltpu.make_async_copy(
                partials[k].at[place.index(at, place.core, whole)], owns[k].at[slot], own_sem.at[k, slot]
            )
            for k in range(count)
        ]
        across = [
            pltpu.make_async_remote_copy(
                src_ref=partials[k].at[place.index(at, 1 - place.core, whole)],
                dst_ref=sibs[k].at[slot],
                send_sem=sib_send.at[k, slot],
                recv_sem=sib_recv.at[k, slot],
                device_id=place.device(here, 1 - place.core),
                device_id_type=MESH,
            )
            for k in range(count)
        ]

        def start(local=local, across=across):
            for copy in across + local:
                copy.start()

        def finish(across=across):
            for copy in across:
                copy.wait_send()

        starts.append((valid, start))
        ends.append((valid, finish))
        info[block] = (at, valid, slot, local, across)

    def land_slot(level, at, shift, side):
        inner, wide = 0, 1
        for name, _ in dims[:level]:
            inner = inner * place.extent(name) + at[name]
            wide = wide * place.extent(name)
        return landings(dims[level][1]).index((shift, side)) * wide + inner

    number = 0
    for block in blocks:
        at, valid, slot, local, across = info[block]
        todo = []
        last = max([k for k, shift in enumerate(block) if shift], default=-1)
        extra_refs = []
        for level in range(len(dims) - 1, max(last, 0) - 1, -1):
            name, spread = dims[level]
            for shift, side in landings(spread):
                if shift == block[level]:
                    _, on = place.moved(name, side)
                    extra_refs.append((level, land_slot(level, at, shift, side), on))

        def arrive(local=local, across=across):
            for copy in local:
                copy.wait()
            for copy in across:
                copy.wait_recv()

        todo.append((valid, arrive))
        for k in range(count):
            sure = [owns[k].at[slot], sibs[k].at[slot]]
            maybe = []
            for level, spot, on in extra_refs:
                ref = lands[level][k].at[spot]

                def wait(ref=ref, k=k, level=level, spot=spot):
                    pltpu.make_async_copy(ref, ref, line_recv[level].at[k, spot]).wait()

                todo.append((both(valid, on), wait))
                if on is None:
                    sure.append(ref)
                else:
                    maybe.append((ref, on))
            if last >= 0:
                target, dtype = owns[k].at[slot], owns[k].dtype
            else:
                target, dtype = outs[k], outs[k].dtype

            def add(sure=sure, maybe=maybe, target=target, dtype=dtype):
                if not maybe:
                    add_into(target, sure, dtype)
                elif len(maybe) == 1:
                    ((ref, on),) = maybe
                    pl.when(on)(lambda: add_into(target, sure + [ref], dtype))
                    pl.when(jnp.logical_not(on))(lambda: add_into(target, sure, dtype))
                else:
                    (low, on_low), (high, on_high) = maybe
                    pl.when(on_low & on_high)(lambda: add_into(target, sure + [low, high], dtype))
                    pl.when(on_low & jnp.logical_not(on_high))(lambda: add_into(target, sure + [low], dtype))
                    pl.when(on_high & jnp.logical_not(on_low))(lambda: add_into(target, sure + [high], dtype))

            todo.append((valid, add))
        if last >= 0:
            name, spread = dims[last]
            way = 1 if block[last] > 0 else -1
            there, _ = place.moved(name, way)
            spot = land_slot(last, at, block[last] - way, -way if len(spread) > 2 else 1)
            made = [
                pltpu.make_async_remote_copy(
                    src_ref=owns[k].at[slot],
                    dst_ref=lands[last][k].at[spot],
                    send_sem=line_send.at[k, number],
                    recv_sem=line_recv[last].at[k, spot],
                    device_id=place.device({**here, name: there}, place.core),
                    device_id_type=MESH,
                )
                for k in range(count)
            ]
            number += 1

            def start(made=made):
                for copy in made:
                    copy.start()

            def finish(made=made):
                for copy in made:
                    copy.wait_send()

            todo.append((valid, start))
            ends.append((valid, finish))
        steps.append(todo)
    return starts, steps, ends


def scatter_sizes(place, order):
    dims = place.dims(order)
    slots, lands = 1, []
    for name, spread in dims:
        lands.append(len(landings(spread)) * slots)
        slots *= place.extent(name)
    return slots, lands, sum(1 for block in relative_blocks(dims) if any(block))


def scatter_kernel(ep_count, tp_count, groups, *refs):
    count = sum(n for _, n in groups)
    partials, outs, refs = refs[:count], refs[count : 2 * count], refs[2 * count :]
    place = Place(ep_count, tp_count)
    greet(place, max((order for order, _ in groups), key=len))
    starts, steps, ends, swaps, first = [], [], [], [], 0
    for order, n in groups:
        mine_in, mine_out = partials[first : first + n], outs[first : first + n]
        first += n
        if order == "t":
            swaps += exchange_copies(place, mine_in, mine_out, refs[0], refs[1])
            refs = refs[2:]
            continue
        used = n * (2 + len(order)) + 4 + len(order)
        more, done, finish = scatter_events(place, order, mine_in, mine_out, refs[:used])
        refs = refs[used:]
        starts += [(i / len(more), len(starts) + i, entry) for i, entry in enumerate(more)]
        steps += [(i / len(done), len(steps) + i, todo) for i, todo in enumerate(done)]
        ends += finish
    for copy in swaps:
        copy.start()
    for _, _, (on, start) in sorted(starts, key=lambda entry: entry[:2]):
        guarded(on, start)
    for _, _, todo in sorted(steps, key=lambda entry: entry[:2]):
        for on, act in todo:
            guarded(on, act)
    for on, finish in ends:
        guarded(on, finish)
    for copy in swaps:
        copy.wait()


def landings(spread):
    if len(spread) == 2:
        return [(0, 1)]
    return [(shift, way) for shift in spread for way in (-1, 1) if shift - way in spread and shift * way <= 0]


def scatter_add(ep_count, tp_count, collective_id, name, groups):
    place = Place(ep_count, tp_count)
    arrays, shapes, scratch, specs = [], [], [], []
    dma = pltpu.SemaphoreType.DMA
    for order, partials in groups:
        arrays += partials
        count = len(partials)
        if order == "t":
            shapes += [jax.ShapeDtypeStruct(p.shape, p.dtype) for p in partials]
            specs += [pl.BlockSpec(memory_space=pl.ANY)] * count
            scratch += [dma((count, tp_count - 1))] * 2
            continue
        slots, lands, sends = scatter_sizes(place, order)
        blocks = [(p.shape[1:], p.dtype) for p in partials]
        shapes += [jax.ShapeDtypeStruct(shape, jnp.float32) for shape, _ in blocks]
        specs += [pl.BlockSpec(memory_space=pltpu.VMEM)] * count
        for wide in [slots, slots] + lands:
            scratch += [pltpu.VMEM((wide,) + shape, dtype) for shape, dtype in blocks]
        scratch += [dma((count, slots))] * 3 + [dma((count, sends))] + [dma((count, wide)) for wide in lands]
    return pl.pallas_call(
        functools.partial(
            scatter_kernel, ep_count, tp_count, tuple((order, len(partials)) for order, partials in groups)
        ),
        out_shape=tuple(shapes),
        in_specs=[pl.BlockSpec(memory_space=pl.ANY)] * len(arrays),
        out_specs=tuple(specs),
        scratch_shapes=scratch,
        compiler_params=pltpu.CompilerParams(
            collective_id=collective_id, has_side_effects=True, vmem_limit_bytes=VMEM_MOST
        ),
        name=name,
    )(*arrays)


def scatter_all(ep_count, tp_count, collective_ids, name, groups):
    place = Place(ep_count, tp_count)
    calls, room = [[]], 0
    for order, partials in groups:
        need = 0
        if order != "t":
            slots, lands, _ = scatter_sizes(place, order)
            for p in partials:
                rows = (p.shape[1] + 15) // 16 * 16
                need += (2 * slots + sum(lands)) * rows * p.shape[2] * p.dtype.itemsize
        if calls[-1] and room + need > VMEM_MOST * 19 // 20:
            calls.append([])
            room = 0
        calls[-1].append((order, partials))
        room += need
    found = []
    for i, call in enumerate(calls):
        found += scatter_add(ep_count, tp_count, collective_ids[i], "%s_%d" % (name, i), call)
    return found

OVER_LAST = (((1,), (1,)), ((), ()))
OVER_FIRST = (((0,), (0,)), ((), ()))
STRAIGHT = (((1,), (0,)), ((), ()))


def mul(left, right, dims=STRAIGHT):
    return lax.dot_general(left, right, dims, preferred_element_type=jnp.float32)


def rope_rows(length):
    places = np.arange(length, dtype=np.float32)
    frequencies = ROPE_BASE ** (-np.arange(HDIM // 2, dtype=np.float32) * np.float32(2.0 / HDIM))
    angles = places[:, None] * frequencies.astype(np.float32)[None, :]
    cosine, sine = np.cos(angles), np.sin(angles)
    return (
        np.concatenate([cosine, cosine], axis=1).astype(np.float32),
        np.concatenate([-sine, sine], axis=1).astype(np.float32),
    )


def unit_of(values):
    factor = lax.rsqrt(jnp.mean(values * values, axis=-1, keepdims=True) + NORM_EPS)
    return values * factor, factor


def masked_probs(queries, keys, allowed):
    raw = mul(queries, keys, OVER_LAST) * HDIM ** (-0.5)
    scores = jnp.where(allowed, raw, NEG_BIG)
    weights = jnp.exp(scores - jnp.max(scores, axis=-1, keepdims=True))
    return weights * (1.0 / jnp.sum(weights, axis=-1, keepdims=True))


def allowed_pairs(seg_row, seg_column):
    length = seg_row.shape[1]
    later = lax.broadcasted_iota(jnp.int32, (length, length), 0)
    earlier = lax.broadcasted_iota(jnp.int32, (length, length), 1)
    return (later >= earlier) & (seg_column[:, 0:1] == seg_row[0:1, :])


def forward_kernel(tokens, seg_row, seg_column, gains, cosine, sine, wq, wk, wv, wo,
                   qkv_out, attended, hidden, normed_two, normed):
    pair = pl.program_id(0)
    width = tokens.shape[1]
    wide = 2 * HDIM

    @pl.when(pair == 0)
    def _():
        values = tokens[...].astype(jnp.float32)
        normed[...] = (unit_of(values)[0] * gains[0:1, :]).astype(jnp.bfloat16)
        hidden[...] = values

    allowed = allowed_pairs(seg_row, seg_column)
    window = pl.ds(pl.multiple_of(pair * wide, wide), wide)
    made = []
    for part, weight in enumerate((wq, wk, wv)):
        projected = mul(normed[...], weight[...])
        heads = []
        for j in range(2):
            head = projected[:, j * HDIM : (j + 1) * HDIM]
            if part < 2:
                head = head * cosine[...] + pltpu.roll(head, HDIM // 2, 1) * sine[...]
            heads.append(head.astype(jnp.bfloat16))
            qkv_out[:, pl.ds(pl.multiple_of(part * width + pair * wide + j * HDIM, HDIM), HDIM)] = heads[j]
        made.append(heads)
    for j in range(2):
        probs = masked_probs(made[0][j], made[1][j], allowed).astype(jnp.bfloat16)
        attended[:, pl.ds(pl.multiple_of(pair * wide + j * HDIM, HDIM), HDIM)] = mul(
            probs, made[2][j]
        ).astype(jnp.bfloat16)
    hidden[...] += mul(attended[:, window], wo[...])

    @pl.when(pair == pl.num_programs(0) - 1)
    def _():
        normed_two[...] = (unit_of(hidden[...])[0] * gains[1:2, :]).astype(jnp.bfloat16)


def attention_forward(tokens, segments, gains, qkv_low, out_low):
    length, width = tokens.shape
    wide, pairs = 2 * HDIM, HEADS // 2
    cosine, sine = rope_rows(length)
    seg_row = jnp.broadcast_to(segments, (8, length))
    seg_column = jnp.broadcast_to(segments.T, (length, 128))
    low = jnp.bfloat16

    def whole(*shape):
        return pl.BlockSpec(shape, lambda i: (0,) * len(shape))

    def columns(part):
        return pl.BlockSpec((width, wide), lambda i: (0, part * pairs + i))

    return pl.pallas_call(
        forward_kernel,
        grid=(pairs,),
        in_specs=[
            whole(length, width), whole(8, length), whole(length, 128), whole(8, width),
            whole(length, HDIM), whole(length, HDIM), columns(0), columns(1), columns(2),
            pl.BlockSpec((wide, width), lambda i: (i, 0)),
        ],
        out_specs=[whole(length, 3 * width), whole(length, width), whole(length, width), whole(length, width)],
        out_shape=[
            jax.ShapeDtypeStruct((length, 3 * width), low),
            jax.ShapeDtypeStruct((length, width), low),
            jax.ShapeDtypeStruct((length, width), jnp.float32),
            jax.ShapeDtypeStruct((length, width), low),
        ],
        scratch_shapes=[pltpu.VMEM((length, width), low)],
        compiler_params=pltpu.CompilerParams(
            dimension_semantics=("arbitrary",), vmem_limit_bytes=VMEM_MOST
        ),
        name="attention_forward",
    )(tokens, seg_row, seg_column, gains, jnp.asarray(cosine), jnp.asarray(sine), qkv_low, qkv_low, qkv_low, out_low)


def spread_matrix(units, padded, group, step):
    unit = lax.broadcasted_iota(jnp.int32, (units, padded), 0)
    spot = lax.broadcasted_iota(jnp.int32, (units, padded), 1)
    within = jnp.bitwise_and(spot, step - 1)
    source = (spot - within) // step * group + within
    return jnp.where((unit == source) & (within < group), 1.0, 0.0).astype(jnp.bfloat16)


def backward_kernel(group, step, tokens, cot, seg_row, seg_column, gains, cosine, sine, qkv_act, attended,
                    hidden, normed_two, routed_grad, wq, wk, wv, wo, shin, shout,
                    base, tokens_grad, gain_grads, qkv_grad, out_grad, shin_grad, shout_grad,
                    normed, normed_turned, branch, grad_hidden, grad_one, pieces, stage, stage_sem):
    at = pl.program_id(0)
    width = tokens.shape[1]
    wide = 2 * HDIM
    low = jnp.bfloat16
    units = shin.shape[1] // 2

    def stage_copy(part, pair):
        return pltpu.make_async_copy(
            stage.at[part],
            qkv_grad.at[:, pl.ds(pl.multiple_of(part * width + pair * wide, wide), wide)],
            stage_sem.at[part],
        )

    @pl.when(at == 0)
    def _():
        unit_one = unit_of(tokens[...].astype(jnp.float32))[0]
        first = unit_one * gains[0:1, :]
        normed[...] = first.astype(low)
        normed_turned[...] = first.T.astype(low)
        pre_gate = mul(normed_two[...], shin[:, :units])
        pre_up = mul(normed_two[...], shin[:, units:])
        sigmoid = jax.nn.sigmoid(pre_gate)
        act = (pre_gate * sigmoid * pre_up).astype(low)
        spread = spread_matrix(units, shout.shape[0], group, step)
        act_spread = mul(act, spread).astype(low)
        base[...] = hidden[...] + mul(act_spread, shout[...])
        shout_grad[...] = mul(act_spread, cot[...], OVER_FIRST).astype(low)
        shout_tight = mul(spread, shout[...]).astype(low)
        grad_act = mul(cot[...], shout_tight, OVER_LAST)
        grad_up = (grad_act * pre_gate * sigmoid).astype(low)
        grad_gate = (grad_act * pre_up * sigmoid * (1.0 + pre_gate * (1.0 - sigmoid))).astype(low)
        shin_grad[:, :units] = mul(normed_two[...], grad_gate, OVER_FIRST).astype(low)
        shin_grad[:, units:] = mul(normed_two[...], grad_up, OVER_FIRST).astype(low)
        grad_two = (
            routed_grad[...]
            + mul(grad_gate, shin[:, :units], OVER_LAST)
            + mul(grad_up, shin[:, units:], OVER_LAST)
        )
        unit_two, factor_two = unit_of(hidden[...])
        gain_grads[...] = jnp.zeros_like(gain_grads)
        gain_grads[1:2, :] = jnp.sum(grad_two * unit_two, axis=0, keepdims=True)
        grad_unit = grad_two * gains[1:2, :]
        back = factor_two * (
            grad_unit - unit_two * jnp.mean(grad_unit * unit_two, axis=-1, keepdims=True)
        )
        grad_hidden[...] = cot[...].astype(jnp.float32) + back
        branch[...] = grad_hidden[...].astype(low)
        grad_one[...] = jnp.zeros_like(grad_one)

    @pl.when(at > 0)
    def _():
        pair = at - 1
        allowed = allowed_pairs(seg_row, seg_column)
        window = pl.ds(pl.multiple_of(pair * wide, wide), wide)
        out_grad[...] = mul(attended[:, window], branch[...], OVER_FIRST).astype(low)
        grad_att = mul(branch[...], wo[...], OVER_LAST).astype(low)
        for j in range(2):

            def head(part):
                start = pl.multiple_of(part * width + pair * wide + j * HDIM, HDIM)
                return qkv_act[:, pl.ds(start, HDIM)]

            queries, keys, values = head(0), head(1), head(2)
            own = slice(j * HDIM, (j + 1) * HDIM)
            grad_own = grad_att[:, own]
            probs = masked_probs(queries, keys, allowed)
            grad_probs = mul(grad_own, values, OVER_LAST)
            grad_values = mul(probs.astype(low), grad_own, OVER_FIRST)
            row_dot = jnp.sum(probs * grad_probs, axis=-1, keepdims=True)
            grad_scores = (probs * (grad_probs - row_dot)).astype(low)
            grad_queries = mul(grad_scores, keys) * HDIM ** (-0.5)
            grad_keys = mul(grad_scores, queries, OVER_FIRST) * HDIM ** (-0.5)
            for part, grad in ((0, grad_queries), (1, grad_keys), (2, grad_values)):
                if part < 2:
                    grad = grad * cosine[...] - pltpu.roll(grad, HDIM // 2, 1) * sine[...]
                pieces[part, :, own] = grad.astype(low)
        for part, weight in enumerate((wq, wk, wv)):

            @pl.when(pair > 0)
            def _(part=part):
                stage_copy(part, pair - 1).wait()

            stage[part] = mul(normed_turned[...], pieces[part]).astype(low)
            stage_copy(part, pair).start()
            grad_one[...] += mul(pieces[part], weight[...], OVER_LAST)

        @pl.when(at == pl.num_programs(0) - 1)
        def _():
            unit_one, factor_one = unit_of(tokens[...].astype(jnp.float32))
            total = grad_one[...]
            gain_grads[0:1, :] = jnp.sum(total * unit_one, axis=0, keepdims=True)
            grad_unit = total * gains[0:1, :]
            back = factor_one * (
                grad_unit - unit_one * jnp.mean(grad_unit * unit_one, axis=-1, keepdims=True)
            )
            tokens_grad[...] = grad_hidden[...] + back
            for part in range(3):
                stage_copy(part, pair).wait()


def dense_backward(group, step, tokens, cot, segments, gains, qkv_act, attended, hidden, normed_two,
                   routed_grad, qkv_low, out_low, shin_low, shout_spread):
    length, width = tokens.shape
    wide, pairs = 2 * HDIM, HEADS // 2
    cosine, sine = rope_rows(length)
    seg_row = jnp.broadcast_to(segments, (8, length))
    seg_column = jnp.broadcast_to(segments.T, (length, 128))
    low = jnp.bfloat16
    once = pl.Buffered(1)

    def whole(*shape):
        return pl.BlockSpec(shape, lambda i: (0,) * len(shape), pipeline_mode=once)

    def kept(*shape):
        return pl.BlockSpec(shape, lambda i: (0,) * len(shape))

    def columns(part):
        return pl.BlockSpec((width, wide), lambda i: (0, part * pairs + jnp.maximum(i - 1, 0)))

    rows = pl.BlockSpec((wide, width), lambda i: (jnp.maximum(i - 1, 0), 0))
    return pl.pallas_call(
        functools.partial(backward_kernel, group, step),
        grid=(pairs + 1,),
        in_specs=[
            whole(length, width), whole(length, width), whole(8, length), whole(length, 128),
            whole(8, width), whole(length, HDIM), whole(length, HDIM), whole(length, 3 * width),
            whole(length, width), whole(length, width), whole(length, width), whole(length, width),
            columns(0), columns(1), columns(2), rows,
            whole(*shin_low.shape), whole(*shout_spread.shape),
        ],
        out_specs=[
            kept(length, width), kept(length, width), kept(8, width),
            pl.BlockSpec(memory_space=pl.ANY), rows, kept(*shin_low.shape), kept(*shout_spread.shape),
        ],
        out_shape=[
            jax.ShapeDtypeStruct((length, width), jnp.float32),
            jax.ShapeDtypeStruct((length, width), jnp.float32),
            jax.ShapeDtypeStruct((8, width), jnp.float32),
            jax.ShapeDtypeStruct((width, 3 * width), low),
            jax.ShapeDtypeStruct((width, width), low),
            jax.ShapeDtypeStruct(shin_low.shape, low),
            jax.ShapeDtypeStruct(shout_spread.shape, low),
        ],
        scratch_shapes=[
            pltpu.VMEM((length, width), low), pltpu.VMEM((width, length), low),
            pltpu.VMEM((length, width), low), pltpu.VMEM((length, width), jnp.float32),
            pltpu.VMEM((length, width), jnp.float32), pltpu.VMEM((3, length, wide), low),
            pltpu.VMEM((3, width, wide), low), pltpu.SemaphoreType.DMA((3,)),
        ],
        compiler_params=pltpu.CompilerParams(
            dimension_semantics=("arbitrary",), vmem_limit_bytes=VMEM_MOST
        ),
        name="dense_backward",
    )(tokens, cot, seg_row, seg_column, gains, jnp.asarray(cosine), jnp.asarray(sine), qkv_act, attended,
      hidden, normed_two, routed_grad, qkv_low, qkv_low, qkv_low, out_low, shin_low, shout_spread)


def expert_kernel(parts, per_step, cap, *refs):
    normed, cot, info = refs[:3]
    ins, outs_w = refs[3 : 3 + parts], refs[3 + parts : 3 + 2 * parts]
    result_ref, input_ref, own_grad = refs[3 + 2 * parts : 6 + 2 * parts]
    sent = refs[6 + 2 * parts : 5 + 3 * parts]
    scratch = refs[5 + 3 * parts :]
    rows_x, rows_g, gate_col, result_acc, input_acc = scratch[:5]
    sums = (own_grad,) + tuple(scratch[5:])
    step = pl.program_id(0)
    tok = normed.shape[1]
    width = normed.shape[2]
    chunk = 256

    @pl.when(step == 0)
    def _():
        for total in sums:
            total[...] = jnp.zeros_like(total)

    slots = lax.broadcasted_iota(jnp.int32, (cap, tok), 0).astype(jnp.float32)
    for s in range(per_step):
        hit = slots == info[s, 0:1, :]
        picks = jnp.where(hit, 1.0, 0.0).astype(jnp.bfloat16)
        gates = jnp.sum(jnp.where(hit, info[s, 1:2, :], 0.0), axis=1, keepdims=True)
        window = pl.ds(s * cap, cap)
        gate_col[window, :] = jnp.broadcast_to(gates, (cap, 128))
        rows_x[window, :] = jnp.dot(picks, normed[s], preferred_element_type=jnp.float32).astype(
            jnp.bfloat16
        )
        taken = jnp.dot(picks, cot[s], preferred_element_type=jnp.float32)
        rows_g[window, :] = (gates * taken).astype(jnp.bfloat16)
    across = (((1,), (1,)), ((), ()))
    down = (((0,), (0,)), ((), ()))

    def mul(left, right, dims):
        return lax.dot_general(left, right, dims, preferred_element_type=jnp.float32)

    straight = (((1,), (0,)), ((), ()))
    for p in range(parts):
        gate_pre = mul(rows_x[...], ins[p][0], across)
        up_pre = mul(rows_x[...], ins[p][1], across)
        sigmoid = jax.nn.sigmoid(gate_pre)
        active = (gate_pre * sigmoid * up_pre).astype(jnp.bfloat16)
        grad_act = mul(rows_g[...], outs_w[p][...], across)
        grad_up = (grad_act * gate_pre * sigmoid).astype(jnp.bfloat16)
        grad_gate = (grad_act * up_pre * sigmoid * (1.0 + gate_pre * (1.0 - sigmoid))).astype(
            jnp.bfloat16
        )
        for first in range(0, width, chunk):
            window = slice(first, first + chunk)
            result = mul(active, outs_w[p][:, window], straight)
            back = mul(grad_gate, ins[p][0, :, window], straight) + mul(
                grad_up, ins[p][1, :, window], straight
            )
            if p == 0:
                result_acc[:, window] = result
                input_acc[:, window] = back
            else:
                result_acc[:, window] += result
                input_acc[:, window] += back
            sums[p][0, :, window] += mul(grad_gate, rows_x[:, window], down)
            sums[p][1, :, window] += mul(grad_up, rows_x[:, window], down)
            sums[p][2, :, window] += mul(active, rows_g[:, window], down)
    for s in range(per_step):
        hit = slots == info[s, 0:1, :]
        picks = jnp.where(hit, 1.0, 0.0).astype(jnp.bfloat16)
        window = pl.ds(s * cap, cap)
        rounded = result_acc[window, :].astype(jnp.bfloat16).astype(jnp.float32)
        weighted = (gate_col[window, 0:1] * rounded).astype(jnp.bfloat16)
        result_ref[s] = mul(picks, weighted, down).astype(jnp.bfloat16)
        input_ref[s] = mul(picks, input_acc[window, :].astype(jnp.bfloat16), down).astype(
            jnp.bfloat16
        )

    @pl.when(step == pl.num_programs(0) - 1)
    def _():
        for p in range(1, parts):
            sent[p - 1][...] = sums[p][...].astype(jnp.bfloat16)


def expert_pass(normed_all, cot_all, info, ins, outs_w, cap):
    ep_count, tok, width = normed_all.shape
    parts = len(ins)
    hidden = ins[0].shape[1]
    per_step = max(1, min(ep_count, 256 // cap))
    rows = per_step * cap
    token_spec = pl.BlockSpec((per_step, tok, width), lambda i: (i, 0, 0))
    once = pl.Buffered(1)
    in_specs = [token_spec, token_spec, pl.BlockSpec((per_step, 2, tok), lambda i: (i, 0, 0))]
    in_specs += [
        pl.BlockSpec((2, hidden, width), lambda i: (0, 0, 0), pipeline_mode=once)
    ] * parts
    in_specs += [pl.BlockSpec((hidden, width), lambda i: (0, 0), pipeline_mode=once)] * parts
    grad_spec = pl.BlockSpec((3, hidden, width), lambda i: (0, 0, 0), pipeline_mode=once)
    token_shape = jax.ShapeDtypeStruct((ep_count, tok, width), jnp.bfloat16)
    out_shape = [token_shape, token_shape, jax.ShapeDtypeStruct((3, hidden, width), jnp.float32)]
    out_shape += [jax.ShapeDtypeStruct((3, hidden, width), jnp.bfloat16)] * (parts - 1)
    scratch = [
        pltpu.VMEM((rows, width), jnp.bfloat16),
        pltpu.VMEM((rows, width), jnp.bfloat16),
        pltpu.VMEM((rows, 128), jnp.float32),
        pltpu.VMEM((rows, width), jnp.float32),
        pltpu.VMEM((rows, width), jnp.float32),
    ] + [pltpu.VMEM((3, hidden, width), jnp.float32)] * (parts - 1)
    found = pl.pallas_call(
        functools.partial(expert_kernel, parts, per_step, cap),
        grid=(ep_count // per_step,),
        in_specs=in_specs,
        out_specs=[token_spec, token_spec] + [grad_spec] * parts,
        out_shape=out_shape,
        scratch_shapes=scratch,
        compiler_params=pltpu.CompilerParams(
            dimension_semantics=("arbitrary",), vmem_limit_bytes=VMEM_MOST
        ),
        cost_estimate=pl.CostEstimate(
            flops=18 * ep_count * cap * parts * hidden * width,
            bytes_accessed=8 * ep_count * tok * width + 30 * parts * hidden * width,
            transcendentals=ep_count * cap * parts * hidden,
        ),
        name="expert_pass",
    )(normed_all, cot_all, info, *ins, *outs_w)
    return found[0], found[1], found[2], found[3:]


def nearest(place):
    count = place.na
    table = [sorted(range(count), key=lambda other: abs(other - own)) for own in range(count)]

    def chip_at(r):
        found = jnp.int32(0)
        for own in range(count):
            for rank in range(count):
                found = found + jnp.where((place.a == own) & (r == rank), table[own][rank], 0)
        return found

    return chip_at


def fused_kernel(parts, ep_count, tp_count, cap, *refs):
    normed, info, cot = refs[:3]
    w_in, w_out = refs[3 : 3 + parts], refs[3 + parts : 3 + 2 * parts]
    refs = refs[3 + 2 * parts :]
    result_ref, routed_ref, own_grad = refs[:3]
    sent = refs[3 : 2 + parts]
    scratch = refs[2 + parts :]
    tok, infos, cots, vin, vout, own, sib, sib_stage, bland, aland, res_stage = scratch[:11]
    rows_x, rows_g, gate_col, result_acc, input_acc, stage = scratch[11:17]
    sums = (own_grad,) + tuple(scratch[17 : 16 + parts])
    (tok_recv, tok_send, local_sem, cot_sem, sib_recv, sib_send, b_recv, b_send, a_recv, a_send,
     res_sem, stage_sem) = scratch[16 + parts :]
    place = Place(ep_count, tp_count)
    na, a, b, core = place.na, place.a, place.b, place.core
    width = normed.shape[1]
    me = (a * 2 + b) * 2 + core
    chip_at = nearest(place)
    chunk = 256

    def device(a_, b_, core_):
        return ((a_ * 2 + b_) * 2 + core_, place.t)

    sibling, across = device(a, b, 1 - core), device(a, 1 - b, core)
    barrier = pltpu.get_barrier_semaphore()
    for target in (sibling, across):
        pl.semaphore_signal(barrier, inc=1, device_id=target, device_id_type=MESH)
    for step in range(1, na):
        pl.semaphore_signal(
            barrier, inc=1, device_id=device(lax.rem(a + step, na), b, core), device_id_type=MESH
        )
    pl.semaphore_wait(barrier, na + 1)

    def hop(index, number, target, first=False):
        return [
            pltpu.make_async_remote_copy(
                src_ref=own_block if first else held.at[index],
                dst_ref=held.at[index],
                send_sem=tok_send.at[k, number],
                recv_sem=tok_recv.at[k, index],
                device_id=target,
                device_id_type=MESH,
            )
            for k, (own_block, held) in enumerate(((normed, tok), (info, infos)))
        ]

    def start(copies):
        for copy in copies:
            copy.start()

    def arrived(index):
        for k, held in enumerate((tok, infos)):
            pltpu.make_async_copy(held.at[index], held.at[index], tok_recv.at[k, index]).wait()

    ends = []

    def launch(on, copies):
        def finish():
            for copy in copies:
                copy.wait_send()

        guarded(on, lambda: start(copies))
        ends.append((on, finish))

    up, down_ok = a + 1 < na, a > 0
    launch(up, hop(me, 0, device(a + 1, b, core), True))
    launch(down_ok, hop(me, 1, device(a - 1, b, core), True))
    launch(None, hop(me, 2, across, True))
    launch(None, hop(me, 3, sibling, True))
    loads = [pltpu.make_async_copy(normed, tok.at[me], local_sem.at[0])]
    loads.append(pltpu.make_async_copy(info, infos.at[me], local_sem.at[1]))
    for p in range(parts):
        loads.append(pltpu.make_async_copy(w_in[p], vin.at[p], local_sem.at[2 + 2 * p]))
        loads.append(pltpu.make_async_copy(w_out[p], vout.at[p], local_sem.at[3 + 2 * p]))
    start(loads)

    def chip_of(k):
        side = lax.rem(k, 2)
        return chip_at(k // 2) * 2 + jnp.where(side == 0, b, 1 - b)

    def cot_copies(k):
        chip, buffer = chip_of(k), lax.rem(k, 2)
        return [
            pltpu.make_async_copy(cot.at[chip * 2 + j], cots.at[buffer, j], cot_sem.at[buffer, j])
            for j in range(2)
        ]

    start(cot_copies(jnp.int32(0)))
    for total in sums:
        total[...] = jnp.zeros_like(total)
    for load in loads:
        load.wait()

    def from_a(r):
        other = chip_at(r)
        index = (other * 2 + b) * 2 + core
        arrived(index)
        first = 4 + 3 * (r - 1)
        beyond = jnp.where(other > a, a - 1, a + 1)
        on = (beyond >= 0) & (beyond < na)
        copies = hop(index, first, device(beyond, b, core))
        pl.when(on)(lambda: start(copies))
        start(hop(index, first + 1, across))
        start(hop(index, first + 2, sibling))

    def from_b(r):
        index = (chip_at(r) * 2 + 1 - b) * 2 + core
        arrived(index)
        start(hop(index, 4 + 3 * (na - 1) + r, sibling))

    def sent_from_a(r):
        other = chip_at(r)
        index = (other * 2 + b) * 2 + core
        first = 4 + 3 * (r - 1)
        beyond = jnp.where(other > a, a - 1, a + 1)
        on = (beyond >= 0) & (beyond < na)

        def finish(number):
            for copy in hop(index, number, sibling):
                copy.wait_send()

        pl.when(on)(lambda: finish(first))
        finish(first + 1)
        finish(first + 2)

    def sib_wait(chip):
        pltpu.make_async_copy(sib.at[chip], sib.at[chip], sib_recv.at[chip]).wait()

    def to_b(r):
        chip = chip_at(r) * 2 + 1 - b
        sib_wait(chip)
        add_into(own.at[chip], [own.at[chip], sib.at[chip]], own.dtype)
        pltpu.make_async_remote_copy(
            src_ref=own.at[chip],
            dst_ref=bland.at[r],
            send_sem=b_send.at[r],
            recv_sem=b_recv.at[r],
            device_id=across,
            device_id_type=MESH,
        ).start()

    def b_wait(r):
        pltpu.make_async_copy(bland.at[r], bland.at[r], b_recv.at[r]).wait()

    def to_a(r):
        other = chip_at(r)
        chip = other * 2 + b
        sib_wait(chip)
        b_wait(r)
        add_into(own.at[chip], [own.at[chip], sib.at[chip], bland.at[r]], own.dtype)
        pltpu.make_async_remote_copy(
            src_ref=own.at[chip],
            dst_ref=aland.at[a],
            send_sem=a_send.at[r],
            recv_sem=a_recv.at[a],
            device_id=device(other, b, core),
            device_id_type=MESH,
        ).start()

    over_last = (((1,), (1,)), ((), ()))
    over_first = (((0,), (0,)), ((), ()))
    straight = (((1,), (0,)), ((), ()))

    def mul(left, right, dims):
        return lax.dot_general(left, right, dims, preferred_element_type=jnp.float32)

    slots = lax.broadcasted_iota(jnp.int32, (cap, normed.shape[0]), 0).astype(jnp.float32)

    def picks_of(source):
        return slots == infos[source, pl.ds(me, 1), :]

    def work(k, carry):
        chip, buffer = chip_of(k), lax.rem(k, 2)

        @pl.when(k + 1 < 2 * na)
        def _():
            start(cot_copies(k + 1))

        for r in range(na):
            if r == 1:
                pl.when(k == 1)(functools.partial(from_a, r))
            pl.when(k == 2 * r + 1)(functools.partial(from_b, r))
        pl.when(k == 2 * na - 2)(functools.partial(to_b, 1))
        arrived(chip * 2 + 1 - core)
        for copy in cot_copies(k):
            copy.wait()
        for j in range(2):
            hit = picks_of(chip * 2 + j)
            picks = jnp.where(hit, 1.0, 0.0).astype(jnp.bfloat16)
            gate_row = infos[chip * 2 + j, pl.ds(ep_count + me, 1), :]
            gates = jnp.sum(jnp.where(hit, gate_row, 0.0), axis=1, keepdims=True)
            window = pl.ds(j * cap, cap)
            gate_col[window, :] = jnp.broadcast_to(gates, (cap, 128))
            rows_x[window, :] = mul(picks, tok[chip * 2 + j], straight).astype(jnp.bfloat16)
            taken = mul(picks, cots[buffer, j], straight)
            rows_g[window, :] = (gates * taken).astype(jnp.bfloat16)
        for p in range(parts):
            gate_pre = mul(rows_x[...], vin[p, 0], over_last)
            up_pre = mul(rows_x[...], vin[p, 1], over_last)
            sigmoid = jax.nn.sigmoid(gate_pre)
            active = (gate_pre * sigmoid * up_pre).astype(jnp.bfloat16)
            grad_act = mul(rows_g[...], vout[p], over_last)
            grad_up = (grad_act * gate_pre * sigmoid).astype(jnp.bfloat16)
            grad_gate = (
                grad_act * up_pre * sigmoid * (1.0 + gate_pre * (1.0 - sigmoid))
            ).astype(jnp.bfloat16)
            for first in range(0, width, chunk):
                window = slice(first, first + chunk)
                result = mul(active, vout[p, :, window], straight)
                back = mul(grad_gate, vin[p, 0, :, window], straight) + mul(
                    grad_up, vin[p, 1, :, window], straight
                )
                if p == 0:
                    result_acc[:, window] = result
                    input_acc[:, window] = back
                else:
                    result_acc[:, window] += result
                    input_acc[:, window] += back
                sums[p][0, :, window] += mul(grad_gate, rows_x[:, window], over_first)
                sums[p][1, :, window] += mul(grad_up, rows_x[:, window], over_first)
                sums[p][2, :, window] += mul(active, rows_g[:, window], over_first)
            if p == 0:
                for r in range(2, na):
                    pl.when(k == 2 * r - 2)(functools.partial(from_a, r))
                    if r < na - 1:
                        pl.when(k == 2 * na - 2)(functools.partial(to_b, r))

        @pl.when(k > 0)
        def _():
            pltpu.make_async_copy(sib_stage, sib_stage, sib_send.at[0]).wait()
            for j in range(2):
                pltpu.make_async_copy(res_stage.at[j], res_stage.at[j], res_sem.at[j]).wait()

        for other in range(2):
            j = 1 - core if other == 0 else core
            source = chip * 2 + j
            picks = jnp.where(picks_of(source), 1.0, 0.0).astype(jnp.bfloat16)
            window = pl.ds(pl.multiple_of(j * cap, cap), cap)
            back = mul(picks, input_acc[window, :].astype(jnp.bfloat16), over_first)
            if other == 0:
                sib_stage[...] = back.astype(jnp.bfloat16)
                pltpu.make_async_remote_copy(
                    src_ref=sib_stage,
                    dst_ref=sib.at[chip],
                    send_sem=sib_send.at[0],
                    recv_sem=sib_recv.at[chip],
                    device_id=sibling,
                    device_id_type=MESH,
                ).start()
            else:
                own[chip] = back.astype(jnp.bfloat16)
            rounded = result_acc[window, :].astype(jnp.bfloat16).astype(jnp.float32)
            weighted = (gate_col[window, 0:1] * rounded).astype(jnp.bfloat16)
            res_stage[other] = mul(picks, weighted, over_first).astype(jnp.bfloat16)
            pltpu.make_async_copy(res_stage.at[other], result_ref.at[source], res_sem.at[other]).start()
        return carry

    lax.fori_loop(0, 2 * na, work, 0)
    to_b(na - 1)
    for p in range(1, parts):
        for q in range(3):
            if p > 1 or q > 0:
                pltpu.make_async_copy(stage, stage, stage_sem.at[0]).wait()
            stage[...] = sums[p][q].astype(jnp.bfloat16)
            pltpu.make_async_copy(stage, sent[p - 1].at[q], stage_sem.at[0]).start()
    for r in range(1, na):
        if r == na - 1:
            to_b(0)
        to_a(r)
    chip = a * 2 + b
    sib_wait(chip)
    b_wait(0)
    add_into(routed_ref, [own.at[chip], sib.at[chip], bland.at[0]], jnp.float32)
    for r in range(1, na):
        other = chip_at(r)
        pltpu.make_async_copy(aland.at[other], aland.at[other], a_recv.at[other]).wait()
        add_into(routed_ref, [routed_ref, aland.at[other]], jnp.float32)
    for on, finish in ends:
        guarded(on, finish)
    for r in range(na):
        if r:
            sent_from_a(r)
            pltpu.make_async_copy(own.at[0], own.at[0], a_send.at[r]).wait()
        for copy in hop(me, 4 + 3 * (na - 1) + r, sibling):
            copy.wait_send()
        pltpu.make_async_copy(own.at[0], own.at[0], b_send.at[r]).wait()
    pltpu.make_async_copy(sib_stage, sib_stage, sib_send.at[0]).wait()
    for j in range(2):
        pltpu.make_async_copy(res_stage.at[j], res_stage.at[j], res_sem.at[j]).wait()
    pltpu.make_async_copy(stage, stage, stage_sem.at[0]).wait()


def fused_experts(ep_count, tp_count, collective_id, normed, info, cot_all, ins, outs_w, cap):
    place = Place(ep_count, tp_count)
    tok, width = normed.shape
    parts = len(ins)
    hidden = ins[0].shape[1]
    na, chips, rows = place.na, 2 * place.na, 2 * cap
    low = jnp.bfloat16
    anywhere = pl.BlockSpec(memory_space=pl.ANY)
    inside = pl.BlockSpec(memory_space=pltpu.VMEM)
    out_shape = [
        jax.ShapeDtypeStruct((ep_count, tok, width), low),
        jax.ShapeDtypeStruct((tok, width), jnp.float32),
        jax.ShapeDtypeStruct((3, hidden, width), jnp.float32),
    ] + [jax.ShapeDtypeStruct((3, hidden, width), low)] * (parts - 1)
    scratch = [
        pltpu.VMEM((ep_count, tok, width), low),
        pltpu.VMEM((ep_count, 2 * ep_count, tok), jnp.float32),
        pltpu.VMEM((2, 2, tok, width), low),
        pltpu.VMEM((parts, 2, hidden, width), low),
        pltpu.VMEM((parts, hidden, width), low),
        pltpu.VMEM((chips, tok, width), low),
        pltpu.VMEM((chips, tok, width), low),
        pltpu.VMEM((tok, width), low),
        pltpu.VMEM((na, tok, width), low),
        pltpu.VMEM((na, tok, width), low),
        pltpu.VMEM((2, tok, width), low),
        pltpu.VMEM((rows, width), low),
        pltpu.VMEM((rows, width), low),
        pltpu.VMEM((rows, 128), jnp.float32),
        pltpu.VMEM((rows, width), jnp.float32),
        pltpu.VMEM((rows, width), jnp.float32),
        pltpu.VMEM((hidden, width), low),
    ] + [pltpu.VMEM((3, hidden, width), jnp.float32)] * (parts - 1)
    dma = pltpu.SemaphoreType.DMA
    scratch += [
        dma((2, ep_count)), dma((2, 4 + 3 * (na - 1) + na)), dma((2 + 2 * parts,)), dma((2, 2)),
        dma((chips,)), dma((1,)), dma((na,)), dma((na,)), dma((na,)), dma((na,)), dma((2,)), dma((1,)),
    ]
    found = pl.pallas_call(
        functools.partial(fused_kernel, parts, ep_count, tp_count, cap),
        in_specs=[anywhere] * (3 + 2 * parts),
        out_specs=[anywhere, inside, inside] + [anywhere] * (parts - 1),
        out_shape=out_shape,
        scratch_shapes=scratch,
        compiler_params=pltpu.CompilerParams(
            collective_id=collective_id, has_side_effects=True, vmem_limit_bytes=VMEM_MOST
        ),
        name="fused_experts",
    )(normed, info, cot_all, *ins, *outs_w)
    return found[0], found[1], found[2], found[3:]


def adam_update(weight, gradient, first, second, clip_scale, rate, decay):
    clipped = gradient * clip_scale
    first_new = BETA_ONE * first + (1.0 - BETA_ONE) * clipped
    second_new = BETA_TWO * second + (1.0 - BETA_TWO) * clipped * clipped
    corr_one = 1.0 - BETA_ONE**STEP
    corr_two = 1.0 - BETA_TWO**STEP
    stepped = first_new / corr_one / (jnp.sqrt(second_new / corr_two) + ADAM_EPS)
    weight_new = weight - rate * (stepped + decay * weight)
    return (weight_new, first_new, second_new, weight_new.astype(jnp.bfloat16))


def per_device(
    tokens,
    cotangent,
    segments,
    routes,
    gates,
    qkv_weight,
    qkv_first,
    qkv_second,
    out_weight,
    out_first,
    out_second,
    shared_in,
    shared_in_first,
    shared_in_second,
    shared_out,
    shared_out_first,
    shared_out_second,
    expert_in,
    expert_in_first,
    expert_in_second,
    expert_out,
    expert_out_first,
    expert_out_second,
    norm_gains,
    gains_first,
    gains_second,
):
    tok_count = tokens.shape[0]
    width = tokens.shape[1]
    ep_count = lax.axis_size("ep")
    tp_count = lax.axis_size("tp")
    devices = ep_count * tp_count
    capacity = tok_count * 8 // ep_count
    low = jnp.bfloat16
    in_own, out_own = expert_in[0].astype(low), expert_out[0].astype(low)
    gain_columns = jnp.pad(norm_gains.T.astype(low), ((0, 0), (0, 126)))
    group = shared_out.shape[0]
    step = 16 * ((group + 15) // 16)
    while step & (step - 1):
        step += 16
    shout_own = jnp.pad(shared_out.astype(low), ((0, step - group), (0, 0)))
    qkv_low, out_low, gains_low, cot_all, in_others, out_others, shin_low, shout_low = gather(
        ep_count,
        tp_count,
        1,
        "gather_weights",
        [
            ("auv", [qkv_weight.astype(low), out_weight.astype(low), gain_columns]),
            ("ab", [cotangent]),
            ("t", [in_own, out_own]),
            ("tba", [shared_in.astype(low), shout_own]),
        ],
    )
    qkv_low = qkv_low.reshape(width, 3 * width)
    out_low = out_low.reshape(width, width)
    shin_low = shin_low.reshape(width, 2 * FF)
    shout_low = shout_low.reshape(devices * step, width)
    gains = jnp.pad(gains_low.reshape(width, 128)[:, :2].T.astype(jnp.float32), ((0, 6), (0, 0)))
    ins_low = [in_own] + [in_others[s] for s in range(tp_count - 1)]
    outs_low = [out_own] + [out_others[s] for s in range(tp_count - 1)]
    expert_ids = jnp.arange(ep_count, dtype=jnp.int32)
    chosen = routes[:, :, None] == expert_ids[None, None, :]
    onehot = jnp.sum(chosen.astype(jnp.float32), axis=1)
    gate_of = jnp.sum(jnp.where(chosen, gates[:, :, None], 0.0), axis=1)
    earlier = jnp.tril(jnp.ones((tok_count, tok_count), low), -1)
    rank = jnp.dot(earlier, onehot.astype(low), preferred_element_type=jnp.float32)
    slot_of = jnp.where(onehot > 0.0, rank, -1.0)
    info_own = jnp.concatenate([slot_of, gate_of], axis=1).T
    qkv_act, attended, hidden, normed_two = attention_forward(
        tokens, segments, gains, qkv_low, out_low
    )
    chips = ep_count // 2
    held = tok_count * width * 2 * (ep_count + 3 * chips + 12) + 9 * tp_count * expert_in.size
    if Place(ep_count, tp_count).nb == 2 and held <= VMEM_MOST * 9 // 10:
        result_part, routed_grad, own_grad, sent_grads = fused_experts(
            ep_count, tp_count, 3, normed_two, info_own, cot_all, ins_low, outs_low, capacity
        )
    else:
        normed_all, info_all = gather(
            ep_count, tp_count, 2, "gather_tokens", [("ab", [normed_two, info_own])]
        )
        info = lax.dynamic_index_in_dim(
            info_all.reshape(ep_count, 2, ep_count, tok_count),
            lax.axis_index("ep"),
            axis=2,
            keepdims=False,
        )
        result_part, input_part, own_grad, sent_grads = expert_pass(
            normed_all, cot_all, info, ins_low, outs_low, capacity
        )
        (routed_grad,) = scatter_add(ep_count, tp_count, 3, "scatter_inputs", [("ab", [input_part])])
    base, tokens_grad, gain_grads, qkv_grad, out_grad, shin_grad, shout_grad = dense_backward(
        group, step, tokens, cotangent, segments, gains, qkv_act, attended, hidden, normed_two,
        routed_grad, qkv_low, out_low, shin_low, shout_low,
    )
    gain_rows = jnp.pad(gain_grads[:2].T.astype(low), ((0, 0), (0, 126)))

    def by_owner(grad):
        return grad.reshape(devices, -1, grad.shape[1])

    qkv_part, out_part, gains_part, shin_part, shout_part, routed, *others = scatter_all(
        ep_count,
        tp_count,
        (4, 6, 7, 8),
        "scatter_weights",
        [
            ("auv", [by_owner(qkv_grad), by_owner(out_grad), by_owner(gain_rows)]),
            ("tba", [by_owner(shin_grad), by_owner(shout_grad)]),
            ("ab", [result_part]),
            ("t", [jnp.stack(sent_grads)]),
        ],
    )
    for shift in range(tp_count - 1):
        own_grad = own_grad + others[0][shift].astype(jnp.float32)
    block_out = (base + routed).astype(low)
    exin_part, exout_part = own_grad[None, :2], own_grad[2:]
    extra = jnp.sum(own_grad * own_grad, axis=(0, 1))[None, :]
    grad_norm = jnp.sqrt(
        sum_of_squares(
            ep_count, tp_count, 5, [qkv_part, out_part, gains_part, shin_part, shout_part], extra
        )
    )
    shout_part = shout_part[:group]
    gains_part = gains_part[:, :2].T
    clip_scale = jnp.minimum(1.0, CLIP_LEVEL / (grad_norm + 1e-06))
    qkv_new, qkv_first_new, qkv_second_new, qkv_copy = adam_update(
        qkv_weight, qkv_part, qkv_first, qkv_second, clip_scale, MATRIX_RATE, WEIGHT_DECAY
    )
    out_new, out_first_new, out_second_new, out_copy = adam_update(
        out_weight, out_part, out_first, out_second, clip_scale, MATRIX_RATE, WEIGHT_DECAY
    )
    shin_new, shin_first_new, shin_second_new, shin_copy = adam_update(
        shared_in,
        shin_part,
        shared_in_first,
        shared_in_second,
        clip_scale,
        MATRIX_RATE,
        WEIGHT_DECAY,
    )
    shout_new, shout_first_new, shout_second_new, shout_copy = adam_update(
        shared_out,
        shout_part,
        shared_out_first,
        shared_out_second,
        clip_scale,
        MATRIX_RATE,
        WEIGHT_DECAY,
    )
    exin_new, exin_first_new, exin_second_new, exin_copy = adam_update(
        expert_in,
        exin_part,
        expert_in_first,
        expert_in_second,
        clip_scale,
        MATRIX_RATE,
        WEIGHT_DECAY,
    )
    exout_new, exout_first_new, exout_second_new, exout_copy = adam_update(
        expert_out,
        exout_part,
        expert_out_first,
        expert_out_second,
        clip_scale,
        MATRIX_RATE,
        WEIGHT_DECAY,
    )
    gains_new, gains_first_new, gains_second_new, gains_copy = adam_update(
        norm_gains, gains_part, gains_first, gains_second, clip_scale, GAIN_RATE, 0.0
    )
    return (
        block_out,
        tokens_grad,
        grad_norm,
        qkv_new,
        qkv_first_new,
        qkv_second_new,
        qkv_copy,
        out_new,
        out_first_new,
        out_second_new,
        out_copy,
        shin_new,
        shin_first_new,
        shin_second_new,
        shin_copy,
        shout_new,
        shout_first_new,
        shout_second_new,
        shout_copy,
        exin_new,
        exin_first_new,
        exin_second_new,
        exin_copy,
        exout_new,
        exout_first_new,
        exout_second_new,
        exout_copy,
        gains_new,
        gains_first_new,
        gains_second_new,
        gains_copy,
    )


def solution(mesh):
    placed = (
        P(("ep", "tp"), None),
        P(("ep", "tp"), None),
        P(("ep", "tp"), None),
        P(("ep", "tp"), None),
        P(("ep", "tp"), None),
        P(("ep", "tp"), None),
        P(("ep", "tp"), None),
        P(("ep", "tp"), None),
        P(("ep", "tp"), None),
        P(("ep", "tp"), None),
        P(("ep", "tp"), None),
        P(("ep", "tp"), None),
        P(("ep", "tp"), None),
        P(("ep", "tp"), None),
        P(("ep", "tp"), None),
        P(("ep", "tp"), None),
        P(("ep", "tp"), None),
        P("ep", None, "tp", None),
        P("ep", None, "tp", None),
        P("ep", None, "tp", None),
        P("ep", "tp", None),
        P("ep", "tp", None),
        P("ep", "tp", None),
        P(None, ("ep", "tp")),
        P(None, ("ep", "tp")),
        P(None, ("ep", "tp")),
    )
    return jax.shard_map(
        per_device,
        mesh=mesh,
        in_specs=placed,
        out_specs=(
            P(("ep", "tp"), None),
            P(("ep", "tp"), None),
            P(),
            P(("ep", "tp"), None),
            P(("ep", "tp"), None),
            P(("ep", "tp"), None),
            P(("ep", "tp"), None),
            P(("ep", "tp"), None),
            P(("ep", "tp"), None),
            P(("ep", "tp"), None),
            P(("ep", "tp"), None),
            P(("ep", "tp"), None),
            P(("ep", "tp"), None),
            P(("ep", "tp"), None),
            P(("ep", "tp"), None),
            P(("ep", "tp"), None),
            P(("ep", "tp"), None),
            P(("ep", "tp"), None),
            P(("ep", "tp"), None),
            P("ep", None, "tp", None),
            P("ep", None, "tp", None),
            P("ep", None, "tp", None),
            P("ep", None, "tp", None),
            P("ep", "tp", None),
            P("ep", "tp", None),
            P("ep", "tp", None),
            P("ep", "tp", None),
            P(None, ("ep", "tp")),
            P(None, ("ep", "tp")),
            P(None, ("ep", "tp")),
            P(None, ("ep", "tp")),
        ),
        check_vma=False,
    )
```

```python
import functools
import jax
import jax.numpy as jnp
import numpy as np
from jax import lax
from jax.experimental import pallas as pl
from jax.experimental.pallas import tpu as pltpu
from jax.sharding import PartitionSpec as P

HEADS = 10
HDIM = 128
FF = 896
TOPK = 7
STEP = 10


MESH = pl.DeviceIdType.MESH
VMEM_MOST = 60 * 1024 * 1024
NEG_BIG = -1000000000.0
NORM_EPS = 1e-06
ROPE_BASE = 10000.0
CLIP_LEVEL = 1.0
BETA_ONE = 0.9
BETA_TWO = 0.95
ADAM_EPS = 1e-08
WEIGHT_DECAY = 0.1
MATRIX_RATE = 0.05
GAIN_RATE = 0.5


class Place:
    def __init__(self, ep_count, tp_count):
        chips = ep_count // 2
        nb = 1
        while nb * nb * 4 <= chips:
            nb *= 2
        self.nb, self.na, self.nt = nb, chips // nb, tp_count
        self.ep_count = ep_count
        self.wrap = chips * tp_count >= 64
        e = lax.axis_index("ep")
        self.t = lax.axis_index("tp")
        self.core = lax.rem(e, 2)
        self.b = lax.rem(e // 2, nb)
        self.a = e // (2 * nb)

    def dims(self, order):
        if "u" in order and self.nb != self.nt:
            order = "abt"
        extents = {"a": self.na, "b": self.nb, "t": self.nt, "u": self.nb, "v": self.nt}
        return tuple((name, shifts(extents[name], self.wrap)) for name in order)

    def extent(self, name):
        return {"a": self.na, "b": self.nb, "t": self.nt, "u": self.nb, "v": self.nt}[name]

    def moved(self, name, shift):
        own, extent = self.own(name), self.extent(name)
        if shift == 0:
            return own, None
        if extent == 2:
            return 1 - own, None
        if self.wrap:
            return lax.rem(own + shift + extent, extent), None
        there = own + shift
        return there, (there >= 0) & (there < extent)

    def own(self, name):
        even = self.core == 0
        if name == "u":
            return jnp.where(even, self.b, self.t)
        if name == "v":
            return jnp.where(even, self.t, self.b)
        return getattr(self, name)

    def chip(self, at):
        a = at.get("a", self.a)
        b, t = at.get("b", self.b), at.get("t", self.t)
        if "u" in at:
            even = self.core == 0
            b = jnp.where(even, at["u"], at["v"])
            t = jnp.where(even, at["v"], at["u"])
        return a, b, t

    def device(self, at, core):
        a, b, t = self.chip(at)
        return ((a * self.nb + b) * 2 + core, t)

    def index(self, at, core, whole):
        e, t = self.device(at, core)
        return e * self.nt + t if whole else e

    def slot(self, at, whole):
        a, b, t = self.chip(at)
        chip = a * self.nb + b
        return chip * self.nt + t if whole else chip


def shifts(extent, wrap):
    if extent == 1:
        return (0,)
    if extent == 2:
        return (0, 1)
    found = [0]
    for step in range(1, extent // 2 + 1 if wrap else extent):
        found += [step, -step]
    return tuple(found[:extent] if wrap else found)


def ways(spread):
    return (1,) if len(spread) == 2 else (1, -1) if len(spread) > 2 else ()


def onward(spread, shift):
    way = -1 if shift > 0 else 1
    return way if len(spread) > 2 and shift - way in spread else 0


def both(one, other):
    if one is None:
        return other
    return one if other is None else one & other


def guarded(condition, body):
    if condition is None:
        body()
    else:
        pl.when(condition)(body)


def greet(place, order):
    barrier = pltpu.get_barrier_semaphore()
    here = {name: place.own(name) for name, _ in place.dims(order)}
    pl.semaphore_signal(barrier, inc=1, device_id=place.device(here, 1 - place.core), device_id_type=MESH)
    count = jnp.int32(1)
    for name, spread in place.dims(order):
        for way in ways(spread):
            there, on = place.moved(name, way)
            target = place.device({**here, name: there}, place.core)

            def signal(target=target):
                pl.semaphore_signal(barrier, inc=1, device_id=target, device_id_type=MESH)

            guarded(on, signal)
            count = count + (1 if on is None else on.astype(jnp.int32))
    if len(order) > 2:
        for s in range(2, place.nt - 1):
            target = place.device({"t": lax.rem(place.t + s, place.nt)}, place.core)
            pl.semaphore_signal(barrier, inc=1, device_id=target, device_id_type=MESH)
            count = count + 1
    pl.semaphore_wait(barrier, count)


def relative_blocks(dims):
    blocks = [()]
    for _, spread in dims:
        blocks = [block + (shift,) for block in blocks for shift in spread]
    return blocks


def by_core(place, order):
    if isinstance(order, str):
        return [(order, None)]
    return [(order[core], place.core == core) for core in range(2)]


def longest(groups):
    return max((order if isinstance(order, str) else order[0] for order, _ in groups), key=len)


def gather_events(place, order, only, pairs, send_sems, recv_sems):
    dims = place.dims(order)
    whole = len(dims) > 2
    here = {name: place.own(name) for name, _ in dims}
    counter = [0]
    ends = []

    def copies(at, target, core_of_block, own):
        index = place.index(at, core_of_block, whole)
        number = counter[0]
        counter[0] += 1
        made = []
        for k, (block, gathered) in enumerate(pairs):
            made.append(
                pltpu.make_async_remote_copy(
                    src_ref=block if own else gathered.at[index],
                    dst_ref=gathered.at[index],
                    send_sem=send_sems.at[k, number],
                    recv_sem=recv_sems.at[k, index],
                    device_id=target,
                    device_id_type=MESH,
                )
            )
        return made

    def send(at, on, target, own, todo):
        made = copies(at, target, place.core, own)

        def start(made=made):
            for copy in made:
                copy.start()

        def finish(made=made):
            for copy in made:
                copy.wait_send()

        todo.append((on, start))
        ends.append((on, finish))

    steps = []
    times = arrival_times(dims)
    for block in relative_blocks(dims):
        at, valid = dict(here), only
        for (name, _), shift in zip(dims, block):
            at[name], on = place.moved(name, shift)
            valid = both(valid, on)
        last = max([k for k, shift in enumerate(block) if shift], default=-1)
        own = last < 0
        todo = []
        for k in range(len(dims) - 1, -1, -1):
            name, spread = dims[k]
            if k < last:
                continue
            if k == last:
                way = onward(spread, block[k])
                sent = [way] if way else []
            else:
                sent = ways(spread)
            for way in sent:
                there, on = place.moved(name, way)
                target = place.device({**here, name: there}, place.core)
                send(at, both(valid, on), target, own, todo)
        send(at, valid, place.device(here, 1 - place.core), own, todo)
        index = place.index(at, place.core, whole)

        def step(index=index, valid=valid, todo=todo, own=own):
            def body():
                if not own:
                    for k, (_, gathered) in enumerate(pairs):
                        pltpu.make_async_copy(gathered.at[index], gathered.at[index], recv_sems.at[k, index]).wait()

            guarded(valid, body)
            for on, start in todo:
                guarded(on, start)

        steps.append((times[block], step))
        other = place.index(at, 1 - place.core, whole)

        def arrived(other=other):
            for k, (_, gathered) in enumerate(pairs):
                pltpu.make_async_copy(gathered.at[other], gathered.at[other], recv_sems.at[k, other]).wait()

        ends.append((valid, arrived))
    return steps, ends, counter[0]


def arrival_times(dims):
    times = {(): 0}
    for _, spread in dims:
        earlier = sorted(times, key=lambda block: times[block])
        found = {block + (0,): times[block] for block in earlier}
        for shift in spread:
            for i, block in enumerate(earlier):
                if shift:
                    far = abs(shift)
                    found[block + (shift,)] = max(times[block] + far, (far - 1) * len(earlier) + i + 1)
        times = found
    return times


def count_gather_sends(dims):
    total = 0
    for block in relative_blocks(dims):
        last = max([k for k, shift in enumerate(block) if shift], default=-1)
        for k, (_, spread) in enumerate(dims):
            if k > last:
                total += len(ways(spread))
            elif k == last and onward(spread, block[k]):
                total += 1
        total += 1
    return total


def exchange_copies(place, blocks, others, send_sems, recv_sems):
    copies = []
    for s in range(1, place.nt):
        back = blocks[0].shape == others[0].shape
        there = lax.rem(place.t + (s if back else place.nt - s), place.nt)
        target = place.device({"t": there}, place.core)
        for k, (block, other) in enumerate(zip(blocks, others)):
            copies.append(
                pltpu.make_async_remote_copy(
                    src_ref=block.at[s - 1] if back else block,
                    dst_ref=other.at[s - 1],
                    send_sem=send_sems.at[k, s - 1],
                    recv_sem=recv_sems.at[k, s - 1],
                    device_id=target,
                    device_id_type=MESH,
                )
            )
    return copies


def gather_kernel(ep_count, tp_count, groups, *refs):
    count = sum(n for _, n in groups)
    blocks, gathered, scratch = refs[:count], refs[count : 2 * count], refs[2 * count :]
    place = Place(ep_count, tp_count)
    greet(place, longest(groups))
    steps, ends, first = [], [], 0
    local, swaps = [], []
    for order, n in groups:
        mine_in, mine_out = blocks[first : first + n], gathered[first : first + n]
        first += n
        if order == "t":
            swaps += exchange_copies(place, mine_in, mine_out, scratch[0], scratch[1])
            scratch = scratch[2:]
            continue
        send_sems, recv_sems, own_sems = scratch[:3]
        scratch = scratch[3:]
        pairs = list(zip(mine_in, mine_out))
        more, finish = [], []
        for lines, only in by_core(place, order):
            found = gather_events(place, lines, only, pairs, send_sems, recv_sems)
            more += found[0]
            finish += found[1]
        lines = by_core(place, order)[0][0]
        size = sum(block.shape[0] * block.shape[1] * (4 if block.dtype == jnp.float32 else 2) for block in mine_in)
        steps += [(key * size, len(steps) + i, step) for i, (key, step) in enumerate(more)]
        ends += finish
        here = {name: place.own(name) for name, _ in place.dims(lines)}
        mine = place.index(here, place.core, len(lines) > 2)
        for k, (block, out) in enumerate(pairs):
            local.append(pltpu.make_async_copy(block, out.at[mine], own_sems.at[k]))
    steps.sort(key=lambda entry: entry[:2])
    lead = sum(1 for key, _, _ in steps if key == 0)
    for _, _, step in steps[:lead]:
        step()
    for copy in swaps + local:
        copy.start()
    for _, _, step in steps[lead:]:
        step()
    for on, finish in ends:
        guarded(on, finish)
    for copy in swaps + local:
        copy.wait()


def gather(ep_count, tp_count, collective_id, name, groups):
    arrays, shapes, scratch = [], [], []
    place = Place(ep_count, tp_count)
    for order, blocks in groups:
        lines = [line for line, _ in by_core(place, order)]
        total = ep_count * tp_count if len(lines[0]) > 2 else ep_count if order != "t" else tp_count - 1
        for block in blocks:
            arrays.append(block)
            shapes.append(jax.ShapeDtypeStruct((total,) + block.shape, block.dtype))
        if order == "t":
            scratch += [pltpu.SemaphoreType.DMA((len(blocks), total))] * 2
            continue
        sends = max(count_gather_sends(place.dims(line)) for line in lines)
        scratch += [
            pltpu.SemaphoreType.DMA((len(blocks), sends)),
            pltpu.SemaphoreType.DMA((len(blocks), total)),
            pltpu.SemaphoreType.DMA((len(blocks),)),
        ]
    return pl.pallas_call(
        functools.partial(
            gather_kernel, ep_count, tp_count, tuple((order, len(blocks)) for order, blocks in groups)
        ),
        out_shape=tuple(shapes),
        in_specs=[pl.BlockSpec(memory_space=pl.ANY)] * len(arrays),
        out_specs=tuple([pl.BlockSpec(memory_space=pl.ANY)] * len(arrays)),
        scratch_shapes=scratch,
        compiler_params=pltpu.CompilerParams(collective_id=collective_id, has_side_effects=True),
        name=name,
    )(*arrays)


def add_into(target, sources, dtype):
    rows, columns = target.shape
    piece = 128
    while columns % (piece * 2) == 0 and rows * piece * 2 <= 40 * 1024:
        piece *= 2

    def body(i, carry):
        window = pl.ds(pl.multiple_of(i * piece, piece), piece)
        total = sources[0][:, window].astype(jnp.float32)
        for source in sources[1:]:
            total = total + source[:, window].astype(jnp.float32)
        target[:, window] = total.astype(dtype)
        return carry

    lax.fori_loop(0, columns // piece, body, 0)


def norm_kernel(ep_count, tp_count, count, *refs):
    parts, extra, out = refs[:count], refs[count], refs[count + 1]
    tile, tiles, send, recv = refs[count + 2 :]
    devices = ep_count * tp_count
    me = lax.axis_index("ep") * tp_count + lax.axis_index("tp")

    def place(i):
        other = lax.rem(me + i, devices)
        return other, (other // tp_count, lax.rem(other, tp_count))

    barrier = pltpu.get_barrier_semaphore()

    def signal(i, carry):
        pl.semaphore_signal(barrier, inc=1, device_id=place(i)[1], device_id_type=MESH)
        return carry

    lax.fori_loop(1, devices, signal, 0)
    tile[...] = jnp.zeros_like(tile)
    for first in range(0, extra.shape[1], 128):
        tile[0:1, :] += extra[:, first : first + 128]
    for part in parts:

        def add(i, carry, part=part):
            piece = part[:, pl.ds(pl.multiple_of(i * 128, 128), 128)]
            tile[0:1, :] += jnp.sum(piece * piece, axis=0, keepdims=True)
            return carry

        lax.fori_loop(0, part.shape[1] // 128, add, 0)
    pl.semaphore_wait(barrier, devices - 1)

    def share(i, carry):
        pltpu.make_async_remote_copy(
            src_ref=tile,
            dst_ref=tiles.at[me],
            send_sem=send.at[i],
            recv_sem=recv.at[me],
            device_id=place(i)[1],
            device_id_type=MESH,
        ).start()
        return carry

    lax.fori_loop(1, devices, share, 0)
    out[...] = tile[...]

    def collect(i, carry):
        other = place(i)[0]
        pltpu.make_async_copy(tiles.at[other], tiles.at[other], recv.at[other]).wait()
        out[...] += tiles[other]
        return carry

    lax.fori_loop(1, devices, collect, 0)

    def sent(i, carry):
        pltpu.make_async_copy(tile, tile, send.at[i]).wait()
        return carry

    lax.fori_loop(1, devices, sent, 0)


def sum_of_squares(ep_count, tp_count, collective_id, parts, extra):
    devices = ep_count * tp_count
    inside = pl.BlockSpec(memory_space=pltpu.VMEM)
    total = pl.pallas_call(
        functools.partial(norm_kernel, ep_count, tp_count, len(parts)),
        out_shape=jax.ShapeDtypeStruct((8, 128), jnp.float32),
        in_specs=[inside] * (len(parts) + 1),
        out_specs=inside,
        scratch_shapes=[
            pltpu.VMEM((8, 128), jnp.float32),
            pltpu.VMEM((devices, 8, 128), jnp.float32),
            pltpu.SemaphoreType.DMA((devices,)),
            pltpu.SemaphoreType.DMA((devices,)),
        ],
        compiler_params=pltpu.CompilerParams(collective_id=collective_id, has_side_effects=True),
        name="sum_of_squares",
    )(*parts, extra)
    return jnp.sum(total)


def scatter_order(dims):
    blocks = sorted(relative_blocks(dims), key=lambda block: -sum(abs(s) for s in block))
    return sorted(blocks, key=lambda block: -max([k for k, s in enumerate(block) if s], default=-1))


def scatter_events(place, order, only, partials, outs, refs):
    count = len(partials)
    dims = place.dims(order)
    whole = len(dims) > 2
    here = {name: place.own(name) for name, _ in dims}
    owns, sibs = refs[:count], refs[count : 2 * count]
    lands = [refs[(2 + k) * count : (3 + k) * count] for k in range(len(dims))]
    sems = refs[(2 + len(dims)) * count :]
    own_sem, sib_send, sib_recv, line_send = sems[:4]
    line_recv = sems[4:]
    blocks = scatter_order(dims)
    info = {}
    starts, steps, ends = [], [], []
    for block in blocks:
        at, valid = dict(here), only
        for (name, _), shift in zip(dims, block):
            at[name], on = place.moved(name, shift)
            valid = both(valid, on)
        slot = place.slot(at, whole)
        local = [
            pltpu.make_async_copy(
                partials[k].at[place.index(at, place.core, whole)], owns[k].at[slot], own_sem.at[k, slot]
            )
            for k in range(count)
        ]
        across = [
            pltpu.make_async_remote_copy(
                src_ref=partials[k].at[place.index(at, 1 - place.core, whole)],
                dst_ref=sibs[k].at[slot],
                send_sem=sib_send.at[k, slot],
                recv_sem=sib_recv.at[k, slot],
                device_id=place.device(here, 1 - place.core),
                device_id_type=MESH,
            )
            for k in range(count)
        ]

        def start(local=local, across=across):
            for copy in across + local:
                copy.start()

        def finish(across=across):
            for copy in across:
                copy.wait_send()

        starts.append((valid, start))
        ends.append((valid, finish))
        info[block] = (at, valid, slot, local, across)

    def land_slot(level, at, shift, side):
        inner, wide = 0, 1
        for name, _ in dims[:level]:
            inner = inner * place.extent(name) + at[name]
            wide = wide * place.extent(name)
        return landings(dims[level][1]).index((shift, side)) * wide + inner

    number = 0
    for block in blocks:
        at, valid, slot, local, across = info[block]
        todo = []
        last = max([k for k, shift in enumerate(block) if shift], default=-1)
        extra_refs = []
        for level in range(len(dims) - 1, max(last, 0) - 1, -1):
            name, spread = dims[level]
            for shift, side in landings(spread):
                if shift == block[level]:
                    _, on = place.moved(name, side)
                    extra_refs.append((level, land_slot(level, at, shift, side), on))

        def arrive(local=local, across=across):
            for copy in local:
                copy.wait()
            for copy in across:
                copy.wait_recv()

        todo.append((valid, arrive))
        for k in range(count):
            sure = [owns[k].at[slot], sibs[k].at[slot]]
            maybe = []
            for level, spot, on in extra_refs:
                ref = lands[level][k].at[spot]

                def wait(ref=ref, k=k, level=level, spot=spot):
                    pltpu.make_async_copy(ref, ref, line_recv[level].at[k, spot]).wait()

                todo.append((both(valid, on), wait))
                if on is None:
                    sure.append(ref)
                else:
                    maybe.append((ref, on))
            if last >= 0:
                target, dtype = owns[k].at[slot], owns[k].dtype
            else:
                target, dtype = outs[k], outs[k].dtype

            def add(sure=sure, maybe=maybe, target=target, dtype=dtype):
                if not maybe:
                    add_into(target, sure, dtype)
                elif len(maybe) == 1:
                    ((ref, on),) = maybe
                    pl.when(on)(lambda: add_into(target, sure + [ref], dtype))
                    pl.when(jnp.logical_not(on))(lambda: add_into(target, sure, dtype))
                else:
                    (low, on_low), (high, on_high) = maybe
                    pl.when(on_low & on_high)(lambda: add_into(target, sure + [low, high], dtype))
                    pl.when(on_low & jnp.logical_not(on_high))(lambda: add_into(target, sure + [low], dtype))
                    pl.when(on_high & jnp.logical_not(on_low))(lambda: add_into(target, sure + [high], dtype))

            todo.append((valid, add))
        if last >= 0:
            name, spread = dims[last]
            way = 1 if block[last] > 0 else -1
            there, _ = place.moved(name, way)
            spot = land_slot(last, at, block[last] - way, -way if len(spread) > 2 else 1)
            made = [
                pltpu.make_async_remote_copy(
                    src_ref=owns[k].at[slot],
                    dst_ref=lands[last][k].at[spot],
                    send_sem=line_send.at[k, number],
                    recv_sem=line_recv[last].at[k, spot],
                    device_id=place.device({**here, name: there}, place.core),
                    device_id_type=MESH,
                )
                for k in range(count)
            ]
            number += 1

            def start(made=made):
                for copy in made:
                    copy.start()

            def finish(made=made):
                for copy in made:
                    copy.wait_send()

            todo.append((valid, start))
            ends.append((valid, finish))
        steps.append(todo)
    return starts, steps, ends


def scatter_sizes(place, order):
    found = []
    for line, _ in by_core(place, order):
        dims = place.dims(line)
        slots, lands = 1, []
        for name, spread in dims:
            lands.append(len(landings(spread)) * slots)
            slots *= place.extent(name)
        found.append((slots, lands, sum(1 for block in relative_blocks(dims) if any(block))))
    lands = [max(wide) for wide in zip(*[entry[1] for entry in found])]
    return found[0][0], lands, max(entry[2] for entry in found)


def scatter_scratch(place, order, partials):
    slots, lands, sends = scatter_sizes(place, order)
    count, dma = len(partials), pltpu.SemaphoreType.DMA
    scratch = []
    for wide in [slots, slots] + lands:
        scratch += [pltpu.VMEM((wide,) + p.shape[1:], p.dtype) for p in partials]
    return scratch + [dma((count, slots))] * 3 + [dma((count, sends))] + [dma((count, wide)) for wide in lands]


def scatter_kernel(ep_count, tp_count, groups, *refs):
    count = sum(n for _, n in groups)
    partials, outs, refs = refs[:count], refs[count : 2 * count], refs[2 * count :]
    place = Place(ep_count, tp_count)
    greet(place, longest(groups))
    starts, steps, ends, swaps, first = [], [], [], [], 0
    for order, n in groups:
        mine_in, mine_out = partials[first : first + n], outs[first : first + n]
        first += n
        if order == "t":
            swaps += exchange_copies(place, mine_in, mine_out, refs[0], refs[1])
            refs = refs[2:]
            continue
        lines = by_core(place, order)
        used = n * (2 + len(lines[0][0])) + 4 + len(lines[0][0])
        for line, only in lines:
            more, done, finish = scatter_events(place, line, only, mine_in, mine_out, refs[:used])
            starts += [(i / len(more), len(starts) + i, entry) for i, entry in enumerate(more)]
            steps += [(i / len(done), len(steps) + i, todo) for i, todo in enumerate(done)]
            ends += finish
        refs = refs[used:]
    for copy in swaps:
        copy.start()
    for _, _, (on, start) in sorted(starts, key=lambda entry: entry[:2]):
        guarded(on, start)
    for _, _, todo in sorted(steps, key=lambda entry: entry[:2]):
        for on, act in todo:
            guarded(on, act)
    for on, finish in ends:
        guarded(on, finish)
    for copy in swaps:
        copy.wait()


def landings(spread):
    if len(spread) == 2:
        return [(0, 1)]
    return [(shift, way) for shift in spread for way in (-1, 1) if shift - way in spread and shift * way <= 0]


def scatter_add(ep_count, tp_count, collective_id, name, groups):
    place = Place(ep_count, tp_count)
    arrays, shapes, scratch, specs = [], [], [], []
    dma = pltpu.SemaphoreType.DMA
    for order, partials in groups:
        arrays += partials
        count = len(partials)
        if order == "t":
            shapes += [jax.ShapeDtypeStruct(p.shape, p.dtype) for p in partials]
            specs += [pl.BlockSpec(memory_space=pl.ANY)] * count
            scratch += [dma((count, tp_count - 1))] * 2
            continue
        shapes += [jax.ShapeDtypeStruct(p.shape[1:], jnp.float32) for p in partials]
        specs += [pl.BlockSpec(memory_space=pltpu.VMEM)] * count
        scratch += scatter_scratch(place, order, partials)
    return pl.pallas_call(
        functools.partial(
            scatter_kernel, ep_count, tp_count, tuple((order, len(partials)) for order, partials in groups)
        ),
        out_shape=tuple(shapes),
        in_specs=[pl.BlockSpec(memory_space=pl.ANY)] * len(arrays),
        out_specs=tuple(specs),
        scratch_shapes=scratch,
        compiler_params=pltpu.CompilerParams(
            collective_id=collective_id, has_side_effects=True, vmem_limit_bytes=VMEM_MOST
        ),
        name=name,
    )(*arrays)


def scatter_room(place, order, partials):
    slots, lands, _ = scatter_sizes(place, order)
    rows = [(p.shape[1] + 15) // 16 * 16 for p in partials]
    sizes = [r * p.shape[2] * p.dtype.itemsize for r, p in zip(rows, partials)]
    return (2 * slots + sum(lands)) * sum(sizes)


def scatter_all(ep_count, tp_count, collective_ids, name, groups):
    place = Place(ep_count, tp_count)
    calls, room = [[]], 0
    for order, partials in groups:
        need = 0 if order == "t" else scatter_room(place, order, partials)
        if calls[-1] and room + need > VMEM_MOST * 19 // 20:
            calls.append([])
            room = 0
        calls[-1].append((order, partials))
        room += need
    found = []
    for i, call in enumerate(calls):
        found += scatter_add(ep_count, tp_count, collective_ids[i], "%s_%d" % (name, i), call)
    return found

OVER_LAST = (((1,), (1,)), ((), ()))
OVER_FIRST = (((0,), (0,)), ((), ()))
STRAIGHT = (((1,), (0,)), ((), ()))


def mul(left, right, dims=STRAIGHT):
    return lax.dot_general(left, right, dims, preferred_element_type=jnp.float32)


def rope_rows(length):
    places = np.arange(length, dtype=np.float32)
    frequencies = ROPE_BASE ** (-np.arange(HDIM // 2, dtype=np.float32) * np.float32(2.0 / HDIM))
    angles = places[:, None] * frequencies.astype(np.float32)[None, :]
    cosine, sine = np.cos(angles), np.sin(angles)
    return (
        np.concatenate([cosine, cosine], axis=1).astype(np.float32),
        np.concatenate([-sine, sine], axis=1).astype(np.float32),
    )


def unit_of(values):
    factor = lax.rsqrt(jnp.mean(values * values, axis=-1, keepdims=True) + NORM_EPS)
    return values * factor, factor


def masked_probs(queries, keys, allowed):
    raw = mul(queries, keys, OVER_LAST) * HDIM ** (-0.5)
    scores = jnp.where(allowed, raw, NEG_BIG)
    weights = jnp.exp(scores - jnp.max(scores, axis=-1, keepdims=True))
    return weights * (1.0 / jnp.sum(weights, axis=-1, keepdims=True))


def allowed_pairs(seg_row, seg_column):
    length = seg_row.shape[1]
    later = lax.broadcasted_iota(jnp.int32, (length, length), 0)
    earlier = lax.broadcasted_iota(jnp.int32, (length, length), 1)
    return (later >= earlier) & (seg_column[:, 0:1] == seg_row[0:1, :])


def forward_kernel(tokens, seg_row, seg_column, gains, cosine, sine, wq, wk, wv, wo,
                   qkv_out, attended, hidden, normed_two, normed):
    pair = pl.program_id(0)
    width = tokens.shape[1]
    wide = 2 * HDIM

    @pl.when(pair == 0)
    def _():
        values = tokens[...].astype(jnp.float32)
        normed[...] = (unit_of(values)[0] * gains[0:1, :]).astype(jnp.bfloat16)
        hidden[...] = values

    allowed = allowed_pairs(seg_row, seg_column)
    window = pl.ds(pl.multiple_of(pair * wide, wide), wide)
    made = []
    for part, weight in enumerate((wq, wk, wv)):
        projected = mul(normed[...], weight[...])
        heads = []
        for j in range(2):
            head = projected[:, j * HDIM : (j + 1) * HDIM]
            if part < 2:
                head = head * cosine[...] + pltpu.roll(head, HDIM // 2, 1) * sine[...]
            heads.append(head.astype(jnp.bfloat16))
            qkv_out[:, pl.ds(pl.multiple_of(part * width + pair * wide + j * HDIM, HDIM), HDIM)] = heads[j]
        made.append(heads)
    for j in range(2):
        probs = masked_probs(made[0][j], made[1][j], allowed).astype(jnp.bfloat16)
        attended[:, pl.ds(pl.multiple_of(pair * wide + j * HDIM, HDIM), HDIM)] = mul(
            probs, made[2][j]
        ).astype(jnp.bfloat16)
    hidden[...] += mul(attended[:, window], wo[...])

    @pl.when(pair == pl.num_programs(0) - 1)
    def _():
        normed_two[...] = (unit_of(hidden[...])[0] * gains[1:2, :]).astype(jnp.bfloat16)


def attention_forward(tokens, segments, gains, qkv_low, out_low):
    length, width = tokens.shape
    wide, pairs = 2 * HDIM, HEADS // 2
    cosine, sine = rope_rows(length)
    seg_row = jnp.broadcast_to(segments, (8, length))
    seg_column = jnp.broadcast_to(segments.T, (length, 128))
    low = jnp.bfloat16

    def whole(*shape):
        return pl.BlockSpec(shape, lambda i: (0,) * len(shape))

    def columns(part):
        return pl.BlockSpec((width, wide), lambda i: (0, part * pairs + i))

    return pl.pallas_call(
        forward_kernel,
        grid=(pairs,),
        in_specs=[
            whole(length, width), whole(8, length), whole(length, 128), whole(8, width),
            whole(length, HDIM), whole(length, HDIM), columns(0), columns(1), columns(2),
            pl.BlockSpec((wide, width), lambda i: (i, 0)),
        ],
        out_specs=[whole(length, 3 * width), whole(length, width), whole(length, width), whole(length, width)],
        out_shape=[
            jax.ShapeDtypeStruct((length, 3 * width), low),
            jax.ShapeDtypeStruct((length, width), low),
            jax.ShapeDtypeStruct((length, width), jnp.float32),
            jax.ShapeDtypeStruct((length, width), low),
        ],
        scratch_shapes=[pltpu.VMEM((length, width), low)],
        compiler_params=pltpu.CompilerParams(
            dimension_semantics=("arbitrary",), vmem_limit_bytes=VMEM_MOST
        ),
        name="attention_forward",
    )(tokens, seg_row, seg_column, gains, jnp.asarray(cosine), jnp.asarray(sine), qkv_low, qkv_low, qkv_low, out_low)


def spread_matrix(units, padded, group, step):
    unit = lax.broadcasted_iota(jnp.int32, (units, padded), 0)
    spot = lax.broadcasted_iota(jnp.int32, (units, padded), 1)
    within = jnp.bitwise_and(spot, step - 1)
    source = (spot - within) // step * group + within
    return jnp.where((unit == source) & (within < group), 1.0, 0.0).astype(jnp.bfloat16)


def backward_kernel(group, step, carried, *refs):
    (tokens, cot, seg_row, seg_column, gains, cosine, sine, qkv_act, attended, hidden, normed_two,
     routed_grad, wq, wk, wv, wo, shin, shout) = refs[:18]
    refs = refs[18:]
    if carried:
        ep_count, tp_count, order = carried
        result_part, sent_grads, refs = refs[0], refs[1], refs[2:]
    base, tokens_grad, gain_grads, qkv_grad, out_grad, shin_grad, shout_grad = refs[:7]
    refs = refs[7:]
    if carried:
        routed, grads_back, refs = refs[0], refs[1], refs[2:]
    (normed, normed_turned, branch, grad_one, pieces, stage, stage_sem) = refs[:7]
    refs = refs[7:]
    at = pl.program_id(0)
    width = tokens.shape[1]
    wide = 2 * HDIM
    low = jnp.bfloat16
    units = shin.shape[1] // 2

    if carried:
        place = Place(ep_count, tp_count)
        starts, lines, ends = scatter_events(place, order, None, [result_part], [routed], refs[:-2])
        swaps = exchange_copies(place, [sent_grads], [grads_back], refs[-2], refs[-1])
        first = sum(1 for block in scatter_order(place.dims(order)) if block[-1])
        turns = {0: lines[:first], 2: lines[first : first + 2], 4: lines[first + 2 : first + 4]}
        turns[5] = lines[first + 4 :]

    def run(entries):
        for on, act in entries:
            guarded(on, act)

    def carry(turn):
        if carried:
            for todo in turns.get(turn, []):
                run(todo)

    def stage_copy(part, pair):
        return pltpu.make_async_copy(
            stage.at[part],
            qkv_grad.at[:, pl.ds(pl.multiple_of(part * width + pair * wide, wide), wide)],
            stage_sem.at[part],
        )

    @pl.when(at == 0)
    def _():
        if carried:
            greet(place, "tab")
            for copy in swaps:
                copy.start()
            run(starts)
        unit_one = unit_of(tokens[...].astype(jnp.float32))[0]
        first = unit_one * gains[0:1, :]
        normed[...] = first.astype(low)
        normed_turned[...] = first.T.astype(low)
        pre_gate = mul(normed_two[...], shin[:, :units])
        pre_up = mul(normed_two[...], shin[:, units:])
        sigmoid = jax.nn.sigmoid(pre_gate)
        act = (pre_gate * sigmoid * pre_up).astype(low)
        spread = spread_matrix(units, shout.shape[0], group, step)
        act_spread = mul(act, spread).astype(low)
        base[...] = hidden[...] + mul(act_spread, shout[...])
        shout_grad[...] = mul(act_spread, cot[...], OVER_FIRST).astype(low)
        carry(0)
        shout_tight = mul(spread, shout[...]).astype(low)
        grad_act = mul(cot[...], shout_tight, OVER_LAST)
        grad_up = (grad_act * pre_gate * sigmoid).astype(low)
        grad_gate = (grad_act * pre_up * sigmoid * (1.0 + pre_gate * (1.0 - sigmoid))).astype(low)
        shin_grad[:, :units] = mul(normed_two[...], grad_gate, OVER_FIRST).astype(low)
        shin_grad[:, units:] = mul(normed_two[...], grad_up, OVER_FIRST).astype(low)
        grad_two = (
            routed_grad[...]
            + mul(grad_gate, shin[:, :units], OVER_LAST)
            + mul(grad_up, shin[:, units:], OVER_LAST)
        )
        unit_two, factor_two = unit_of(hidden[...])
        gain_grads[...] = jnp.zeros_like(gain_grads)
        gain_grads[1:2, :] = jnp.sum(grad_two * unit_two, axis=0, keepdims=True)
        grad_unit = grad_two * gains[1:2, :]
        back = factor_two * (
            grad_unit - unit_two * jnp.mean(grad_unit * unit_two, axis=-1, keepdims=True)
        )
        tokens_grad[...] = cot[...].astype(jnp.float32) + back
        branch[...] = tokens_grad[...].astype(low)
        grad_one[...] = jnp.zeros_like(grad_one)

    @pl.when(at > 0)
    def _():
        pair = at - 1
        allowed = allowed_pairs(seg_row, seg_column)
        window = pl.ds(pl.multiple_of(pair * wide, wide), wide)
        out_grad[...] = mul(attended[:, window], branch[...], OVER_FIRST).astype(low)
        grad_att = mul(branch[...], wo[...], OVER_LAST).astype(low)
        for j in range(2):

            def head(part):
                start = pl.multiple_of(part * width + pair * wide + j * HDIM, HDIM)
                return qkv_act[:, pl.ds(start, HDIM)]

            queries, keys, values = head(0), head(1), head(2)
            own = slice(j * HDIM, (j + 1) * HDIM)
            grad_own = grad_att[:, own]
            probs = masked_probs(queries, keys, allowed)
            grad_probs = mul(grad_own, values, OVER_LAST)
            grad_values = mul(probs.astype(low), grad_own, OVER_FIRST)
            row_dot = jnp.sum(probs * grad_probs, axis=-1, keepdims=True)
            grad_scores = (probs * (grad_probs - row_dot)).astype(low)
            grad_queries = mul(grad_scores, keys) * HDIM ** (-0.5)
            grad_keys = mul(grad_scores, queries, OVER_FIRST) * HDIM ** (-0.5)
            for part, grad in ((0, grad_queries), (1, grad_keys), (2, grad_values)):
                if part < 2:
                    grad = grad * cosine[...] - pltpu.roll(grad, HDIM // 2, 1) * sine[...]
                pieces[part, :, own] = grad.astype(low)
        for part, weight in enumerate((wq, wk, wv)):

            @pl.when(pair > 0)
            def _(part=part):
                stage_copy(part, pair - 1).wait()

            stage[part] = mul(normed_turned[...], pieces[part]).astype(low)
            stage_copy(part, pair).start()
            grad_one[...] += mul(pieces[part], weight[...], OVER_LAST)

        for turn in (2, 4):
            pl.when(at == turn)(functools.partial(carry, turn))

        @pl.when(at == pl.num_programs(0) - 1)
        def _():
            unit_one, factor_one = unit_of(tokens[...].astype(jnp.float32))
            total = grad_one[...]
            gain_grads[0:1, :] = jnp.sum(total * unit_one, axis=0, keepdims=True)
            grad_unit = total * gains[0:1, :]
            back = factor_one * (
                grad_unit - unit_one * jnp.mean(grad_unit * unit_one, axis=-1, keepdims=True)
            )
            tokens_grad[...] += back
            for part in range(3):
                stage_copy(part, pair).wait()
            carry(5)
            if carried:
                run(ends)
                for copy in swaps:
                    copy.wait()


def dense_backward(group, step, tokens, cot, segments, gains, qkv_act, attended, hidden, normed_two,
                   routed_grad, qkv_low, out_low, shin_low, shout_spread, ep_count, tp_count,
                   collective_id, order, result_part, sent_grads):
    length, width = tokens.shape
    wide, pairs = 2 * HDIM, HEADS // 2
    cosine, sine = rope_rows(length)
    seg_row = jnp.broadcast_to(segments, (8, length))
    seg_column = jnp.broadcast_to(segments.T, (length, 128))
    low = jnp.bfloat16
    once = pl.Buffered(1)

    def whole(*shape):
        return pl.BlockSpec(shape, lambda i: (0,) * len(shape), pipeline_mode=once)

    def columns(part):
        return pl.BlockSpec((width, wide), lambda i: (0, part * pairs + jnp.maximum(i - 1, 0)))

    rows = pl.BlockSpec((wide, width), lambda i: (jnp.maximum(i - 1, 0), 0))
    in_specs = [
        whole(length, width), whole(length, width), whole(8, length), whole(length, 128),
        whole(8, width), whole(length, HDIM), whole(length, HDIM), whole(length, 3 * width),
        whole(length, width), whole(length, width), whole(length, width), whole(length, width),
        columns(0), columns(1), columns(2), rows,
        whole(*shin_low.shape), whole(*shout_spread.shape),
    ]
    anywhere = pl.BlockSpec(memory_space=pl.ANY)
    out_specs = [
        whole(length, width), whole(length, width), whole(8, width),
        anywhere, rows, whole(*shin_low.shape), whole(*shout_spread.shape),
    ]
    out_shape = [
        jax.ShapeDtypeStruct((length, width), jnp.float32),
        jax.ShapeDtypeStruct((length, width), jnp.float32),
        jax.ShapeDtypeStruct((8, width), jnp.float32),
        jax.ShapeDtypeStruct((width, 3 * width), low),
        jax.ShapeDtypeStruct((width, width), low),
        jax.ShapeDtypeStruct(shin_low.shape, low),
        jax.ShapeDtypeStruct(shout_spread.shape, low),
    ]
    scratch = [
        pltpu.VMEM((length, width), low), pltpu.VMEM((width, length), low),
        pltpu.VMEM((length, width), low), pltpu.VMEM((length, width), jnp.float32),
        pltpu.VMEM((3, length, wide), low),
        pltpu.VMEM((3, width, wide), low), pltpu.SemaphoreType.DMA((3,)),
    ]
    arguments = [tokens, cot, seg_row, seg_column, gains, jnp.asarray(cosine), jnp.asarray(sine), qkv_act,
                 attended, hidden, normed_two, routed_grad, qkv_low, qkv_low, qkv_low, out_low, shin_low,
                 shout_spread]
    carried, more = None, {}
    if result_part is not None:
        carried, more = (ep_count, tp_count, order), dict(collective_id=collective_id, has_side_effects=True)
        arguments += [result_part, sent_grads]
        in_specs += [anywhere, anywhere]
        out_specs += [whole(length, width), anywhere]
        out_shape += [
            jax.ShapeDtypeStruct((length, width), jnp.float32),
            jax.ShapeDtypeStruct(sent_grads.shape, sent_grads.dtype),
        ]
        scratch += scatter_scratch(Place(ep_count, tp_count), order, [result_part])
        scratch += [pltpu.SemaphoreType.DMA((1, tp_count - 1))] * 2
    return pl.pallas_call(
        functools.partial(backward_kernel, group, step, carried),
        grid=(pairs + 1,),
        in_specs=in_specs,
        out_specs=out_specs,
        out_shape=out_shape,
        scratch_shapes=scratch,
        compiler_params=pltpu.CompilerParams(
            dimension_semantics=("arbitrary",), vmem_limit_bytes=VMEM_MOST, **more
        ),
        name="dense_backward",
    )(*arguments)


def expert_kernel(parts, per_step, cap, *refs):
    normed, cot, info = refs[:3]
    ins, outs_w = refs[3 : 3 + parts], refs[3 + parts : 3 + 2 * parts]
    result_ref, input_ref, own_grad = refs[3 + 2 * parts : 6 + 2 * parts]
    sent = refs[6 + 2 * parts : 5 + 3 * parts]
    scratch = refs[5 + 3 * parts :]
    rows_x, rows_g, gate_col, result_acc, input_acc = scratch[:5]
    sums = (own_grad,) + tuple(scratch[5:])
    step = pl.program_id(0)
    tok = normed.shape[1]
    width = normed.shape[2]
    chunk = 256

    @pl.when(step == 0)
    def _():
        for total in sums:
            total[...] = jnp.zeros_like(total)

    slots = lax.broadcasted_iota(jnp.int32, (cap, tok), 0).astype(jnp.float32)
    for s in range(per_step):
        hit = slots == info[s, 0:1, :]
        picks = jnp.where(hit, 1.0, 0.0).astype(jnp.bfloat16)
        gates = jnp.sum(jnp.where(hit, info[s, 1:2, :], 0.0), axis=1, keepdims=True)
        window = pl.ds(s * cap, cap)
        gate_col[window, :] = jnp.broadcast_to(gates, (cap, 128))
        rows_x[window, :] = jnp.dot(picks, normed[s], preferred_element_type=jnp.float32).astype(
            jnp.bfloat16
        )
        taken = jnp.dot(picks, cot[s], preferred_element_type=jnp.float32)
        rows_g[window, :] = (gates * taken).astype(jnp.bfloat16)
    across = (((1,), (1,)), ((), ()))
    down = (((0,), (0,)), ((), ()))

    def mul(left, right, dims):
        return lax.dot_general(left, right, dims, preferred_element_type=jnp.float32)

    straight = (((1,), (0,)), ((), ()))
    for p in range(parts):
        gate_pre = mul(rows_x[...], ins[p][0], across)
        up_pre = mul(rows_x[...], ins[p][1], across)
        sigmoid = jax.nn.sigmoid(gate_pre)
        active = (gate_pre * sigmoid * up_pre).astype(jnp.bfloat16)
        grad_act = mul(rows_g[...], outs_w[p][...], across)
        grad_up = (grad_act * gate_pre * sigmoid).astype(jnp.bfloat16)
        grad_gate = (grad_act * up_pre * sigmoid * (1.0 + gate_pre * (1.0 - sigmoid))).astype(
            jnp.bfloat16
        )
        for first in range(0, width, chunk):
            window = slice(first, first + chunk)
            result = mul(active, outs_w[p][:, window], straight)
            back = mul(grad_gate, ins[p][0, :, window], straight) + mul(
                grad_up, ins[p][1, :, window], straight
            )
            if p == 0:
                result_acc[:, window] = result
                input_acc[:, window] = back
            else:
                result_acc[:, window] += result
                input_acc[:, window] += back
            sums[p][0, :, window] += mul(grad_gate, rows_x[:, window], down)
            sums[p][1, :, window] += mul(grad_up, rows_x[:, window], down)
            sums[p][2, :, window] += mul(active, rows_g[:, window], down)
    for s in range(per_step):
        hit = slots == info[s, 0:1, :]
        picks = jnp.where(hit, 1.0, 0.0).astype(jnp.bfloat16)
        window = pl.ds(s * cap, cap)
        rounded = result_acc[window, :].astype(jnp.bfloat16).astype(jnp.float32)
        weighted = (gate_col[window, 0:1] * rounded).astype(jnp.bfloat16)
        result_ref[s] = mul(picks, weighted, down).astype(jnp.bfloat16)
        input_ref[s] = mul(picks, input_acc[window, :].astype(jnp.bfloat16), down).astype(
            jnp.bfloat16
        )

    @pl.when(step == pl.num_programs(0) - 1)
    def _():
        for p in range(1, parts):
            sent[p - 1][...] = sums[p][...].astype(jnp.bfloat16)


def expert_pass(normed_all, cot_all, info, ins, outs_w, cap):
    ep_count, tok, width = normed_all.shape
    parts = len(ins)
    hidden = ins[0].shape[1]
    per_step = max(1, min(ep_count, 256 // cap))
    rows = per_step * cap
    token_spec = pl.BlockSpec((per_step, tok, width), lambda i: (i, 0, 0))
    once = pl.Buffered(1)
    in_specs = [token_spec, token_spec, pl.BlockSpec((per_step, 2, tok), lambda i: (i, 0, 0))]
    in_specs += [
        pl.BlockSpec((2, hidden, width), lambda i: (0, 0, 0), pipeline_mode=once)
    ] * parts
    in_specs += [pl.BlockSpec((hidden, width), lambda i: (0, 0), pipeline_mode=once)] * parts
    grad_spec = pl.BlockSpec((3, hidden, width), lambda i: (0, 0, 0), pipeline_mode=once)
    token_shape = jax.ShapeDtypeStruct((ep_count, tok, width), jnp.bfloat16)
    out_shape = [token_shape, token_shape, jax.ShapeDtypeStruct((3, hidden, width), jnp.float32)]
    out_shape += [jax.ShapeDtypeStruct((3, hidden, width), jnp.bfloat16)] * (parts - 1)
    scratch = [
        pltpu.VMEM((rows, width), jnp.bfloat16),
        pltpu.VMEM((rows, width), jnp.bfloat16),
        pltpu.VMEM((rows, 128), jnp.float32),
        pltpu.VMEM((rows, width), jnp.float32),
        pltpu.VMEM((rows, width), jnp.float32),
    ] + [pltpu.VMEM((3, hidden, width), jnp.float32)] * (parts - 1)
    found = pl.pallas_call(
        functools.partial(expert_kernel, parts, per_step, cap),
        grid=(ep_count // per_step,),
        in_specs=in_specs,
        out_specs=[token_spec, token_spec] + [grad_spec] * parts,
        out_shape=out_shape,
        scratch_shapes=scratch,
        compiler_params=pltpu.CompilerParams(
            dimension_semantics=("arbitrary",), vmem_limit_bytes=VMEM_MOST
        ),
        cost_estimate=pl.CostEstimate(
            flops=18 * ep_count * cap * parts * hidden * width,
            bytes_accessed=8 * ep_count * tok * width + 30 * parts * hidden * width,
            transcendentals=ep_count * cap * parts * hidden,
        ),
        name="expert_pass",
    )(normed_all, cot_all, info, *ins, *outs_w)
    return found[0], found[1], found[2], found[3:]


def nearest(place):
    count = place.na
    table = [sorted(range(count), key=lambda other: abs(other - own)) for own in range(count)]

    def chip_at(r):
        found = jnp.int32(0)
        for own in range(count):
            for rank in range(count):
                found = found + jnp.where((place.a == own) & (r == rank), table[own][rank], 0)
        return found

    return chip_at


def fused_kernel(parts, ep_count, tp_count, cap, *refs):
    normed, info, cot = refs[:3]
    w_in, w_out = refs[3 : 3 + parts], refs[3 + parts : 3 + 2 * parts]
    refs = refs[3 + 2 * parts :]
    result_ref, routed_ref, own_grad = refs[:3]
    sent = refs[3 : 2 + parts]
    scratch = refs[2 + parts :]
    tok, infos, cots, vin, vout, own, sib, sib_stage, bland, aland, res_stage = scratch[:11]
    rows_x, rows_g, gate_col, result_acc, input_acc, stage = scratch[11:17]
    sums = (own_grad,) + tuple(scratch[17 : 16 + parts])
    (tok_recv, tok_send, local_sem, cot_sem, sib_recv, sib_send, b_recv, b_send, a_recv, a_send,
     res_sem, stage_sem) = scratch[16 + parts :]
    place = Place(ep_count, tp_count)
    na, a, b, core = place.na, place.a, place.b, place.core
    width = normed.shape[1]
    me = (a * 2 + b) * 2 + core
    chip_at = nearest(place)
    chunk = 256

    def device(a_, b_, core_):
        return ((a_ * 2 + b_) * 2 + core_, place.t)

    sibling, across = device(a, b, 1 - core), device(a, 1 - b, core)
    barrier = pltpu.get_barrier_semaphore()
    for target in (sibling, across):
        pl.semaphore_signal(barrier, inc=1, device_id=target, device_id_type=MESH)
    for step in range(1, na):
        pl.semaphore_signal(
            barrier, inc=1, device_id=device(lax.rem(a + step, na), b, core), device_id_type=MESH
        )
    pl.semaphore_wait(barrier, na + 1)

    def hop(index, number, target, first=False):
        return [
            pltpu.make_async_remote_copy(
                src_ref=own_block if first else held.at[index],
                dst_ref=held.at[index],
                send_sem=tok_send.at[k, number],
                recv_sem=tok_recv.at[k, index],
                device_id=target,
                device_id_type=MESH,
            )
            for k, (own_block, held) in enumerate(((normed, tok), (info, infos)))
        ]

    def start(copies):
        for copy in copies:
            copy.start()

    def arrived(index):
        for k, held in enumerate((tok, infos)):
            pltpu.make_async_copy(held.at[index], held.at[index], tok_recv.at[k, index]).wait()

    ends = []

    def launch(on, copies):
        def finish():
            for copy in copies:
                copy.wait_send()

        guarded(on, lambda: start(copies))
        ends.append((on, finish))

    up, down_ok = a + 1 < na, a > 0
    launch(up, hop(me, 0, device(a + 1, b, core), True))
    launch(down_ok, hop(me, 1, device(a - 1, b, core), True))
    launch(None, hop(me, 2, across, True))
    launch(None, hop(me, 3, sibling, True))
    loads = [pltpu.make_async_copy(normed, tok.at[me], local_sem.at[0])]
    loads.append(pltpu.make_async_copy(info, infos.at[me], local_sem.at[1]))
    for p in range(parts):
        loads.append(pltpu.make_async_copy(w_in[p], vin.at[p], local_sem.at[2 + 2 * p]))
        loads.append(pltpu.make_async_copy(w_out[p], vout.at[p], local_sem.at[3 + 2 * p]))
    start(loads)

    def chip_of(k):
        side = lax.rem(k, 2)
        return chip_at(k // 2) * 2 + jnp.where(side == 0, b, 1 - b)

    def cot_copies(k):
        chip, buffer = chip_of(k), lax.rem(k, 2)
        return [
            pltpu.make_async_copy(cot.at[chip * 2 + j], cots.at[buffer, j], cot_sem.at[buffer, j])
            for j in range(2)
        ]

    start(cot_copies(jnp.int32(0)))
    for total in sums:
        total[...] = jnp.zeros_like(total)
    for load in loads:
        load.wait()

    def from_a(r):
        other = chip_at(r)
        index = (other * 2 + b) * 2 + core
        arrived(index)
        first = 4 + 3 * (r - 1)
        beyond = jnp.where(other > a, a - 1, a + 1)
        on = (beyond >= 0) & (beyond < na)
        copies = hop(index, first, device(beyond, b, core))
        pl.when(on)(lambda: start(copies))
        start(hop(index, first + 1, across))
        start(hop(index, first + 2, sibling))

    def from_b(r):
        index = (chip_at(r) * 2 + 1 - b) * 2 + core
        arrived(index)
        start(hop(index, 4 + 3 * (na - 1) + r, sibling))

    def sent_from_a(r):
        other = chip_at(r)
        index = (other * 2 + b) * 2 + core
        first = 4 + 3 * (r - 1)
        beyond = jnp.where(other > a, a - 1, a + 1)
        on = (beyond >= 0) & (beyond < na)

        def finish(number):
            for copy in hop(index, number, sibling):
                copy.wait_send()

        pl.when(on)(lambda: finish(first))
        finish(first + 1)
        finish(first + 2)

    def sib_wait(chip):
        pltpu.make_async_copy(sib.at[chip], sib.at[chip], sib_recv.at[chip]).wait()

    def to_b(r):
        chip = chip_at(r) * 2 + 1 - b
        sib_wait(chip)
        add_into(own.at[chip], [own.at[chip], sib.at[chip]], own.dtype)
        pltpu.make_async_remote_copy(
            src_ref=own.at[chip],
            dst_ref=bland.at[r],
            send_sem=b_send.at[r],
            recv_sem=b_recv.at[r],
            device_id=across,
            device_id_type=MESH,
        ).start()

    def b_wait(r):
        pltpu.make_async_copy(bland.at[r], bland.at[r], b_recv.at[r]).wait()

    def to_a(r):
        other = chip_at(r)
        chip = other * 2 + b
        sib_wait(chip)
        b_wait(r)
        add_into(own.at[chip], [own.at[chip], sib.at[chip], bland.at[r]], own.dtype)
        pltpu.make_async_remote_copy(
            src_ref=own.at[chip],
            dst_ref=aland.at[a],
            send_sem=a_send.at[r],
            recv_sem=a_recv.at[a],
            device_id=device(other, b, core),
            device_id_type=MESH,
        ).start()

    over_last = (((1,), (1,)), ((), ()))
    over_first = (((0,), (0,)), ((), ()))
    straight = (((1,), (0,)), ((), ()))

    def mul(left, right, dims):
        return lax.dot_general(left, right, dims, preferred_element_type=jnp.float32)

    slots = lax.broadcasted_iota(jnp.int32, (cap, normed.shape[0]), 0).astype(jnp.float32)

    def picks_of(source):
        return slots == infos[source, pl.ds(me, 1), :]

    def work(k, carry):
        chip, buffer = chip_of(k), lax.rem(k, 2)

        @pl.when(k + 1 < 2 * na)
        def _():
            start(cot_copies(k + 1))

        for r in range(na):
            if r == 1:
                pl.when(k == 1)(functools.partial(from_a, r))
            pl.when(k == 2 * r + 1)(functools.partial(from_b, r))
        pl.when(k == 2 * na - 2)(functools.partial(to_b, 1))
        arrived(chip * 2 + 1 - core)
        for copy in cot_copies(k):
            copy.wait()
        for j in range(2):
            hit = picks_of(chip * 2 + j)
            picks = jnp.where(hit, 1.0, 0.0).astype(jnp.bfloat16)
            gate_row = infos[chip * 2 + j, pl.ds(ep_count + me, 1), :]
            gates = jnp.sum(jnp.where(hit, gate_row, 0.0), axis=1, keepdims=True)
            window = pl.ds(j * cap, cap)
            gate_col[window, :] = jnp.broadcast_to(gates, (cap, 128))
            rows_x[window, :] = mul(picks, tok[chip * 2 + j], straight).astype(jnp.bfloat16)
            taken = mul(picks, cots[buffer, j], straight)
            rows_g[window, :] = (gates * taken).astype(jnp.bfloat16)
        for p in range(parts):
            gate_pre = mul(rows_x[...], vin[p, 0], over_last)
            up_pre = mul(rows_x[...], vin[p, 1], over_last)
            sigmoid = jax.nn.sigmoid(gate_pre)
            active = (gate_pre * sigmoid * up_pre).astype(jnp.bfloat16)
            grad_act = mul(rows_g[...], vout[p], over_last)
            grad_up = (grad_act * gate_pre * sigmoid).astype(jnp.bfloat16)
            grad_gate = (
                grad_act * up_pre * sigmoid * (1.0 + gate_pre * (1.0 - sigmoid))
            ).astype(jnp.bfloat16)
            for first in range(0, width, chunk):
                window = slice(first, first + chunk)
                result = mul(active, vout[p, :, window], straight)
                back = mul(grad_gate, vin[p, 0, :, window], straight) + mul(
                    grad_up, vin[p, 1, :, window], straight
                )
                if p == 0:
                    result_acc[:, window] = result
                    input_acc[:, window] = back
                else:
                    result_acc[:, window] += result
                    input_acc[:, window] += back
                sums[p][0, :, window] += mul(grad_gate, rows_x[:, window], over_first)
                sums[p][1, :, window] += mul(grad_up, rows_x[:, window], over_first)
                sums[p][2, :, window] += mul(active, rows_g[:, window], over_first)
            if p == 0:
                for r in range(2, na):
                    pl.when(k == 2 * r - 2)(functools.partial(from_a, r))
                    if r < na - 1:
                        pl.when(k == 2 * na - 2)(functools.partial(to_b, r))

        @pl.when(k > 0)
        def _():
            pltpu.make_async_copy(sib_stage, sib_stage, sib_send.at[0]).wait()
            for j in range(2):
                pltpu.make_async_copy(res_stage.at[j], res_stage.at[j], res_sem.at[j]).wait()

        for other in range(2):
            j = 1 - core if other == 0 else core
            source = chip * 2 + j
            picks = jnp.where(picks_of(source), 1.0, 0.0).astype(jnp.bfloat16)
            window = pl.ds(pl.multiple_of(j * cap, cap), cap)
            back = mul(picks, input_acc[window, :].astype(jnp.bfloat16), over_first)
            if other == 0:
                sib_stage[...] = back.astype(jnp.bfloat16)
                pltpu.make_async_remote_copy(
                    src_ref=sib_stage,
                    dst_ref=sib.at[chip],
                    send_sem=sib_send.at[0],
                    recv_sem=sib_recv.at[chip],
                    device_id=sibling,
                    device_id_type=MESH,
                ).start()
            else:
                own[chip] = back.astype(jnp.bfloat16)
            rounded = result_acc[window, :].astype(jnp.bfloat16).astype(jnp.float32)
            weighted = (gate_col[window, 0:1] * rounded).astype(jnp.bfloat16)
            res_stage[other] = mul(picks, weighted, over_first).astype(jnp.bfloat16)
            pltpu.make_async_copy(res_stage.at[other], result_ref.at[source], res_sem.at[other]).start()
        return carry

    lax.fori_loop(0, 2 * na, work, 0)
    to_b(na - 1)
    for p in range(1, parts):
        for q in range(3):
            if p > 1 or q > 0:
                pltpu.make_async_copy(stage, stage, stage_sem.at[0]).wait()
            stage[...] = sums[p][q].astype(jnp.bfloat16)
            pltpu.make_async_copy(stage, sent[p - 1].at[q], stage_sem.at[0]).start()
    for r in range(1, na):
        if r == na - 1:
            to_b(0)
        to_a(r)
    chip = a * 2 + b
    sib_wait(chip)
    b_wait(0)
    add_into(routed_ref, [own.at[chip], sib.at[chip], bland.at[0]], jnp.float32)
    for r in range(1, na):
        other = chip_at(r)
        pltpu.make_async_copy(aland.at[other], aland.at[other], a_recv.at[other]).wait()
        add_into(routed_ref, [routed_ref, aland.at[other]], jnp.float32)
    for on, finish in ends:
        guarded(on, finish)
    for r in range(na):
        if r:
            sent_from_a(r)
            pltpu.make_async_copy(own.at[0], own.at[0], a_send.at[r]).wait()
        for copy in hop(me, 4 + 3 * (na - 1) + r, sibling):
            copy.wait_send()
        pltpu.make_async_copy(own.at[0], own.at[0], b_send.at[r]).wait()
    pltpu.make_async_copy(sib_stage, sib_stage, sib_send.at[0]).wait()
    for j in range(2):
        pltpu.make_async_copy(res_stage.at[j], res_stage.at[j], res_sem.at[j]).wait()
    pltpu.make_async_copy(stage, stage, stage_sem.at[0]).wait()


def fused_experts(ep_count, tp_count, collective_id, normed, info, cot_all, ins, outs_w, cap):
    place = Place(ep_count, tp_count)
    tok, width = normed.shape
    parts = len(ins)
    hidden = ins[0].shape[1]
    na, chips, rows = place.na, 2 * place.na, 2 * cap
    low = jnp.bfloat16
    anywhere = pl.BlockSpec(memory_space=pl.ANY)
    inside = pl.BlockSpec(memory_space=pltpu.VMEM)
    out_shape = [
        jax.ShapeDtypeStruct((ep_count, tok, width), low),
        jax.ShapeDtypeStruct((tok, width), jnp.float32),
        jax.ShapeDtypeStruct((3, hidden, width), jnp.float32),
    ] + [jax.ShapeDtypeStruct((3, hidden, width), low)] * (parts - 1)
    scratch = [
        pltpu.VMEM((ep_count, tok, width), low),
        pltpu.VMEM((ep_count, 2 * ep_count, tok), jnp.float32),
        pltpu.VMEM((2, 2, tok, width), low),
        pltpu.VMEM((parts, 2, hidden, width), low),
        pltpu.VMEM((parts, hidden, width), low),
        pltpu.VMEM((chips, tok, width), low),
        pltpu.VMEM((chips, tok, width), low),
        pltpu.VMEM((tok, width), low),
        pltpu.VMEM((na, tok, width), low),
        pltpu.VMEM((na, tok, width), low),
        pltpu.VMEM((2, tok, width), low),
        pltpu.VMEM((rows, width), low),
        pltpu.VMEM((rows, width), low),
        pltpu.VMEM((rows, 128), jnp.float32),
        pltpu.VMEM((rows, width), jnp.float32),
        pltpu.VMEM((rows, width), jnp.float32),
        pltpu.VMEM((hidden, width), low),
    ] + [pltpu.VMEM((3, hidden, width), jnp.float32)] * (parts - 1)
    dma = pltpu.SemaphoreType.DMA
    scratch += [
        dma((2, ep_count)), dma((2, 4 + 3 * (na - 1) + na)), dma((2 + 2 * parts,)), dma((2, 2)),
        dma((chips,)), dma((1,)), dma((na,)), dma((na,)), dma((na,)), dma((na,)), dma((2,)), dma((1,)),
    ]
    found = pl.pallas_call(
        functools.partial(fused_kernel, parts, ep_count, tp_count, cap),
        in_specs=[anywhere] * (3 + 2 * parts),
        out_specs=[anywhere, inside, inside] + [anywhere] * (parts - 1),
        out_shape=out_shape,
        scratch_shapes=scratch,
        compiler_params=pltpu.CompilerParams(
            collective_id=collective_id, has_side_effects=True, vmem_limit_bytes=VMEM_MOST
        ),
        name="fused_experts",
    )(normed, info, cot_all, *ins, *outs_w)
    return found[0], found[1], found[2], found[3:]


def adam_update(weight, gradient, first, second, clip_scale, rate, decay):
    clipped = gradient * clip_scale
    first_new = BETA_ONE * first + (1.0 - BETA_ONE) * clipped
    second_new = BETA_TWO * second + (1.0 - BETA_TWO) * clipped * clipped
    corr_one = 1.0 - BETA_ONE**STEP
    corr_two = 1.0 - BETA_TWO**STEP
    stepped = first_new / corr_one / (jnp.sqrt(second_new / corr_two) + ADAM_EPS)
    weight_new = weight - rate * (stepped + decay * weight)
    return (weight_new, first_new, second_new, weight_new.astype(jnp.bfloat16))


def per_device(
    tokens,
    cotangent,
    segments,
    routes,
    gates,
    qkv_weight,
    qkv_first,
    qkv_second,
    out_weight,
    out_first,
    out_second,
    shared_in,
    shared_in_first,
    shared_in_second,
    shared_out,
    shared_out_first,
    shared_out_second,
    expert_in,
    expert_in_first,
    expert_in_second,
    expert_out,
    expert_out_first,
    expert_out_second,
    norm_gains,
    gains_first,
    gains_second,
):
    tok_count = tokens.shape[0]
    width = tokens.shape[1]
    ep_count = lax.axis_size("ep")
    tp_count = lax.axis_size("tp")
    devices = ep_count * tp_count
    capacity = tok_count * 8 // ep_count
    low = jnp.bfloat16
    in_own, out_own = expert_in[0].astype(low), expert_out[0].astype(low)
    gain_columns = jnp.pad(norm_gains.T.astype(low), ((0, 0), (0, 126)))
    group = shared_out.shape[0]
    step = 16 * ((group + 15) // 16)
    while step & (step - 1):
        step += 16
    shout_own = jnp.pad(shared_out.astype(low), ((0, step - group), (0, 0)))
    qkv_low, out_low, gains_low, cot_all, in_others, out_others, shin_low, shout_low = gather(
        ep_count,
        tp_count,
        1,
        "gather_weights",
        [
            (("tab", "abt"), [qkv_weight.astype(low), out_weight.astype(low), gain_columns]),
            (("ab", "ba"), [cotangent]),
            ("t", [in_own, out_own]),
            (("tab", "atb"), [shared_in.astype(low), shout_own]),
        ],
    )
    qkv_low = qkv_low.reshape(width, 3 * width)
    out_low = out_low.reshape(width, width)
    shin_low = shin_low.reshape(width, 2 * FF)
    shout_low = shout_low.reshape(devices * step, width)
    gains = jnp.pad(gains_low.reshape(width, 128)[:, :2].T.astype(jnp.float32), ((0, 6), (0, 0)))
    ins_low = [in_own] + [in_others[s] for s in range(tp_count - 1)]
    outs_low = [out_own] + [out_others[s] for s in range(tp_count - 1)]
    expert_ids = jnp.arange(ep_count, dtype=jnp.int32)
    chosen = routes[:, :, None] == expert_ids[None, None, :]
    onehot = jnp.sum(chosen.astype(jnp.float32), axis=1)
    gate_of = jnp.sum(jnp.where(chosen, gates[:, :, None], 0.0), axis=1)
    earlier = jnp.tril(jnp.ones((tok_count, tok_count), low), -1)
    rank = jnp.dot(earlier, onehot.astype(low), preferred_element_type=jnp.float32)
    slot_of = jnp.where(onehot > 0.0, rank, -1.0)
    info_own = jnp.concatenate([slot_of, gate_of], axis=1).T
    qkv_act, attended, hidden, normed_two = attention_forward(
        tokens, segments, gains, qkv_low, out_low
    )
    chips = ep_count // 2
    held = tok_count * width * 2 * (ep_count + 3 * chips + 12) + 9 * tp_count * expert_in.size
    if Place(ep_count, tp_count).nb == 2 and held <= VMEM_MOST * 9 // 10:
        result_part, routed_grad, own_grad, sent_grads = fused_experts(
            ep_count, tp_count, 3, normed_two, info_own, cot_all, ins_low, outs_low, capacity
        )
    else:
        normed_all, info_all = gather(
            ep_count, tp_count, 2, "gather_tokens", [("ab", [normed_two, info_own])]
        )
        info = lax.dynamic_index_in_dim(
            info_all.reshape(ep_count, 2, ep_count, tok_count),
            lax.axis_index("ep"),
            axis=2,
            keepdims=False,
        )
        result_part, input_part, own_grad, sent_grads = expert_pass(
            normed_all, cot_all, info, ins_low, outs_low, capacity
        )
        (routed_grad,) = scatter_add(ep_count, tp_count, 3, "scatter_inputs", [("ab", [input_part])])
    sent = jnp.stack(sent_grads)
    lean = scatter_room(Place(ep_count, tp_count), "ab", [result_part]) <= VMEM_MOST // 3
    base, tokens_grad, gain_grads, qkv_grad, out_grad, shin_grad, shout_grad, *carried = dense_backward(
        group, step, tokens, cotangent, segments, gains, qkv_act, attended, hidden, normed_two,
        routed_grad, qkv_low, out_low, shin_low, shout_low, ep_count, tp_count, 9, "ab",
        result_part if lean else None, sent,
    )
    gain_rows = jnp.pad(gain_grads[:2].T.astype(low), ((0, 0), (0, 126)))

    def by_owner(grad):
        return grad.reshape(devices, -1, grad.shape[1])

    scattered = [
        (("abt", "tab"), [by_owner(qkv_grad), by_owner(out_grad), by_owner(gain_rows)]),
        (("abt", "bta"), [by_owner(shin_grad), by_owner(shout_grad)]),
    ]
    if not lean:
        scattered += [("ab", [result_part]), ("t", [sent])]
    qkv_part, out_part, gains_part, shin_part, shout_part, *more = scatter_all(
        ep_count, tp_count, (4, 6, 7, 8), "scatter_weights", scattered
    )
    routed, others = carried or more
    for shift in range(tp_count - 1):
        own_grad = own_grad + others[shift].astype(jnp.float32)
    block_out = (base + routed).astype(low)
    exin_part, exout_part = own_grad[None, :2], own_grad[2:]
    extra = jnp.sum(own_grad * own_grad, axis=(0, 1))[None, :]
    grad_norm = jnp.sqrt(
        sum_of_squares(
            ep_count, tp_count, 5, [qkv_part, out_part, gains_part, shin_part, shout_part], extra
        )
    )
    shout_part = shout_part[:group]
    gains_part = gains_part[:, :2].T
    clip_scale = jnp.minimum(1.0, CLIP_LEVEL / (grad_norm + 1e-06))
    qkv_new, qkv_first_new, qkv_second_new, qkv_copy = adam_update(
        qkv_weight, qkv_part, qkv_first, qkv_second, clip_scale, MATRIX_RATE, WEIGHT_DECAY
    )
    out_new, out_first_new, out_second_new, out_copy = adam_update(
        out_weight, out_part, out_first, out_second, clip_scale, MATRIX_RATE, WEIGHT_DECAY
    )
    shin_new, shin_first_new, shin_second_new, shin_copy = adam_update(
        shared_in,
        shin_part,
        shared_in_first,
        shared_in_second,
        clip_scale,
        MATRIX_RATE,
        WEIGHT_DECAY,
    )
    shout_new, shout_first_new, shout_second_new, shout_copy = adam_update(
        shared_out,
        shout_part,
        shared_out_first,
        shared_out_second,
        clip_scale,
        MATRIX_RATE,
        WEIGHT_DECAY,
    )
    exin_new, exin_first_new, exin_second_new, exin_copy = adam_update(
        expert_in,
        exin_part,
        expert_in_first,
        expert_in_second,
        clip_scale,
        MATRIX_RATE,
        WEIGHT_DECAY,
    )
    exout_new, exout_first_new, exout_second_new, exout_copy = adam_update(
        expert_out,
        exout_part,
        expert_out_first,
        expert_out_second,
        clip_scale,
        MATRIX_RATE,
        WEIGHT_DECAY,
    )
    gains_new, gains_first_new, gains_second_new, gains_copy = adam_update(
        norm_gains, gains_part, gains_first, gains_second, clip_scale, GAIN_RATE, 0.0
    )
    return (
        block_out,
        tokens_grad,
        grad_norm,
        qkv_new,
        qkv_first_new,
        qkv_second_new,
        qkv_copy,
        out_new,
        out_first_new,
        out_second_new,
        out_copy,
        shin_new,
        shin_first_new,
        shin_second_new,
        shin_copy,
        shout_new,
        shout_first_new,
        shout_second_new,
        shout_copy,
        exin_new,
        exin_first_new,
        exin_second_new,
        exin_copy,
        exout_new,
        exout_first_new,
        exout_second_new,
        exout_copy,
        gains_new,
        gains_first_new,
        gains_second_new,
        gains_copy,
    )


def solution(mesh):
    placed = (
        P(("ep", "tp"), None),
        P(("ep", "tp"), None),
        P(("ep", "tp"), None),
        P(("ep", "tp"), None),
        P(("ep", "tp"), None),
        P(("ep", "tp"), None),
        P(("ep", "tp"), None),
        P(("ep", "tp"), None),
        P(("ep", "tp"), None),
        P(("ep", "tp"), None),
        P(("ep", "tp"), None),
        P(("ep", "tp"), None),
        P(("ep", "tp"), None),
        P(("ep", "tp"), None),
        P(("ep", "tp"), None),
        P(("ep", "tp"), None),
        P(("ep", "tp"), None),
        P("ep", None, "tp", None),
        P("ep", None, "tp", None),
        P("ep", None, "tp", None),
        P("ep", "tp", None),
        P("ep", "tp", None),
        P("ep", "tp", None),
        P(None, ("ep", "tp")),
        P(None, ("ep", "tp")),
        P(None, ("ep", "tp")),
    )
    return jax.shard_map(
        per_device,
        mesh=mesh,
        in_specs=placed,
        out_specs=(
            P(("ep", "tp"), None),
            P(("ep", "tp"), None),
            P(),
            P(("ep", "tp"), None),
            P(("ep", "tp"), None),
            P(("ep", "tp"), None),
            P(("ep", "tp"), None),
            P(("ep", "tp"), None),
            P(("ep", "tp"), None),
            P(("ep", "tp"), None),
            P(("ep", "tp"), None),
            P(("ep", "tp"), None),
            P(("ep", "tp"), None),
            P(("ep", "tp"), None),
            P(("ep", "tp"), None),
            P(("ep", "tp"), None),
            P(("ep", "tp"), None),
            P(("ep", "tp"), None),
            P(("ep", "tp"), None),
            P("ep", None, "tp", None),
            P("ep", None, "tp", None),
            P("ep", None, "tp", None),
            P("ep", None, "tp", None),
            P("ep", "tp", None),
            P("ep", "tp", None),
            P("ep", "tp", None),
            P("ep", "tp", None),
            P(None, ("ep", "tp")),
            P(None, ("ep", "tp")),
            P(None, ("ep", "tp")),
            P(None, ("ep", "tp")),
        ),
        check_vma=False,
    )
```

```python
import functools
import jax
import jax.numpy as jnp
import numpy as np
from jax import lax
from jax.experimental import pallas as pl
from jax.experimental.pallas import tpu as pltpu
from jax.sharding import PartitionSpec as P

HEADS = 10
HDIM = 128
FF = 896
TOPK = 7
STEP = 10


MESH = pl.DeviceIdType.MESH
VMEM_MOST = 60 * 1024 * 1024
NEG_BIG = -1000000000.0
NORM_EPS = 1e-06
ROPE_BASE = 10000.0
CLIP_LEVEL = 1.0
BETA_ONE = 0.9
BETA_TWO = 0.95
ADAM_EPS = 1e-08
WEIGHT_DECAY = 0.1
MATRIX_RATE = 0.05
GAIN_RATE = 0.5


class Place:
    def __init__(self, ep_count, tp_count):
        chips = ep_count // 2
        nb = 1
        while nb * nb * 4 <= chips:
            nb *= 2
        self.nb, self.na, self.nt = nb, chips // nb, tp_count
        self.ep_count = ep_count
        self.wrap = chips * tp_count >= 64
        e = lax.axis_index("ep")
        self.t = lax.axis_index("tp")
        self.core = lax.rem(e, 2)
        self.b = lax.rem(e // 2, nb)
        self.a = e // (2 * nb)

    def dims(self, order):
        if "u" in order and self.nb != self.nt:
            order = "abt"
        extents = {"a": self.na, "b": self.nb, "t": self.nt, "u": self.nb, "v": self.nt}
        return tuple((name, shifts(extents[name], self.wrap)) for name in order)

    def extent(self, name):
        return {"a": self.na, "b": self.nb, "t": self.nt, "u": self.nb, "v": self.nt}[name]

    def moved(self, name, shift):
        own, extent = self.own(name), self.extent(name)
        if shift == 0:
            return own, None
        if extent == 2:
            return 1 - own, None
        if self.wrap:
            return lax.rem(own + shift + extent, extent), None
        there = own + shift
        return there, (there >= 0) & (there < extent)

    def own(self, name):
        even = self.core == 0
        if name == "u":
            return jnp.where(even, self.b, self.t)
        if name == "v":
            return jnp.where(even, self.t, self.b)
        return getattr(self, name)

    def chip(self, at):
        a = at.get("a", self.a)
        b, t = at.get("b", self.b), at.get("t", self.t)
        if "u" in at:
            even = self.core == 0
            b = jnp.where(even, at["u"], at["v"])
            t = jnp.where(even, at["v"], at["u"])
        return a, b, t

    def device(self, at, core):
        a, b, t = self.chip(at)
        return ((a * self.nb + b) * 2 + core, t)

    def index(self, at, core, whole):
        e, t = self.device(at, core)
        return e * self.nt + t if whole else e

    def slot(self, at, whole):
        a, b, t = self.chip(at)
        chip = a * self.nb + b
        return chip * self.nt + t if whole else chip


def shifts(extent, wrap):
    if extent == 1:
        return (0,)
    if extent == 2:
        return (0, 1)
    found = [0]
    for step in range(1, extent // 2 + 1 if wrap else extent):
        found += [step, -step]
    return tuple(found[:extent] if wrap else found)


def ways(spread):
    return (1,) if len(spread) == 2 else (1, -1) if len(spread) > 2 else ()


def onward(spread, shift):
    way = -1 if shift > 0 else 1
    return way if len(spread) > 2 and shift - way in spread else 0


def both(one, other):
    if one is None:
        return other
    return one if other is None else one & other


def guarded(condition, body):
    if condition is None:
        body()
    else:
        pl.when(condition)(body)


def greet(place, order):
    barrier = pltpu.get_barrier_semaphore()
    here = {name: place.own(name) for name, _ in place.dims(order)}
    pl.semaphore_signal(barrier, inc=1, device_id=place.device(here, 1 - place.core), device_id_type=MESH)
    count = jnp.int32(1)
    for name, spread in place.dims(order):
        for way in ways(spread):
            there, on = place.moved(name, way)
            target = place.device({**here, name: there}, place.core)

            def signal(target=target):
                pl.semaphore_signal(barrier, inc=1, device_id=target, device_id_type=MESH)

            guarded(on, signal)
            count = count + (1 if on is None else on.astype(jnp.int32))
    if len(order) > 2:
        for s in range(2, place.nt - 1):
            target = place.device({"t": lax.rem(place.t + s, place.nt)}, place.core)
            pl.semaphore_signal(barrier, inc=1, device_id=target, device_id_type=MESH)
            count = count + 1
    pl.semaphore_wait(barrier, count)


def relative_blocks(dims):
    blocks = [()]
    for _, spread in dims:
        blocks = [block + (shift,) for block in blocks for shift in spread]
    return blocks


def by_core(place, order):
    if isinstance(order, str):
        return [(order, None)]
    return [(order[core], place.core == core) for core in range(2)]


def longest(groups):
    return max((order if isinstance(order, str) else order[0] for order, _ in groups), key=len)


def gather_events(place, order, only, pairs, send_sems, recv_sems):
    dims = place.dims(order)
    whole = len(dims) > 2
    here = {name: place.own(name) for name, _ in dims}
    counter = [0]
    ends = []

    def copies(at, target, core_of_block, own):
        index = place.index(at, core_of_block, whole)
        number = counter[0]
        counter[0] += 1
        made = []
        for k, (block, gathered) in enumerate(pairs):
            made.append(
                pltpu.make_async_remote_copy(
                    src_ref=block if own else gathered.at[index],
                    dst_ref=gathered.at[index],
                    send_sem=send_sems.at[k, number],
                    recv_sem=recv_sems.at[k, index],
                    device_id=target,
                    device_id_type=MESH,
                )
            )
        return made

    def send(at, on, target, own, todo):
        made = copies(at, target, place.core, own)

        def start(made=made):
            for copy in made:
                copy.start()

        def finish(made=made):
            for copy in made:
                copy.wait_send()

        todo.append((on, start))
        ends.append((on, finish))

    steps = []
    times = arrival_times(dims)
    for block in relative_blocks(dims):
        at, valid = dict(here), only
        for (name, _), shift in zip(dims, block):
            at[name], on = place.moved(name, shift)
            valid = both(valid, on)
        last = max([k for k, shift in enumerate(block) if shift], default=-1)
        own = last < 0
        todo = []
        for k in range(len(dims) - 1, -1, -1):
            name, spread = dims[k]
            if k < last:
                continue
            if k == last:
                way = onward(spread, block[k])
                sent = [way] if way else []
            else:
                sent = ways(spread)
            for way in sent:
                there, on = place.moved(name, way)
                target = place.device({**here, name: there}, place.core)
                send(at, both(valid, on), target, own, todo)
        send(at, valid, place.device(here, 1 - place.core), own, todo)
        index = place.index(at, place.core, whole)

        def step(index=index, valid=valid, todo=todo, own=own):
            def body():
                if not own:
                    for k, (_, gathered) in enumerate(pairs):
                        pltpu.make_async_copy(gathered.at[index], gathered.at[index], recv_sems.at[k, index]).wait()

            guarded(valid, body)
            for on, start in todo:
                guarded(on, start)

        steps.append((times[block], step))
        other = place.index(at, 1 - place.core, whole)

        def arrived(other=other):
            for k, (_, gathered) in enumerate(pairs):
                pltpu.make_async_copy(gathered.at[other], gathered.at[other], recv_sems.at[k, other]).wait()

        ends.append((valid, arrived))
    return steps, ends, counter[0]


def arrival_times(dims):
    times = {(): 0}
    for _, spread in dims:
        earlier = sorted(times, key=lambda block: times[block])
        found = {block + (0,): times[block] for block in earlier}
        for shift in spread:
            for i, block in enumerate(earlier):
                if shift:
                    far = abs(shift)
                    found[block + (shift,)] = max(times[block] + far, (far - 1) * len(earlier) + i + 1)
        times = found
    return times


def count_gather_sends(dims):
    total = 0
    for block in relative_blocks(dims):
        last = max([k for k, shift in enumerate(block) if shift], default=-1)
        for k, (_, spread) in enumerate(dims):
            if k > last:
                total += len(ways(spread))
            elif k == last and onward(spread, block[k]):
                total += 1
        total += 1
    return total


def exchange_copies(place, blocks, others, send_sems, recv_sems):
    copies = []
    for s in range(1, place.nt):
        back = blocks[0].shape == others[0].shape
        there = lax.rem(place.t + (s if back else place.nt - s), place.nt)
        target = place.device({"t": there}, place.core)
        for k, (block, other) in enumerate(zip(blocks, others)):
            copies.append(
                pltpu.make_async_remote_copy(
                    src_ref=block.at[s - 1] if back else block,
                    dst_ref=other.at[s - 1],
                    send_sem=send_sems.at[k, s - 1],
                    recv_sem=recv_sems.at[k, s - 1],
                    device_id=target,
                    device_id_type=MESH,
                )
            )
    return copies


def gather_kernel(ep_count, tp_count, groups, *refs):
    count = sum(n for _, n, _ in groups)
    blocks, gathered, scratch = refs[:count], refs[count : 2 * count], refs[2 * count :]
    place = Place(ep_count, tp_count)
    greet(place, longest([group[:2] for group in groups]))
    steps, ends, first = [], [], 0
    local, swaps = [], []
    for order, n, patience in groups:
        mine_in, mine_out = blocks[first : first + n], gathered[first : first + n]
        first += n
        if order == "t":
            swaps += exchange_copies(place, mine_in, mine_out, scratch[0], scratch[1])
            scratch = scratch[2:]
            continue
        send_sems, recv_sems, own_sems = scratch[:3]
        scratch = scratch[3:]
        pairs = list(zip(mine_in, mine_out))
        more, finish = [], []
        for lines, only in by_core(place, order):
            found = gather_events(place, lines, only, pairs, send_sems, recv_sems)
            more += found[0]
            finish += found[1]
        lines = by_core(place, order)[0][0]
        size = sum(block.shape[0] * block.shape[1] * (4 if block.dtype == jnp.float32 else 2) for block in mine_in)
        steps += [(key * size * patience, len(steps) + i, step) for i, (key, step) in enumerate(more)]
        ends += finish
        here = {name: place.own(name) for name, _ in place.dims(lines)}
        mine = place.index(here, place.core, len(lines) > 2)
        for k, (block, out) in enumerate(pairs):
            local.append(pltpu.make_async_copy(block, out.at[mine], own_sems.at[k]))
    steps.sort(key=lambda entry: entry[:2])
    lead = sum(1 for key, _, _ in steps if key == 0)
    for _, _, step in steps[:lead]:
        step()
    for copy in swaps + local:
        copy.start()
    for _, _, step in steps[lead:]:
        step()
    for on, finish in ends:
        guarded(on, finish)
    for copy in swaps + local:
        copy.wait()


def gather(ep_count, tp_count, collective_id, name, groups):
    arrays, shapes, scratch = [], [], []
    place = Place(ep_count, tp_count)
    for order, blocks, _ in groups:
        lines = [line for line, _ in by_core(place, order)]
        total = ep_count * tp_count if len(lines[0]) > 2 else ep_count if order != "t" else tp_count - 1
        for block in blocks:
            arrays.append(block)
            shapes.append(jax.ShapeDtypeStruct((total,) + block.shape, block.dtype))
        if order == "t":
            scratch += [pltpu.SemaphoreType.DMA((len(blocks), total))] * 2
            continue
        sends = max(count_gather_sends(place.dims(line)) for line in lines)
        scratch += [
            pltpu.SemaphoreType.DMA((len(blocks), sends)),
            pltpu.SemaphoreType.DMA((len(blocks), total)),
            pltpu.SemaphoreType.DMA((len(blocks),)),
        ]
    return pl.pallas_call(
        functools.partial(
            gather_kernel,
            ep_count,
            tp_count,
            tuple((order, len(blocks), patience) for order, blocks, patience in groups),
        ),
        out_shape=tuple(shapes),
        in_specs=[pl.BlockSpec(memory_space=pl.ANY)] * len(arrays),
        out_specs=tuple([pl.BlockSpec(memory_space=pl.ANY)] * len(arrays)),
        scratch_shapes=scratch,
        compiler_params=pltpu.CompilerParams(collective_id=collective_id, has_side_effects=True),
        name=name,
    )(*arrays)


def add_into(target, sources, dtype):
    rows, columns = target.shape
    piece = 128
    while columns % (piece * 2) == 0 and rows * piece * 2 <= 40 * 1024:
        piece *= 2

    def body(i, carry):
        window = pl.ds(pl.multiple_of(i * piece, piece), piece)
        total = sources[0][:, window].astype(jnp.float32)
        for source in sources[1:]:
            total = total + source[:, window].astype(jnp.float32)
        target[:, window] = total.astype(dtype)
        return carry

    lax.fori_loop(0, columns // piece, body, 0)


def norm_kernel(ep_count, tp_count, count, *refs):
    parts, extra, out = refs[:count], refs[count], refs[count + 1]
    tile, tiles, send, recv = refs[count + 2 :]
    devices = ep_count * tp_count
    me = lax.axis_index("ep") * tp_count + lax.axis_index("tp")

    def place(i):
        other = lax.rem(me + i, devices)
        return other, (other // tp_count, lax.rem(other, tp_count))

    barrier = pltpu.get_barrier_semaphore()

    def signal(i, carry):
        pl.semaphore_signal(barrier, inc=1, device_id=place(i)[1], device_id_type=MESH)
        return carry

    lax.fori_loop(1, devices, signal, 0)
    tile[...] = jnp.zeros_like(tile)
    for first in range(0, extra.shape[1], 128):
        tile[0:1, :] += extra[:, first : first + 128]
    for part in parts:

        def add(i, carry, part=part):
            piece = part[:, pl.ds(pl.multiple_of(i * 128, 128), 128)]
            tile[0:1, :] += jnp.sum(piece * piece, axis=0, keepdims=True)
            return carry

        lax.fori_loop(0, part.shape[1] // 128, add, 0)
    pl.semaphore_wait(barrier, devices - 1)

    def share(i, carry):
        pltpu.make_async_remote_copy(
            src_ref=tile,
            dst_ref=tiles.at[me],
            send_sem=send.at[i],
            recv_sem=recv.at[me],
            device_id=place(i)[1],
            device_id_type=MESH,
        ).start()
        return carry

    lax.fori_loop(1, devices, share, 0)
    out[...] = tile[...]

    def collect(i, carry):
        other = place(i)[0]
        pltpu.make_async_copy(tiles.at[other], tiles.at[other], recv.at[other]).wait()
        out[...] += tiles[other]
        return carry

    lax.fori_loop(1, devices, collect, 0)

    def sent(i, carry):
        pltpu.make_async_copy(tile, tile, send.at[i]).wait()
        return carry

    lax.fori_loop(1, devices, sent, 0)


def sum_of_squares(ep_count, tp_count, collective_id, parts, extra):
    devices = ep_count * tp_count
    inside = pl.BlockSpec(memory_space=pltpu.VMEM)
    total = pl.pallas_call(
        functools.partial(norm_kernel, ep_count, tp_count, len(parts)),
        out_shape=jax.ShapeDtypeStruct((8, 128), jnp.float32),
        in_specs=[inside] * (len(parts) + 1),
        out_specs=inside,
        scratch_shapes=[
            pltpu.VMEM((8, 128), jnp.float32),
            pltpu.VMEM((devices, 8, 128), jnp.float32),
            pltpu.SemaphoreType.DMA((devices,)),
            pltpu.SemaphoreType.DMA((devices,)),
        ],
        compiler_params=pltpu.CompilerParams(collective_id=collective_id, has_side_effects=True),
        name="sum_of_squares",
    )(*parts, extra)
    return jnp.sum(total)


def scatter_order(dims):
    blocks = sorted(relative_blocks(dims), key=lambda block: -sum(abs(s) for s in block))
    return sorted(blocks, key=lambda block: -max([k for k, s in enumerate(block) if s], default=-1))


def scatter_events(place, order, only, partials, outs, refs):
    count = len(partials)
    dims = place.dims(order)
    whole = len(dims) > 2
    here = {name: place.own(name) for name, _ in dims}
    owns, sibs = refs[:count], refs[count : 2 * count]
    lands = [refs[(2 + k) * count : (3 + k) * count] for k in range(len(dims))]
    sems = refs[(2 + len(dims)) * count :]
    own_sem, sib_send, sib_recv, line_send = sems[:4]
    line_recv = sems[4:]
    blocks = scatter_order(dims)
    info = {}
    starts, steps, ends = [], [], []
    for block in blocks:
        at, valid = dict(here), only
        for (name, _), shift in zip(dims, block):
            at[name], on = place.moved(name, shift)
            valid = both(valid, on)
        slot = place.slot(at, whole)
        local = [
            pltpu.make_async_copy(
                partials[k].at[place.index(at, place.core, whole)], owns[k].at[slot], own_sem.at[k, slot]
            )
            for k in range(count)
        ]
        across = [
            pltpu.make_async_remote_copy(
                src_ref=partials[k].at[place.index(at, 1 - place.core, whole)],
                dst_ref=sibs[k].at[slot],
                send_sem=sib_send.at[k, slot],
                recv_sem=sib_recv.at[k, slot],
                device_id=place.device(here, 1 - place.core),
                device_id_type=MESH,
            )
            for k in range(count)
        ]

        def start(local=local, across=across):
            for copy in across + local:
                copy.start()

        def finish(across=across):
            for copy in across:
                copy.wait_send()

        starts.append((valid, start))
        ends.append((valid, finish))
        info[block] = (at, valid, slot, local, across)

    def land_slot(level, at, shift, side):
        inner, wide = 0, 1
        for name, _ in dims[:level]:
            inner = inner * place.extent(name) + at[name]
            wide = wide * place.extent(name)
        return landings(dims[level][1]).index((shift, side)) * wide + inner

    number = 0
    for block in blocks:
        at, valid, slot, local, across = info[block]
        todo = []
        last = max([k for k, shift in enumerate(block) if shift], default=-1)
        extra_refs = []
        for level in range(len(dims) - 1, max(last, 0) - 1, -1):
            name, spread = dims[level]
            for shift, side in landings(spread):
                if shift == block[level]:
                    _, on = place.moved(name, side)
                    extra_refs.append((level, land_slot(level, at, shift, side), on))

        def arrive(local=local, across=across):
            for copy in local:
                copy.wait()
            for copy in across:
                copy.wait_recv()

        todo.append((valid, arrive))
        for k in range(count):
            sure = [owns[k].at[slot], sibs[k].at[slot]]
            maybe = []
            for level, spot, on in extra_refs:
                ref = lands[level][k].at[spot]

                def wait(ref=ref, k=k, level=level, spot=spot):
                    pltpu.make_async_copy(ref, ref, line_recv[level].at[k, spot]).wait()

                todo.append((both(valid, on), wait))
                if on is None:
                    sure.append(ref)
                else:
                    maybe.append((ref, on))
            if last >= 0:
                target, dtype = owns[k].at[slot], owns[k].dtype
            else:
                target, dtype = outs[k], outs[k].dtype

            def add(sure=sure, maybe=maybe, target=target, dtype=dtype):
                if not maybe:
                    add_into(target, sure, dtype)
                elif len(maybe) == 1:
                    ((ref, on),) = maybe
                    pl.when(on)(lambda: add_into(target, sure + [ref], dtype))
                    pl.when(jnp.logical_not(on))(lambda: add_into(target, sure, dtype))
                else:
                    (low, on_low), (high, on_high) = maybe
                    pl.when(on_low & on_high)(lambda: add_into(target, sure + [low, high], dtype))
                    pl.when(on_low & jnp.logical_not(on_high))(lambda: add_into(target, sure + [low], dtype))
                    pl.when(on_high & jnp.logical_not(on_low))(lambda: add_into(target, sure + [high], dtype))

            todo.append((valid, add))
        if last >= 0:
            name, spread = dims[last]
            way = 1 if block[last] > 0 else -1
            there, _ = place.moved(name, way)
            spot = land_slot(last, at, block[last] - way, -way if len(spread) > 2 else 1)
            made = [
                pltpu.make_async_remote_copy(
                    src_ref=owns[k].at[slot],
                    dst_ref=lands[last][k].at[spot],
                    send_sem=line_send.at[k, number],
                    recv_sem=line_recv[last].at[k, spot],
                    device_id=place.device({**here, name: there}, place.core),
                    device_id_type=MESH,
                )
                for k in range(count)
            ]
            number += 1

            def start(made=made):
                for copy in made:
                    copy.start()

            def finish(made=made):
                for copy in made:
                    copy.wait_send()

            todo.append((valid, start))
            ends.append((valid, finish))
        steps.append(todo)
    return starts, steps, ends


def scatter_sizes(place, order):
    found = []
    for line, _ in by_core(place, order):
        dims = place.dims(line)
        slots, lands = 1, []
        for name, spread in dims:
            lands.append(len(landings(spread)) * slots)
            slots *= place.extent(name)
        found.append((slots, lands, sum(1 for block in relative_blocks(dims) if any(block))))
    lands = [max(wide) for wide in zip(*[entry[1] for entry in found])]
    return found[0][0], lands, max(entry[2] for entry in found)


def scatter_scratch(place, order, partials):
    slots, lands, sends = scatter_sizes(place, order)
    count, dma = len(partials), pltpu.SemaphoreType.DMA
    scratch = []
    for wide in [slots, slots] + lands:
        scratch += [pltpu.VMEM((wide,) + p.shape[1:], p.dtype) for p in partials]
    return scratch + [dma((count, slots))] * 3 + [dma((count, sends))] + [dma((count, wide)) for wide in lands]


def greet_all(ep_count, tp_count):
    devices = ep_count * tp_count
    me = lax.axis_index("ep") * tp_count + lax.axis_index("tp")
    barrier = pltpu.get_barrier_semaphore()

    def signal(i, carry):
        other = lax.rem(me + i, devices)
        target = (other // tp_count, lax.rem(other, tp_count))
        pl.semaphore_signal(barrier, inc=1, device_id=target, device_id_type=MESH)
        return carry

    lax.fori_loop(1, devices, signal, 0)
    pl.semaphore_wait(barrier, devices - 1)


def add_squares(total, ref):
    def add(i, carry):
        piece = ref[:, pl.ds(pl.multiple_of(i * 128, 128), 128)]
        total[0:1, :] += jnp.sum(piece * piece, axis=0, keepdims=True)
        return carry

    lax.fori_loop(0, ref.shape[1] // 128, add, 0)


def exchanged_pieces(own, others, summed, total, held, come, load_sems, save_sem):
    pieces, parts = own.shape[0], others.shape[0]

    def loads(q):
        found = [pltpu.make_async_copy(own.at[q], held.at[q % 2], load_sems.at[q % 2, 0])]
        for s in range(parts):
            found.append(pltpu.make_async_copy(others.at[s, q], come.at[q % 2, s], load_sems.at[q % 2, s + 1]))
        return found

    def save(q):
        return pltpu.make_async_copy(held.at[q % 2], summed.at[q], save_sem.at[q % 2])

    def load(q):
        if q >= 2:
            save(q - 2).wait()
        for copy in loads(q):
            copy.start()

    def piece(q):
        for copy in loads(q):
            copy.wait()
        arrived = [come.at[q % 2, s] for s in range(parts)]
        add_into(held.at[q % 2], [held.at[q % 2]] + arrived, jnp.float32)
        add_squares(total, held.at[q % 2])
        save(q).start()
        if q + 2 < pieces:
            load(q + 2)

    def finish():
        for q in range(max(0, pieces - 2), pieces):
            save(q).wait()

    for q in range(min(2, pieces)):
        load(q)
    return [functools.partial(piece, q) for q in range(pieces)] + [finish]


def share_total(ep_count, tp_count, total, totals, send, recv, norm):
    devices = ep_count * tp_count
    me = lax.axis_index("ep") * tp_count + lax.axis_index("tp")

    def share(i, carry):
        other = lax.rem(me + i, devices)
        pltpu.make_async_remote_copy(
            src_ref=total,
            dst_ref=totals.at[me],
            send_sem=send.at[i],
            recv_sem=recv.at[me],
            device_id=(other // tp_count, lax.rem(other, tp_count)),
            device_id_type=MESH,
        ).start()
        return carry

    lax.fori_loop(1, devices, share, 0)
    norm[...] = total[...]

    def collect(i, carry):
        other = lax.rem(me + i, devices)
        pltpu.make_async_copy(totals.at[other], totals.at[other], recv.at[other]).wait()
        norm[...] += totals[other]
        return carry

    lax.fori_loop(1, devices, collect, 0)
    norm[...] = jnp.broadcast_to(jnp.sqrt(jnp.sum(norm[...], keepdims=True)), norm.shape)

    def sent(i, carry):
        pltpu.make_async_copy(total, total, send.at[i]).wait()
        return carry

    lax.fori_loop(1, devices, sent, 0)


def scatter_kernel(ep_count, tp_count, groups, normed, *refs):
    count = sum(n for _, n in groups)
    partials, refs = refs[:count], refs[count:]
    if normed:
        own, others, refs = refs[0], refs[1], refs[2:]
    outs, refs = refs[:count], refs[count:]
    if normed:
        summed, norm, refs = refs[0], refs[1], refs[2:]
        total, totals, held, come, load_sems, save_sem, send, recv = refs[:8]
        refs = refs[8:]
    place = Place(ep_count, tp_count)
    if normed:
        greet_all(ep_count, tp_count)
    else:
        greet(place, longest(groups))
    starts, steps, ends, swaps, first = [], [], [], [], 0
    for order, n in groups:
        mine_in, mine_out = partials[first : first + n], outs[first : first + n]
        first += n
        if order == "t":
            swaps += exchange_copies(place, mine_in, mine_out, refs[0], refs[1])
            refs = refs[2:]
            continue
        lines = by_core(place, order)
        used = n * (2 + len(lines[0][0])) + 4 + len(lines[0][0])
        for line, only in lines:
            more, done, finish = scatter_events(place, line, only, mine_in, mine_out, refs[:used])
            starts += [(i / len(more), len(starts) + i, entry) for i, entry in enumerate(more)]
            steps += [(i / len(done), len(steps) + i, todo) for i, todo in enumerate(done)]
            ends += finish
        refs = refs[used:]
    for copy in swaps:
        copy.start()
    for _, _, (on, start) in sorted(starts, key=lambda entry: entry[:2]):
        guarded(on, start)
    steps = [todo for _, _, todo in sorted(steps, key=lambda entry: entry[:2])]
    if normed:
        total[...] = jnp.zeros_like(total)
        extras = exchanged_pieces(own, others, summed, total, held, come, load_sems, save_sem)
        for i, act in enumerate(extras):
            steps.insert((4 + i) * len(steps) // (5 + len(extras)), [(None, act)])
    for todo in steps:
        for on, act in todo:
            guarded(on, act)
    if normed:
        for out in outs:
            add_squares(total, out)
        share_total(ep_count, tp_count, total, totals, send, recv, norm)
    for on, finish in ends:
        guarded(on, finish)
    for copy in swaps:
        copy.wait()


def landings(spread):
    if len(spread) == 2:
        return [(0, 1)]
    return [(shift, way) for shift in spread for way in (-1, 1) if shift - way in spread and shift * way <= 0]


def scatter_add(ep_count, tp_count, collective_id, name, groups, grads=None):
    place = Place(ep_count, tp_count)
    arrays, shapes, scratch, specs = [], [], [], []
    normed = grads is not None
    dma = pltpu.SemaphoreType.DMA
    for order, partials in groups:
        arrays += partials
        count = len(partials)
        if order == "t":
            shapes += [jax.ShapeDtypeStruct(p.shape, p.dtype) for p in partials]
            specs += [pl.BlockSpec(memory_space=pl.ANY)] * count
            scratch += [dma((count, tp_count - 1))] * 2
            continue
        shapes += [jax.ShapeDtypeStruct(p.shape[1:], jnp.float32) for p in partials]
        specs += [pl.BlockSpec(memory_space=pltpu.VMEM)] * count
        scratch += scatter_scratch(place, order, partials)
    if normed:
        own, others = grads
        arrays += [own, others]
        devices, parts = ep_count * tp_count, others.shape[0]
        shapes += [jax.ShapeDtypeStruct(own.shape, own.dtype), jax.ShapeDtypeStruct((8, 128), jnp.float32)]
        specs += [pl.BlockSpec(memory_space=pl.ANY), pl.BlockSpec(memory_space=pltpu.VMEM)]
        scratch = [
            pltpu.VMEM((8, 128), jnp.float32),
            pltpu.VMEM((devices, 8, 128), jnp.float32),
            pltpu.VMEM((2,) + own.shape[1:], own.dtype),
            pltpu.VMEM((2, parts) + own.shape[1:], others.dtype),
            dma((2, parts + 1)),
            dma((2,)),
            dma((devices,)),
            dma((devices,)),
        ] + scratch
    return pl.pallas_call(
        functools.partial(
            scatter_kernel,
            ep_count,
            tp_count,
            tuple((order, len(partials)) for order, partials in groups),
            normed,
        ),
        out_shape=tuple(shapes),
        in_specs=[pl.BlockSpec(memory_space=pl.ANY)] * len(arrays),
        out_specs=tuple(specs),
        scratch_shapes=scratch,
        compiler_params=pltpu.CompilerParams(
            collective_id=collective_id, has_side_effects=True, vmem_limit_bytes=VMEM_MOST
        ),
        name=name,
    )(*arrays)


def scatter_room(place, order, partials):
    slots, lands, _ = scatter_sizes(place, order)
    rows = [(p.shape[1] + 15) // 16 * 16 for p in partials]
    sizes = [r * p.shape[2] * p.dtype.itemsize for r, p in zip(rows, partials)]
    return (2 * slots + sum(lands)) * sum(sizes)


def scatter_all(ep_count, tp_count, collective_ids, name, groups):
    place = Place(ep_count, tp_count)
    calls, room = [[]], 0
    for order, partials in groups:
        need = 0 if order == "t" else scatter_room(place, order, partials)
        if calls[-1] and room + need > VMEM_MOST * 19 // 20:
            calls.append([])
            room = 0
        calls[-1].append((order, partials))
        room += need
    found = []
    for i, call in enumerate(calls):
        found += scatter_add(ep_count, tp_count, collective_ids[i], "%s_%d" % (name, i), call)
    return found

OVER_LAST = (((1,), (1,)), ((), ()))
OVER_FIRST = (((0,), (0,)), ((), ()))
STRAIGHT = (((1,), (0,)), ((), ()))


def mul(left, right, dims=STRAIGHT):
    return lax.dot_general(left, right, dims, preferred_element_type=jnp.float32)


def rope_rows(length):
    places = np.arange(length, dtype=np.float32)
    frequencies = ROPE_BASE ** (-np.arange(HDIM // 2, dtype=np.float32) * np.float32(2.0 / HDIM))
    angles = places[:, None] * frequencies.astype(np.float32)[None, :]
    cosine, sine = np.cos(angles), np.sin(angles)
    return (
        np.concatenate([cosine, cosine], axis=1).astype(np.float32),
        np.concatenate([-sine, sine], axis=1).astype(np.float32),
    )


def unit_of(values):
    factor = lax.rsqrt(jnp.mean(values * values, axis=-1, keepdims=True) + NORM_EPS)
    return values * factor, factor


def masked_probs(queries, keys, allowed):
    raw = mul(queries, keys, OVER_LAST) * HDIM ** (-0.5)
    scores = jnp.where(allowed, raw, NEG_BIG)
    weights = jnp.exp(scores - jnp.max(scores, axis=-1, keepdims=True))
    return weights * (1.0 / jnp.sum(weights, axis=-1, keepdims=True))


def allowed_pairs(seg_row, seg_column):
    length = seg_row.shape[1]
    later = lax.broadcasted_iota(jnp.int32, (length, length), 0)
    earlier = lax.broadcasted_iota(jnp.int32, (length, length), 1)
    return (later >= earlier) & (seg_column[:, 0:1] == seg_row[0:1, :])


def forward_kernel(tokens, seg_row, seg_column, gains, cosine, sine, wq, wk, wv, wo,
                   qkv_out, attended, hidden, normed_two, normed):
    pair = pl.program_id(0)
    width = tokens.shape[1]
    wide = 2 * HDIM

    @pl.when(pair == 0)
    def _():
        values = tokens[...].astype(jnp.float32)
        normed[...] = (unit_of(values)[0] * gains[0:1, :]).astype(jnp.bfloat16)
        hidden[...] = values

    allowed = allowed_pairs(seg_row, seg_column)
    window = pl.ds(pl.multiple_of(pair * wide, wide), wide)
    made = []
    for part, weight in enumerate((wq, wk, wv)):
        projected = mul(normed[...], weight[...])
        heads = []
        for j in range(2):
            head = projected[:, j * HDIM : (j + 1) * HDIM]
            if part < 2:
                head = head * cosine[...] + pltpu.roll(head, HDIM // 2, 1) * sine[...]
            heads.append(head.astype(jnp.bfloat16))
            qkv_out[:, pl.ds(pl.multiple_of(part * width + pair * wide + j * HDIM, HDIM), HDIM)] = heads[j]
        made.append(heads)
    for j in range(2):
        probs = masked_probs(made[0][j], made[1][j], allowed).astype(jnp.bfloat16)
        attended[:, pl.ds(pl.multiple_of(pair * wide + j * HDIM, HDIM), HDIM)] = mul(
            probs, made[2][j]
        ).astype(jnp.bfloat16)
    hidden[...] += mul(attended[:, window], wo[...])

    @pl.when(pair == pl.num_programs(0) - 1)
    def _():
        normed_two[...] = (unit_of(hidden[...])[0] * gains[1:2, :]).astype(jnp.bfloat16)


def attention_forward(tokens, segments, gains, qkv_low, out_low):
    length, width = tokens.shape
    wide, pairs = 2 * HDIM, HEADS // 2
    cosine, sine = rope_rows(length)
    seg_row = jnp.broadcast_to(segments, (8, length))
    seg_column = jnp.broadcast_to(segments.T, (length, 128))
    low = jnp.bfloat16

    def whole(*shape):
        return pl.BlockSpec(shape, lambda i: (0,) * len(shape))

    def columns(part):
        return pl.BlockSpec((width, wide), lambda i: (0, part * pairs + i))

    return pl.pallas_call(
        forward_kernel,
        grid=(pairs,),
        in_specs=[
            whole(length, width), whole(8, length), whole(length, 128), whole(8, width),
            whole(length, HDIM), whole(length, HDIM), columns(0), columns(1), columns(2),
            pl.BlockSpec((wide, width), lambda i: (i, 0)),
        ],
        out_specs=[whole(length, 3 * width), whole(length, width), whole(length, width), whole(length, width)],
        out_shape=[
            jax.ShapeDtypeStruct((length, 3 * width), low),
            jax.ShapeDtypeStruct((length, width), low),
            jax.ShapeDtypeStruct((length, width), jnp.float32),
            jax.ShapeDtypeStruct((length, width), low),
        ],
        scratch_shapes=[pltpu.VMEM((length, width), low)],
        compiler_params=pltpu.CompilerParams(
            dimension_semantics=("arbitrary",), vmem_limit_bytes=VMEM_MOST
        ),
        name="attention_forward",
    )(tokens, seg_row, seg_column, gains, jnp.asarray(cosine), jnp.asarray(sine), qkv_low, qkv_low, qkv_low, out_low)


def spread_matrix(units, padded, group, step):
    unit = lax.broadcasted_iota(jnp.int32, (units, padded), 0)
    spot = lax.broadcasted_iota(jnp.int32, (units, padded), 1)
    within = jnp.bitwise_and(spot, step - 1)
    source = (spot - within) // step * group + within
    return jnp.where((unit == source) & (within < group), 1.0, 0.0).astype(jnp.bfloat16)


def backward_kernel(group, step, carried, *refs):
    (tokens, cot, seg_row, seg_column, gains, cosine, sine, qkv_act, attended, hidden, normed_two,
     routed_grad, wq, wk, wv, wo, shin, shout) = refs[:18]
    refs = refs[18:]
    if carried:
        ep_count, tp_count, order = carried
        result_part, sent_grads, refs = refs[0], refs[1], refs[2:]
    base, tokens_grad, gain_grads, qkv_grad, out_grad, shin_grad, shout_grad = refs[:7]
    refs = refs[7:]
    if carried:
        routed, grads_back, refs = refs[0], refs[1], refs[2:]
    (normed, normed_turned, branch, grad_one, pieces, stage, stage_sem) = refs[:7]
    refs = refs[7:]
    at = pl.program_id(0)
    width = tokens.shape[1]
    wide = 2 * HDIM
    low = jnp.bfloat16
    units = shin.shape[1] // 2

    if carried:
        place = Place(ep_count, tp_count)
        starts, lines, ends = scatter_events(place, order, None, [result_part], [routed], refs[:-2])
        swaps = exchange_copies(place, [sent_grads], [grads_back], refs[-2], refs[-1])
        first = sum(1 for block in scatter_order(place.dims(order)) if block[-1])
        turns = {0: lines[:first], 2: lines[first : first + 2], 4: lines[first + 2 : first + 4]}
        turns[5] = lines[first + 4 :]

    def run(entries):
        for on, act in entries:
            guarded(on, act)

    def carry(turn):
        if carried:
            for todo in turns.get(turn, []):
                run(todo)

    def stage_copy(part, pair):
        return pltpu.make_async_copy(
            stage.at[part],
            qkv_grad.at[:, pl.ds(pl.multiple_of(part * width + pair * wide, wide), wide)],
            stage_sem.at[part],
        )

    @pl.when(at == 0)
    def _():
        if carried:
            greet(place, "tab")
            for copy in swaps:
                copy.start()
            run(starts)
        unit_one = unit_of(tokens[...].astype(jnp.float32))[0]
        first = unit_one * gains[0:1, :]
        normed[...] = first.astype(low)
        normed_turned[...] = first.T.astype(low)
        pre_gate = mul(normed_two[...], shin[:, :units])
        pre_up = mul(normed_two[...], shin[:, units:])
        sigmoid = jax.nn.sigmoid(pre_gate)
        act = (pre_gate * sigmoid * pre_up).astype(low)
        spread = spread_matrix(units, shout.shape[0], group, step)
        act_spread = mul(act, spread).astype(low)
        base[...] = hidden[...] + mul(act_spread, shout[...])
        shout_grad[...] = mul(act_spread, cot[...], OVER_FIRST).astype(low)
        carry(0)
        shout_tight = mul(spread, shout[...]).astype(low)
        grad_act = mul(cot[...], shout_tight, OVER_LAST)
        grad_up = (grad_act * pre_gate * sigmoid).astype(low)
        grad_gate = (grad_act * pre_up * sigmoid * (1.0 + pre_gate * (1.0 - sigmoid))).astype(low)
        shin_grad[:, :units] = mul(normed_two[...], grad_gate, OVER_FIRST).astype(low)
        shin_grad[:, units:] = mul(normed_two[...], grad_up, OVER_FIRST).astype(low)
        grad_two = (
            routed_grad[...]
            + mul(grad_gate, shin[:, :units], OVER_LAST)
            + mul(grad_up, shin[:, units:], OVER_LAST)
        )
        unit_two, factor_two = unit_of(hidden[...])
        gain_grads[...] = jnp.zeros_like(gain_grads)
        gain_grads[1:2, :] = jnp.sum(grad_two * unit_two, axis=0, keepdims=True)
        grad_unit = grad_two * gains[1:2, :]
        back = factor_two * (
            grad_unit - unit_two * jnp.mean(grad_unit * unit_two, axis=-1, keepdims=True)
        )
        tokens_grad[...] = cot[...].astype(jnp.float32) + back
        branch[...] = tokens_grad[...].astype(low)
        grad_one[...] = jnp.zeros_like(grad_one)

    @pl.when(at > 0)
    def _():
        pair = at - 1
        allowed = allowed_pairs(seg_row, seg_column)
        window = pl.ds(pl.multiple_of(pair * wide, wide), wide)
        out_grad[...] = mul(attended[:, window], branch[...], OVER_FIRST).astype(low)
        grad_att = mul(branch[...], wo[...], OVER_LAST).astype(low)
        for j in range(2):

            def head(part):
                start = pl.multiple_of(part * width + pair * wide + j * HDIM, HDIM)
                return qkv_act[:, pl.ds(start, HDIM)]

            queries, keys, values = head(0), head(1), head(2)
            own = slice(j * HDIM, (j + 1) * HDIM)
            grad_own = grad_att[:, own]
            probs = masked_probs(queries, keys, allowed)
            grad_probs = mul(grad_own, values, OVER_LAST)
            grad_values = mul(probs.astype(low), grad_own, OVER_FIRST)
            row_dot = jnp.sum(probs * grad_probs, axis=-1, keepdims=True)
            grad_scores = (probs * (grad_probs - row_dot)).astype(low)
            grad_queries = mul(grad_scores, keys) * HDIM ** (-0.5)
            grad_keys = mul(grad_scores, queries, OVER_FIRST) * HDIM ** (-0.5)
            for part, grad in ((0, grad_queries), (1, grad_keys), (2, grad_values)):
                if part < 2:
                    grad = grad * cosine[...] - pltpu.roll(grad, HDIM // 2, 1) * sine[...]
                pieces[part, :, own] = grad.astype(low)
        for part, weight in enumerate((wq, wk, wv)):

            @pl.when(pair > 0)
            def _(part=part):
                stage_copy(part, pair - 1).wait()

            stage[part] = mul(normed_turned[...], pieces[part]).astype(low)
            stage_copy(part, pair).start()
            grad_one[...] += mul(pieces[part], weight[...], OVER_LAST)

        for turn in (2, 4):
            pl.when(at == turn)(functools.partial(carry, turn))

        @pl.when(at == pl.num_programs(0) - 1)
        def _():
            unit_one, factor_one = unit_of(tokens[...].astype(jnp.float32))
            total = grad_one[...]
            gain_grads[0:1, :] = jnp.sum(total * unit_one, axis=0, keepdims=True)
            grad_unit = total * gains[0:1, :]
            back = factor_one * (
                grad_unit - unit_one * jnp.mean(grad_unit * unit_one, axis=-1, keepdims=True)
            )
            tokens_grad[...] += back
            for part in range(3):
                stage_copy(part, pair).wait()
            carry(5)
            if carried:
                run(ends)
                for copy in swaps:
                    copy.wait()


def dense_backward(group, step, tokens, cot, segments, gains, qkv_act, attended, hidden, normed_two,
                   routed_grad, qkv_low, out_low, shin_low, shout_spread, ep_count, tp_count,
                   collective_id, order, result_part, sent_grads):
    length, width = tokens.shape
    wide, pairs = 2 * HDIM, HEADS // 2
    cosine, sine = rope_rows(length)
    seg_row = jnp.broadcast_to(segments, (8, length))
    seg_column = jnp.broadcast_to(segments.T, (length, 128))
    low = jnp.bfloat16
    once = pl.Buffered(1)

    def whole(*shape):
        return pl.BlockSpec(shape, lambda i: (0,) * len(shape), pipeline_mode=once)

    def columns(part):
        return pl.BlockSpec((width, wide), lambda i: (0, part * pairs + jnp.maximum(i - 1, 0)))

    rows = pl.BlockSpec((wide, width), lambda i: (jnp.maximum(i - 1, 0), 0))
    in_specs = [
        whole(length, width), whole(length, width), whole(8, length), whole(length, 128),
        whole(8, width), whole(length, HDIM), whole(length, HDIM), whole(length, 3 * width),
        whole(length, width), whole(length, width), whole(length, width), whole(length, width),
        columns(0), columns(1), columns(2), rows,
        whole(*shin_low.shape), whole(*shout_spread.shape),
    ]
    anywhere = pl.BlockSpec(memory_space=pl.ANY)
    out_specs = [
        whole(length, width), whole(length, width), whole(8, width),
        anywhere, rows, whole(*shin_low.shape), whole(*shout_spread.shape),
    ]
    out_shape = [
        jax.ShapeDtypeStruct((length, width), jnp.float32),
        jax.ShapeDtypeStruct((length, width), jnp.float32),
        jax.ShapeDtypeStruct((8, width), jnp.float32),
        jax.ShapeDtypeStruct((width, 3 * width), low),
        jax.ShapeDtypeStruct((width, width), low),
        jax.ShapeDtypeStruct(shin_low.shape, low),
        jax.ShapeDtypeStruct(shout_spread.shape, low),
    ]
    scratch = [
        pltpu.VMEM((length, width), low), pltpu.VMEM((width, length), low),
        pltpu.VMEM((length, width), low), pltpu.VMEM((length, width), jnp.float32),
        pltpu.VMEM((3, length, wide), low),
        pltpu.VMEM((3, width, wide), low), pltpu.SemaphoreType.DMA((3,)),
    ]
    arguments = [tokens, cot, seg_row, seg_column, gains, jnp.asarray(cosine), jnp.asarray(sine), qkv_act,
                 attended, hidden, normed_two, routed_grad, qkv_low, qkv_low, qkv_low, out_low, shin_low,
                 shout_spread]
    carried, more = None, {}
    if result_part is not None:
        carried, more = (ep_count, tp_count, order), dict(collective_id=collective_id, has_side_effects=True)
        arguments += [result_part, sent_grads]
        in_specs += [anywhere, anywhere]
        out_specs += [whole(length, width), anywhere]
        out_shape += [
            jax.ShapeDtypeStruct((length, width), jnp.float32),
            jax.ShapeDtypeStruct(sent_grads.shape, sent_grads.dtype),
        ]
        scratch += scatter_scratch(Place(ep_count, tp_count), order, [result_part])
        scratch += [pltpu.SemaphoreType.DMA((1, tp_count - 1))] * 2
    return pl.pallas_call(
        functools.partial(backward_kernel, group, step, carried),
        grid=(pairs + 1,),
        in_specs=in_specs,
        out_specs=out_specs,
        out_shape=out_shape,
        scratch_shapes=scratch,
        compiler_params=pltpu.CompilerParams(
            dimension_semantics=("arbitrary",), vmem_limit_bytes=VMEM_MOST, **more
        ),
        name="dense_backward",
    )(*arguments)


def expert_kernel(parts, per_step, cap, *refs):
    normed, cot, info = refs[:3]
    ins, outs_w = refs[3 : 3 + parts], refs[3 + parts : 3 + 2 * parts]
    result_ref, input_ref, own_grad = refs[3 + 2 * parts : 6 + 2 * parts]
    sent = refs[6 + 2 * parts : 5 + 3 * parts]
    scratch = refs[5 + 3 * parts :]
    rows_x, rows_g, gate_col, result_acc, input_acc = scratch[:5]
    sums = (own_grad,) + tuple(scratch[5:])
    step = pl.program_id(0)
    tok = normed.shape[1]
    width = normed.shape[2]
    chunk = 256

    @pl.when(step == 0)
    def _():
        for total in sums:
            total[...] = jnp.zeros_like(total)

    slots = lax.broadcasted_iota(jnp.int32, (cap, tok), 0).astype(jnp.float32)
    for s in range(per_step):
        hit = slots == info[s, 0:1, :]
        picks = jnp.where(hit, 1.0, 0.0).astype(jnp.bfloat16)
        gates = jnp.sum(jnp.where(hit, info[s, 1:2, :], 0.0), axis=1, keepdims=True)
        window = pl.ds(s * cap, cap)
        gate_col[window, :] = jnp.broadcast_to(gates, (cap, 128))
        rows_x[window, :] = jnp.dot(picks, normed[s], preferred_element_type=jnp.float32).astype(
            jnp.bfloat16
        )
        taken = jnp.dot(picks, cot[s], preferred_element_type=jnp.float32)
        rows_g[window, :] = (gates * taken).astype(jnp.bfloat16)
    across = (((1,), (1,)), ((), ()))
    down = (((0,), (0,)), ((), ()))

    def mul(left, right, dims):
        return lax.dot_general(left, right, dims, preferred_element_type=jnp.float32)

    straight = (((1,), (0,)), ((), ()))
    for p in range(parts):
        gate_pre = mul(rows_x[...], ins[p][0], across)
        up_pre = mul(rows_x[...], ins[p][1], across)
        sigmoid = jax.nn.sigmoid(gate_pre)
        active = (gate_pre * sigmoid * up_pre).astype(jnp.bfloat16)
        grad_act = mul(rows_g[...], outs_w[p][...], across)
        grad_up = (grad_act * gate_pre * sigmoid).astype(jnp.bfloat16)
        grad_gate = (grad_act * up_pre * sigmoid * (1.0 + gate_pre * (1.0 - sigmoid))).astype(
            jnp.bfloat16
        )
        for first in range(0, width, chunk):
            window = slice(first, first + chunk)
            result = mul(active, outs_w[p][:, window], straight)
            back = mul(grad_gate, ins[p][0, :, window], straight) + mul(
                grad_up, ins[p][1, :, window], straight
            )
            if p == 0:
                result_acc[:, window] = result
                input_acc[:, window] = back
            else:
                result_acc[:, window] += result
                input_acc[:, window] += back
            sums[p][0, :, window] += mul(grad_gate, rows_x[:, window], down)
            sums[p][1, :, window] += mul(grad_up, rows_x[:, window], down)
            sums[p][2, :, window] += mul(active, rows_g[:, window], down)
    for s in range(per_step):
        hit = slots == info[s, 0:1, :]
        picks = jnp.where(hit, 1.0, 0.0).astype(jnp.bfloat16)
        window = pl.ds(s * cap, cap)
        rounded = result_acc[window, :].astype(jnp.bfloat16).astype(jnp.float32)
        weighted = (gate_col[window, 0:1] * rounded).astype(jnp.bfloat16)
        result_ref[s] = mul(picks, weighted, down).astype(jnp.bfloat16)
        input_ref[s] = mul(picks, input_acc[window, :].astype(jnp.bfloat16), down).astype(
            jnp.bfloat16
        )

    @pl.when(step == pl.num_programs(0) - 1)
    def _():
        for p in range(1, parts):
            sent[p - 1][...] = sums[p][...].astype(jnp.bfloat16)


def expert_pass(normed_all, cot_all, info, ins, outs_w, cap):
    ep_count, tok, width = normed_all.shape
    parts = len(ins)
    hidden = ins[0].shape[1]
    per_step = max(1, min(ep_count, 256 // cap))
    rows = per_step * cap
    token_spec = pl.BlockSpec((per_step, tok, width), lambda i: (i, 0, 0))
    once = pl.Buffered(1)
    in_specs = [token_spec, token_spec, pl.BlockSpec((per_step, 2, tok), lambda i: (i, 0, 0))]
    in_specs += [
        pl.BlockSpec((2, hidden, width), lambda i: (0, 0, 0), pipeline_mode=once)
    ] * parts
    in_specs += [pl.BlockSpec((hidden, width), lambda i: (0, 0), pipeline_mode=once)] * parts
    grad_spec = pl.BlockSpec((3, hidden, width), lambda i: (0, 0, 0), pipeline_mode=once)
    token_shape = jax.ShapeDtypeStruct((ep_count, tok, width), jnp.bfloat16)
    out_shape = [token_shape, token_shape, jax.ShapeDtypeStruct((3, hidden, width), jnp.float32)]
    out_shape += [jax.ShapeDtypeStruct((3, hidden, width), jnp.bfloat16)] * (parts - 1)
    scratch = [
        pltpu.VMEM((rows, width), jnp.bfloat16),
        pltpu.VMEM((rows, width), jnp.bfloat16),
        pltpu.VMEM((rows, 128), jnp.float32),
        pltpu.VMEM((rows, width), jnp.float32),
        pltpu.VMEM((rows, width), jnp.float32),
    ] + [pltpu.VMEM((3, hidden, width), jnp.float32)] * (parts - 1)
    found = pl.pallas_call(
        functools.partial(expert_kernel, parts, per_step, cap),
        grid=(ep_count // per_step,),
        in_specs=in_specs,
        out_specs=[token_spec, token_spec] + [grad_spec] * parts,
        out_shape=out_shape,
        scratch_shapes=scratch,
        compiler_params=pltpu.CompilerParams(
            dimension_semantics=("arbitrary",), vmem_limit_bytes=VMEM_MOST
        ),
        cost_estimate=pl.CostEstimate(
            flops=18 * ep_count * cap * parts * hidden * width,
            bytes_accessed=8 * ep_count * tok * width + 30 * parts * hidden * width,
            transcendentals=ep_count * cap * parts * hidden,
        ),
        name="expert_pass",
    )(normed_all, cot_all, info, *ins, *outs_w)
    return found[0], found[1], found[2], found[3:]


def adam_rows(source, target, grad, clip, rate, decay):
    weight, first, second = source
    clipped = grad * clip
    first_new = BETA_ONE * first + (1.0 - BETA_ONE) * clipped
    second_new = BETA_TWO * second + (1.0 - BETA_TWO) * clipped * clipped
    corr_one = 1.0 - BETA_ONE**STEP
    corr_two = 1.0 - BETA_TWO**STEP
    stepped = first_new * (1.0 / corr_one) / (jnp.sqrt(second_new * (1.0 / corr_two)) + ADAM_EPS)
    weight_new = weight - rate * (stepped + decay * weight)
    refs, window = target
    for ref, value in zip(refs, (weight_new, first_new, second_new, weight_new)):
        ref[window] = value.astype(ref.dtype)


def adam_kernel(first_blocks, dense_blocks, *refs):
    dense = len(dense_blocks)
    norm, grads = refs[:2]
    inside, outside = refs[2:5], refs[5:8]
    refs = refs[8:]
    dense_in, refs = refs[: 4 * dense], refs[4 * dense :]
    inside_new, outside_new, dense_new = refs[:4], refs[4:8], refs[8:]
    at = pl.program_id(0)
    clip = jnp.minimum(1.0, CLIP_LEVEL / (norm[0:1, 0:1] + 1e-06))

    def block(source, target):
        def rows(i, carry):
            window = (pl.ds(pl.multiple_of(i * 16, 16), 16), slice(None))
            values = [ref[window] for ref in source]
            adam_rows(values, (target, window), grads[window], clip, MATRIX_RATE, WEIGHT_DECAY)
            return carry

        lax.fori_loop(0, grads.shape[0] // 16, rows, 0)

    pl.when(at < first_blocks)(lambda: block(inside, inside_new))
    pl.when(at >= first_blocks)(lambda: block(outside, outside_new))

    def one(k):
        source, grad = dense_in[4 * k : 4 * k + 3], dense_in[4 * k + 3]
        rows, width = source[0].shape
        last = k == dense - 1
        everything = (slice(None), slice(None))
        adam_rows(
            [ref[...] for ref in source],
            (dense_new[4 * k : 4 * k + 4], everything),
            grad[:rows, :width],
            clip,
            GAIN_RATE if last else MATRIX_RATE,
            0.0 if last else WEIGHT_DECAY,
        )

    for k, count in enumerate(dense_blocks):
        pl.when(at < count)(functools.partial(one, k))


def adam_all(norm, grads, inside, outside, dense):
    hidden, width = grads.shape[1:]
    rows = hidden // 4 if hidden % 64 == 0 else hidden // 2
    inner = 2 * hidden // rows
    steps = 3 * hidden // rows

    def blocks_of(columns):
        return max(n for n in range(1, steps + 1) if columns % (128 * n) == 0 or n == 1)

    counts = tuple(blocks_of(entry[0].shape[1]) for entry in dense)

    def slab(array, count):
        columns = array.shape[1] // count
        return pl.BlockSpec((array.shape[0], columns), lambda i: (0, jnp.minimum(i, count - 1)))

    first_spec = pl.BlockSpec((rows, width), lambda i: (jnp.minimum(i, inner - 1), 0))
    second_spec = pl.BlockSpec((rows, width), lambda i: (jnp.maximum(i - inner, 0), 0))
    flat = [a.reshape(2 * hidden, width) for a in inside] + [a.reshape(hidden, width) for a in outside]
    low, full = jnp.bfloat16, jnp.float32
    kinds = (full, full, full, low)
    out_shape = [jax.ShapeDtypeStruct((2 * hidden, width), kind) for kind in kinds]
    out_shape += [jax.ShapeDtypeStruct((hidden, width), kind) for kind in kinds]
    out_specs = [first_spec] * 4 + [second_spec] * 4
    in_specs = [pl.BlockSpec(norm.shape, lambda i: (0, 0)), pl.BlockSpec((rows, width), lambda i: (i, 0))]
    in_specs += [first_spec] * 3 + [second_spec] * 3
    more = []
    for entry, count in zip(dense, counts):
        more += entry
        in_specs += [slab(array, count) for array in entry]
        out_specs += [slab(entry[0], count)] * 4
        out_shape += [jax.ShapeDtypeStruct(entry[0].shape, kind) for kind in kinds]
    found = pl.pallas_call(
        functools.partial(adam_kernel, inner, counts),
        grid=(steps,),
        in_specs=in_specs,
        out_specs=out_specs,
        out_shape=out_shape,
        compiler_params=pltpu.CompilerParams(
            dimension_semantics=("arbitrary",), vmem_limit_bytes=VMEM_MOST
        ),
        name="adam",
    )(norm, grads.reshape(3 * hidden, width), *flat, *more)
    first = [a.reshape(inside[0].shape) for a in found[:4]]
    second = [a.reshape(outside[0].shape) for a in found[4:8]]
    return first, second, [found[8 + 4 * k : 12 + 4 * k] for k in range(len(dense))]


FROM_A = {1: (1, 0), 2: (2, 1), 3: (4, 1)}
FROM_B = {0: (0, 2), 1: (2, 1), 2: (4, 1), 3: (6, 0)}
TO_B = {1: (6, 1), 2: (5, 2), 3: (7, 2)}
TO_A = {2: (6, 2)}


def nearest(place):
    count = place.na
    table = [sorted(range(count), key=lambda other: abs(other - own)) for own in range(count)]

    def chip_at(r):
        found = jnp.int32(0)
        for own in range(count):
            for rank in range(count):
                found = found + jnp.where((place.a == own) & (r == rank), table[own][rank], 0)
        return found

    return chip_at


def fused_kernel(parts, ep_count, tp_count, cap, *refs):
    normed, info, cot = refs[:3]
    w_in, w_out = refs[3 : 3 + parts], refs[3 + parts : 3 + 2 * parts]
    refs = refs[3 + 2 * parts :]
    result_ref, routed_ref, own_grad = refs[:3]
    sent = refs[3 : 2 + parts]
    scratch = refs[2 + parts :]
    tok, infos, cots, vin, vout, own, sib, sib_stage, bland, aland, res_stage = scratch[:11]
    rows_x, rows_g, gate_col, result_acc, input_acc, stage = scratch[11:17]
    sums = (own_grad,) + tuple(scratch[17 : 16 + parts])
    (tok_recv, tok_send, local_sem, cot_sem, sib_recv, sib_send, b_recv, b_send, a_recv, a_send,
     res_sem, stage_sem) = scratch[16 + parts :]
    place = Place(ep_count, tp_count)
    na, a, b, core = place.na, place.a, place.b, place.core
    width = normed.shape[1]
    me = (a * 2 + b) * 2 + core
    chip_at = nearest(place)
    chunk = 256

    def device(a_, b_, core_):
        return ((a_ * 2 + b_) * 2 + core_, place.t)

    sibling, across = device(a, b, 1 - core), device(a, 1 - b, core)
    barrier = pltpu.get_barrier_semaphore()
    for target in (sibling, across):
        pl.semaphore_signal(barrier, inc=1, device_id=target, device_id_type=MESH)
    for step in range(1, na):
        pl.semaphore_signal(
            barrier, inc=1, device_id=device(lax.rem(a + step, na), b, core), device_id_type=MESH
        )
    pl.semaphore_wait(barrier, na + 1)

    def hop(index, number, target, first=False):
        return [
            pltpu.make_async_remote_copy(
                src_ref=own_block if first else held.at[index],
                dst_ref=held.at[index],
                send_sem=tok_send.at[k, number],
                recv_sem=tok_recv.at[k, index],
                device_id=target,
                device_id_type=MESH,
            )
            for k, (own_block, held) in enumerate(((normed, tok), (info, infos)))
        ]

    def start(copies):
        for copy in copies:
            copy.start()

    def arrived(index):
        for k, held in enumerate((tok, infos)):
            pltpu.make_async_copy(held.at[index], held.at[index], tok_recv.at[k, index]).wait()

    ends = []

    def launch(on, copies):
        def finish():
            for copy in copies:
                copy.wait_send()

        guarded(on, lambda: start(copies))
        ends.append((on, finish))

    up, down_ok = a + 1 < na, a > 0
    launch(up, hop(me, 0, device(a + 1, b, core), True))
    launch(down_ok, hop(me, 1, device(a - 1, b, core), True))
    launch(None, hop(me, 2, across, True))
    launch(None, hop(me, 3, sibling, True))
    loads = [pltpu.make_async_copy(normed, tok.at[me], local_sem.at[0])]
    loads.append(pltpu.make_async_copy(info, infos.at[me], local_sem.at[1]))
    for p in range(parts):
        loads.append(pltpu.make_async_copy(w_in[p], vin.at[p], local_sem.at[2 + 2 * p]))
        loads.append(pltpu.make_async_copy(w_out[p], vout.at[p], local_sem.at[3 + 2 * p]))
    start(loads)

    def chip_of(k):
        near = (lax.rem(k, 2) == 0) == (k < 2 * na - 2)
        return chip_at(k // 2) * 2 + jnp.where(near, b, 1 - b)

    def cot_copies(k):
        chip, buffer = chip_of(k), lax.rem(k, 2)
        return [
            pltpu.make_async_copy(cot.at[chip * 2 + j], cots.at[buffer, j], cot_sem.at[buffer, j])
            for j in range(2)
        ]

    start(cot_copies(jnp.int32(0)))
    for total in sums:
        total[...] = jnp.zeros_like(total)
    for load in loads:
        load.wait()

    def from_a(r):
        other = chip_at(r)
        index = (other * 2 + b) * 2 + core
        arrived(index)
        first = 4 + 3 * (r - 1)
        beyond = jnp.where(other > a, a - 1, a + 1)
        on = (beyond >= 0) & (beyond < na)
        copies = hop(index, first, device(beyond, b, core))
        pl.when(on)(lambda: start(copies))
        start(hop(index, first + 1, across))
        start(hop(index, first + 2, sibling))

    def from_b(r):
        index = (chip_at(r) * 2 + 1 - b) * 2 + core
        arrived(index)
        start(hop(index, 4 + 3 * (na - 1) + r, sibling))

    def sent_from_a(r):
        other = chip_at(r)
        index = (other * 2 + b) * 2 + core
        first = 4 + 3 * (r - 1)
        beyond = jnp.where(other > a, a - 1, a + 1)
        on = (beyond >= 0) & (beyond < na)

        def finish(number):
            for copy in hop(index, number, sibling):
                copy.wait_send()

        pl.when(on)(lambda: finish(first))
        finish(first + 1)
        finish(first + 2)

    def sib_wait(chip):
        pltpu.make_async_copy(sib.at[chip], sib.at[chip], sib_recv.at[chip]).wait()

    def to_b(r):
        chip = chip_at(r) * 2 + 1 - b
        sib_wait(chip)
        add_into(own.at[chip], [own.at[chip], sib.at[chip]], own.dtype)
        pltpu.make_async_remote_copy(
            src_ref=own.at[chip],
            dst_ref=bland.at[r],
            send_sem=b_send.at[r],
            recv_sem=b_recv.at[r],
            device_id=across,
            device_id_type=MESH,
        ).start()

    def b_wait(r):
        pltpu.make_async_copy(bland.at[r], bland.at[r], b_recv.at[r]).wait()

    def to_a(r):
        other = chip_at(r)
        chip = other * 2 + b
        sib_wait(chip)
        b_wait(r)
        add_into(own.at[chip], [own.at[chip], sib.at[chip], bland.at[r]], own.dtype)
        pltpu.make_async_remote_copy(
            src_ref=own.at[chip],
            dst_ref=aland.at[a],
            send_sem=a_send.at[r],
            recv_sem=a_recv.at[a],
            device_id=device(other, b, core),
            device_id_type=MESH,
        ).start()

    over_last = (((1,), (1,)), ((), ()))
    over_first = (((0,), (0,)), ((), ()))
    straight = (((1,), (0,)), ((), ()))

    def mul(left, right, dims):
        return lax.dot_general(left, right, dims, preferred_element_type=jnp.float32)

    slots = lax.broadcasted_iota(jnp.int32, (cap, normed.shape[0]), 0).astype(jnp.float32)

    def picks_of(source):
        return slots == infos[source, pl.ds(me, 1), :]

    def turn(k, phase):
        for r in range(1, na):
            for far, spot in FROM_A.items():
                if spot[1] == phase and (r + 1) // 2 <= far <= r:
                    on = (k == spot[0]) & (jnp.abs(chip_at(r) - a) == far)
                    pl.when(on)(functools.partial(from_a, r))
        for act, spots in ((from_b, FROM_B), (to_b, TO_B), (to_a, TO_A)):
            for r, spot in spots.items():
                if spot[1] == phase:
                    pl.when(k == spot[0])(functools.partial(act, r))

    def work(k, carry):
        chip, buffer = chip_of(k), lax.rem(k, 2)

        @pl.when(k + 1 < 2 * na)
        def _():
            start(cot_copies(k + 1))

        turn(k, 0)
        arrived(chip * 2 + 1 - core)
        for copy in cot_copies(k):
            copy.wait()
        for j in range(2):
            hit = picks_of(chip * 2 + j)
            picks = jnp.where(hit, 1.0, 0.0).astype(jnp.bfloat16)
            gate_row = infos[chip * 2 + j, pl.ds(ep_count + me, 1), :]
            gates = jnp.sum(jnp.where(hit, gate_row, 0.0), axis=1, keepdims=True)
            window = pl.ds(j * cap, cap)
            gate_col[window, :] = jnp.broadcast_to(gates, (cap, 128))
            rows_x[window, :] = mul(picks, tok[chip * 2 + j], straight).astype(jnp.bfloat16)
            taken = mul(picks, cots[buffer, j], straight)
            rows_g[window, :] = (gates * taken).astype(jnp.bfloat16)
        for p in range(parts):
            gate_pre = mul(rows_x[...], vin[p, 0], over_last)
            up_pre = mul(rows_x[...], vin[p, 1], over_last)
            sigmoid = jax.nn.sigmoid(gate_pre)
            active = (gate_pre * sigmoid * up_pre).astype(jnp.bfloat16)
            grad_act = mul(rows_g[...], vout[p], over_last)
            grad_up = (grad_act * gate_pre * sigmoid).astype(jnp.bfloat16)
            grad_gate = (
                grad_act * up_pre * sigmoid * (1.0 + gate_pre * (1.0 - sigmoid))
            ).astype(jnp.bfloat16)
            for first in range(0, width, chunk):
                window = slice(first, first + chunk)
                result = mul(active, vout[p, :, window], straight)
                back = mul(grad_gate, vin[p, 0, :, window], straight) + mul(
                    grad_up, vin[p, 1, :, window], straight
                )
                if p == 0:
                    result_acc[:, window] = result
                    input_acc[:, window] = back
                else:
                    result_acc[:, window] += result
                    input_acc[:, window] += back
                sums[p][0, :, window] += mul(grad_gate, rows_x[:, window], over_first)
                sums[p][1, :, window] += mul(grad_up, rows_x[:, window], over_first)
                sums[p][2, :, window] += mul(active, rows_g[:, window], over_first)
            if p == 0:
                turn(k, 1)

        @pl.when(k > 0)
        def _():
            pltpu.make_async_copy(sib_stage, sib_stage, sib_send.at[0]).wait()
            for j in range(2):
                pltpu.make_async_copy(res_stage.at[j], res_stage.at[j], res_sem.at[j]).wait()

        for other in range(2):
            j = 1 - core if other == 0 else core
            source = chip * 2 + j
            picks = jnp.where(picks_of(source), 1.0, 0.0).astype(jnp.bfloat16)
            window = pl.ds(pl.multiple_of(j * cap, cap), cap)
            back = mul(picks, input_acc[window, :].astype(jnp.bfloat16), over_first)
            if other == 0:
                sib_stage[...] = back.astype(jnp.bfloat16)
                pltpu.make_async_remote_copy(
                    src_ref=sib_stage,
                    dst_ref=sib.at[chip],
                    send_sem=sib_send.at[0],
                    recv_sem=sib_recv.at[chip],
                    device_id=sibling,
                    device_id_type=MESH,
                ).start()
            else:
                own[chip] = back.astype(jnp.bfloat16)
            rounded = result_acc[window, :].astype(jnp.bfloat16).astype(jnp.float32)
            weighted = (gate_col[window, 0:1] * rounded).astype(jnp.bfloat16)
            res_stage[other] = mul(picks, weighted, over_first).astype(jnp.bfloat16)
            pltpu.make_async_copy(res_stage.at[other], result_ref.at[source], res_sem.at[other]).start()
        turn(k, 2)
        return carry

    lax.fori_loop(0, 2 * na, work, 0)
    to_a(1)
    to_b(0)
    for p in range(1, parts):
        for q in range(3):
            if p > 1 or q > 0:
                pltpu.make_async_copy(stage, stage, stage_sem.at[0]).wait()
            stage[...] = sums[p][q].astype(jnp.bfloat16)
            pltpu.make_async_copy(stage, sent[p - 1].at[q], stage_sem.at[0]).start()
    to_a(3)
    chip = a * 2 + b
    sib_wait(chip)
    b_wait(0)
    add_into(routed_ref, [own.at[chip], sib.at[chip], bland.at[0]], jnp.float32)
    for r in range(1, na):
        other = chip_at(r)
        pltpu.make_async_copy(aland.at[other], aland.at[other], a_recv.at[other]).wait()
        add_into(routed_ref, [routed_ref, aland.at[other]], jnp.float32)
    for on, finish in ends:
        guarded(on, finish)
    for r in range(na):
        if r:
            sent_from_a(r)
            pltpu.make_async_copy(own.at[0], own.at[0], a_send.at[r]).wait()
        for copy in hop(me, 4 + 3 * (na - 1) + r, sibling):
            copy.wait_send()
        pltpu.make_async_copy(own.at[0], own.at[0], b_send.at[r]).wait()
    pltpu.make_async_copy(sib_stage, sib_stage, sib_send.at[0]).wait()
    for j in range(2):
        pltpu.make_async_copy(res_stage.at[j], res_stage.at[j], res_sem.at[j]).wait()
    pltpu.make_async_copy(stage, stage, stage_sem.at[0]).wait()


def fused_experts(ep_count, tp_count, collective_id, normed, info, cot_all, ins, outs_w, cap):
    place = Place(ep_count, tp_count)
    tok, width = normed.shape
    parts = len(ins)
    hidden = ins[0].shape[1]
    na, chips, rows = place.na, 2 * place.na, 2 * cap
    low = jnp.bfloat16
    anywhere = pl.BlockSpec(memory_space=pl.ANY)
    inside = pl.BlockSpec(memory_space=pltpu.VMEM)
    out_shape = [
        jax.ShapeDtypeStruct((ep_count, tok, width), low),
        jax.ShapeDtypeStruct((tok, width), jnp.float32),
        jax.ShapeDtypeStruct((3, hidden, width), jnp.float32),
    ] + [jax.ShapeDtypeStruct((3, hidden, width), low)] * (parts - 1)
    scratch = [
        pltpu.VMEM((ep_count, tok, width), low),
        pltpu.VMEM((ep_count, 2 * ep_count, tok), jnp.float32),
        pltpu.VMEM((2, 2, tok, width), low),
        pltpu.VMEM((parts, 2, hidden, width), low),
        pltpu.VMEM((parts, hidden, width), low),
        pltpu.VMEM((chips, tok, width), low),
        pltpu.VMEM((chips, tok, width), low),
        pltpu.VMEM((tok, width), low),
        pltpu.VMEM((na, tok, width), low),
        pltpu.VMEM((na, tok, width), low),
        pltpu.VMEM((2, tok, width), low),
        pltpu.VMEM((rows, width), low),
        pltpu.VMEM((rows, width), low),
        pltpu.VMEM((rows, 128), jnp.float32),
        pltpu.VMEM((rows, width), jnp.float32),
        pltpu.VMEM((rows, width), jnp.float32),
        pltpu.VMEM((hidden, width), low),
    ] + [pltpu.VMEM((3, hidden, width), jnp.float32)] * (parts - 1)
    dma = pltpu.SemaphoreType.DMA
    scratch += [
        dma((2, ep_count)), dma((2, 4 + 3 * (na - 1) + na)), dma((2 + 2 * parts,)), dma((2, 2)),
        dma((chips,)), dma((1,)), dma((na,)), dma((na,)), dma((na,)), dma((na,)), dma((2,)), dma((1,)),
    ]
    found = pl.pallas_call(
        functools.partial(fused_kernel, parts, ep_count, tp_count, cap),
        in_specs=[anywhere] * (3 + 2 * parts),
        out_specs=[anywhere, inside, inside] + [anywhere] * (parts - 1),
        out_shape=out_shape,
        scratch_shapes=scratch,
        compiler_params=pltpu.CompilerParams(
            collective_id=collective_id, has_side_effects=True, vmem_limit_bytes=VMEM_MOST
        ),
        name="fused_experts",
    )(normed, info, cot_all, *ins, *outs_w)
    return found[0], found[1], found[2], found[3:]


def per_device(
    tokens,
    cotangent,
    segments,
    routes,
    gates,
    qkv_weight,
    qkv_first,
    qkv_second,
    out_weight,
    out_first,
    out_second,
    shared_in,
    shared_in_first,
    shared_in_second,
    shared_out,
    shared_out_first,
    shared_out_second,
    expert_in,
    expert_in_first,
    expert_in_second,
    expert_out,
    expert_out_first,
    expert_out_second,
    norm_gains,
    gains_first,
    gains_second,
):
    tok_count = tokens.shape[0]
    width = tokens.shape[1]
    ep_count = lax.axis_size("ep")
    tp_count = lax.axis_size("tp")
    devices = ep_count * tp_count
    capacity = tok_count * 8 // ep_count
    low = jnp.bfloat16
    in_own, out_own = expert_in[0].astype(low), expert_out[0].astype(low)
    gain_columns = jnp.pad(norm_gains.T.astype(low), ((0, 0), (0, 126)))
    group = shared_out.shape[0]
    step = 16 * ((group + 15) // 16)
    while step & (step - 1):
        step += 16
    shout_own = jnp.pad(shared_out.astype(low), ((0, step - group), (0, 0)))
    qkv_low, out_low, gains_low, cot_all, in_others, out_others, shin_low, shout_low = gather(
        ep_count,
        tp_count,
        1,
        "gather_weights",
        [
            (("tab", "abt"), [qkv_weight.astype(low), out_weight.astype(low), gain_columns], 1.0),
            (("ab", "ba"), [cotangent], 0.92),
            ("t", [in_own, out_own], 1.0),
            (("tab", "atb"), [shared_in.astype(low), shout_own], 2.9),
        ],
    )
    qkv_low = qkv_low.reshape(width, 3 * width)
    out_low = out_low.reshape(width, width)
    shin_low = shin_low.reshape(width, 2 * FF)
    shout_low = shout_low.reshape(devices * step, width)
    gains = jnp.pad(gains_low.reshape(width, 128)[:, :2].T.astype(jnp.float32), ((0, 6), (0, 0)))
    ins_low = [in_own] + [in_others[s] for s in range(tp_count - 1)]
    outs_low = [out_own] + [out_others[s] for s in range(tp_count - 1)]
    expert_ids = jnp.arange(ep_count, dtype=jnp.int32)
    chosen = routes[:, :, None] == expert_ids[None, None, :]
    onehot = jnp.sum(chosen.astype(jnp.float32), axis=1)
    gate_of = jnp.sum(jnp.where(chosen, gates[:, :, None], 0.0), axis=1)
    earlier = jnp.tril(jnp.ones((tok_count, tok_count), low), -1)
    rank = jnp.dot(earlier, onehot.astype(low), preferred_element_type=jnp.float32)
    slot_of = jnp.where(onehot > 0.0, rank, -1.0)
    info_own = jnp.concatenate([slot_of, gate_of], axis=1).T
    qkv_act, attended, hidden, normed_two = attention_forward(
        tokens, segments, gains, qkv_low, out_low
    )
    chips = ep_count // 2
    held = tok_count * width * 2 * (ep_count + 3 * chips + 12) + 9 * tp_count * expert_in.size
    place = Place(ep_count, tp_count)
    if (place.na, place.nb) == (4, 2) and held <= VMEM_MOST * 9 // 10:
        result_part, routed_grad, own_grad, sent_grads = fused_experts(
            ep_count, tp_count, 3, normed_two, info_own, cot_all, ins_low, outs_low, capacity
        )
    else:
        normed_all, info_all = gather(
            ep_count, tp_count, 2, "gather_tokens", [("ab", [normed_two, info_own], 1.0)]
        )
        info = lax.dynamic_index_in_dim(
            info_all.reshape(ep_count, 2, ep_count, tok_count),
            lax.axis_index("ep"),
            axis=2,
            keepdims=False,
        )
        result_part, input_part, own_grad, sent_grads = expert_pass(
            normed_all, cot_all, info, ins_low, outs_low, capacity
        )
        (routed_grad,) = scatter_add(ep_count, tp_count, 3, "scatter_inputs", [("ab", [input_part])])
    sent = jnp.stack(sent_grads)
    lean = scatter_room(Place(ep_count, tp_count), "ab", [result_part]) <= VMEM_MOST // 3
    base, tokens_grad, gain_grads, qkv_grad, out_grad, shin_grad, shout_grad, *carried = dense_backward(
        group, step, tokens, cotangent, segments, gains, qkv_act, attended, hidden, normed_two,
        routed_grad, qkv_low, out_low, shin_low, shout_low, ep_count, tp_count, 9, "ab",
        result_part if lean else None, sent,
    )
    own_gains = norm_gains.shape[1]
    gain_rows = gain_grads[:2].astype(low).reshape(2, devices, own_gains).transpose(1, 0, 2)
    gain_rows = jnp.pad(gain_rows, ((0, 0), (0, 14), (0, 128 - own_gains)))

    def by_owner(grad):
        return grad.reshape(devices, -1, grad.shape[1])

    scattered = [
        (("abt", "tab"), [by_owner(qkv_grad), by_owner(out_grad), gain_rows]),
        (("abt", "bta"), [by_owner(shin_grad), by_owner(shout_grad)]),
    ]
    if lean:
        routed, others = carried
        qkv_part, out_part, gains_part, shin_part, shout_part, own_grad, norm = scatter_add(
            ep_count, tp_count, 4, "scatter_weights", scattered, (own_grad, others)
        )
    else:
        scattered += [("ab", [result_part]), ("t", [sent])]
        qkv_part, out_part, gains_part, shin_part, shout_part, routed, others = scatter_all(
            ep_count, tp_count, (4, 6, 7, 8), "scatter_weights", scattered
        )
        for shift in range(tp_count - 1):
            own_grad = own_grad + others[shift].astype(jnp.float32)
        extra = jnp.sum(own_grad * own_grad, axis=(0, 1))[None, :]
        norm = sum_of_squares(
            ep_count, tp_count, 5, [qkv_part, out_part, gains_part, shin_part, shout_part], extra
        )
        norm = jnp.broadcast_to(jnp.sqrt(norm), (8, 128))
    grad_norm = norm[0, 0]
    block_out = (base + routed).astype(low)
    exin, exout, dense = adam_all(
        norm,
        own_grad,
        (expert_in, expert_in_first, expert_in_second),
        (expert_out, expert_out_first, expert_out_second),
        [
            (qkv_weight, qkv_first, qkv_second, qkv_part),
            (out_weight, out_first, out_second, out_part),
            (shared_in, shared_in_first, shared_in_second, shin_part),
            (shared_out, shared_out_first, shared_out_second, shout_part),
            (norm_gains, gains_first, gains_second, gains_part),
        ],
    )
    qkv_all, out_all, shin_all, shout_all, gains_all = dense
    return (
        block_out, tokens_grad, grad_norm, *qkv_all, *out_all, *shin_all, *shout_all, *exin, *exout, *gains_all
    )


def solution(mesh):
    placed = (
        P(("ep", "tp"), None),
        P(("ep", "tp"), None),
        P(("ep", "tp"), None),
        P(("ep", "tp"), None),
        P(("ep", "tp"), None),
        P(("ep", "tp"), None),
        P(("ep", "tp"), None),
        P(("ep", "tp"), None),
        P(("ep", "tp"), None),
        P(("ep", "tp"), None),
        P(("ep", "tp"), None),
        P(("ep", "tp"), None),
        P(("ep", "tp"), None),
        P(("ep", "tp"), None),
        P(("ep", "tp"), None),
        P(("ep", "tp"), None),
        P(("ep", "tp"), None),
        P("ep", None, "tp", None),
        P("ep", None, "tp", None),
        P("ep", None, "tp", None),
        P("ep", "tp", None),
        P("ep", "tp", None),
        P("ep", "tp", None),
        P(None, ("ep", "tp")),
        P(None, ("ep", "tp")),
        P(None, ("ep", "tp")),
    )
    return jax.shard_map(
        per_device,
        mesh=mesh,
        in_specs=placed,
        out_specs=(
            P(("ep", "tp"), None),
            P(("ep", "tp"), None),
            P(),
            P(("ep", "tp"), None),
            P(("ep", "tp"), None),
            P(("ep", "tp"), None),
            P(("ep", "tp"), None),
            P(("ep", "tp"), None),
            P(("ep", "tp"), None),
            P(("ep", "tp"), None),
            P(("ep", "tp"), None),
            P(("ep", "tp"), None),
            P(("ep", "tp"), None),
            P(("ep", "tp"), None),
            P(("ep", "tp"), None),
            P(("ep", "tp"), None),
            P(("ep", "tp"), None),
            P(("ep", "tp"), None),
            P(("ep", "tp"), None),
            P("ep", None, "tp", None),
            P("ep", None, "tp", None),
            P("ep", None, "tp", None),
            P("ep", None, "tp", None),
            P("ep", "tp", None),
            P("ep", "tp", None),
            P("ep", "tp", None),
            P("ep", "tp", None),
            P(None, ("ep", "tp")),
            P(None, ("ep", "tp")),
            P(None, ("ep", "tp")),
            P(None, ("ep", "tp")),
        ),
        check_vma=False,
    )
```

```python
import functools
import jax
import jax.numpy as jnp
import numpy as np
from jax import lax
from jax.experimental import pallas as pl
from jax.experimental.pallas import tpu as pltpu
from jax.sharding import PartitionSpec as P

HEADS = 10
HDIM = 128
FF = 896
TOPK = 7
STEP = 10


MESH = pl.DeviceIdType.MESH
VMEM_MOST = 60 * 1024 * 1024
NEG_BIG = -1000000000.0
NORM_EPS = 1e-06
ROPE_BASE = 10000.0
CLIP_LEVEL = 1.0
BETA_ONE = 0.9
BETA_TWO = 0.95
ADAM_EPS = 1e-08
WEIGHT_DECAY = 0.1
MATRIX_RATE = 0.05
GAIN_RATE = 0.5


class Place:
    def __init__(self, ep_count, tp_count):
        chips = ep_count // 2
        nb = 1
        while nb * nb * 4 <= chips:
            nb *= 2
        self.nb, self.na, self.nt = nb, chips // nb, tp_count
        self.ep_count = ep_count
        self.wrap = chips * tp_count >= 64
        e = lax.axis_index("ep")
        self.t = lax.axis_index("tp")
        self.core = lax.rem(e, 2)
        self.b = lax.rem(e // 2, nb)
        self.a = e // (2 * nb)

    def dims(self, order):
        if "u" in order and self.nb != self.nt:
            order = "abt"
        extents = {"a": self.na, "b": self.nb, "t": self.nt, "u": self.nb, "v": self.nt}
        return tuple((name, shifts(extents[name], self.wrap)) for name in order)

    def extent(self, name):
        return {"a": self.na, "b": self.nb, "t": self.nt, "u": self.nb, "v": self.nt}[name]

    def moved(self, name, shift):
        own, extent = self.own(name), self.extent(name)
        if shift == 0:
            return own, None
        if extent == 2:
            return 1 - own, None
        if self.wrap:
            return lax.rem(own + shift + extent, extent), None
        there = own + shift
        return there, (there >= 0) & (there < extent)

    def own(self, name):
        even = self.core == 0
        if name == "u":
            return jnp.where(even, self.b, self.t)
        if name == "v":
            return jnp.where(even, self.t, self.b)
        return getattr(self, name)

    def chip(self, at):
        a = at.get("a", self.a)
        b, t = at.get("b", self.b), at.get("t", self.t)
        if "u" in at:
            even = self.core == 0
            b = jnp.where(even, at["u"], at["v"])
            t = jnp.where(even, at["v"], at["u"])
        return a, b, t

    def device(self, at, core):
        a, b, t = self.chip(at)
        return ((a * self.nb + b) * 2 + core, t)

    def index(self, at, core, whole):
        e, t = self.device(at, core)
        return e * self.nt + t if whole else e

    def slot(self, at, whole):
        a, b, t = self.chip(at)
        chip = a * self.nb + b
        return chip * self.nt + t if whole else chip


def shifts(extent, wrap):
    if extent == 1:
        return (0,)
    if extent == 2:
        return (0, 1)
    found = [0]
    for step in range(1, extent // 2 + 1 if wrap else extent):
        found += [step, -step]
    return tuple(found[:extent] if wrap else found)


def ways(spread):
    return (1,) if len(spread) == 2 else (1, -1) if len(spread) > 2 else ()


def onward(spread, shift):
    way = -1 if shift > 0 else 1
    return way if len(spread) > 2 and shift - way in spread else 0


def both(one, other):
    if one is None:
        return other
    return one if other is None else one & other


def guarded(condition, body):
    if condition is None:
        body()
    else:
        pl.when(condition)(body)


def greet(place, order):
    barrier = pltpu.get_barrier_semaphore()
    here = {name: place.own(name) for name, _ in place.dims(order)}
    pl.semaphore_signal(barrier, inc=1, device_id=place.device(here, 1 - place.core), device_id_type=MESH)
    count = jnp.int32(1)
    for name, spread in place.dims(order):
        for way in ways(spread):
            there, on = place.moved(name, way)
            target = place.device({**here, name: there}, place.core)

            def signal(target=target):
                pl.semaphore_signal(barrier, inc=1, device_id=target, device_id_type=MESH)

            guarded(on, signal)
            count = count + (1 if on is None else on.astype(jnp.int32))
    if len(order) > 2:
        for s in range(2, place.nt - 1):
            target = place.device({"t": lax.rem(place.t + s, place.nt)}, place.core)
            pl.semaphore_signal(barrier, inc=1, device_id=target, device_id_type=MESH)
            count = count + 1
    pl.semaphore_wait(barrier, count)


def relative_blocks(dims):
    blocks = [()]
    for _, spread in dims:
        blocks = [block + (shift,) for block in blocks for shift in spread]
    return blocks


def by_core(place, order):
    if isinstance(order, str):
        return [(order, None)]
    return [(order[core], place.core == core) for core in range(2)]


def longest(groups):
    return max((order if isinstance(order, str) else order[0] for order, _ in groups), key=len)


def gather_events(place, order, only, pairs, send_sems, recv_sems):
    dims = place.dims(order)
    whole = len(dims) > 2
    here = {name: place.own(name) for name, _ in dims}
    counter = [0]
    ends = []

    def copies(at, target, core_of_block, own):
        index = place.index(at, core_of_block, whole)
        number = counter[0]
        counter[0] += 1
        made = []
        for k, (block, gathered) in enumerate(pairs):
            made.append(
                pltpu.make_async_remote_copy(
                    src_ref=block if own else gathered.at[index],
                    dst_ref=gathered.at[index],
                    send_sem=send_sems.at[k, number],
                    recv_sem=recv_sems.at[k, index],
                    device_id=target,
                    device_id_type=MESH,
                )
            )
        return made

    def send(at, on, target, own, todo):
        made = copies(at, target, place.core, own)

        def start(made=made):
            for copy in made:
                copy.start()

        def finish(made=made):
            for copy in made:
                copy.wait_send()

        todo.append((on, start))
        ends.append((on, finish))

    steps = []
    times = arrival_times(dims)
    for block in relative_blocks(dims):
        at, valid = dict(here), only
        for (name, _), shift in zip(dims, block):
            at[name], on = place.moved(name, shift)
            valid = both(valid, on)
        last = max([k for k, shift in enumerate(block) if shift], default=-1)
        own = last < 0
        todo = []
        for k in range(len(dims) - 1, -1, -1):
            name, spread = dims[k]
            if k < last:
                continue
            if k == last:
                way = onward(spread, block[k])
                sent = [way] if way else []
            else:
                sent = ways(spread)
            for way in sent:
                there, on = place.moved(name, way)
                target = place.device({**here, name: there}, place.core)
                send(at, both(valid, on), target, own, todo)
        send(at, valid, place.device(here, 1 - place.core), own, todo)
        index = place.index(at, place.core, whole)

        def step(index=index, valid=valid, todo=todo, own=own):
            def body():
                if not own:
                    for k, (_, gathered) in enumerate(pairs):
                        pltpu.make_async_copy(gathered.at[index], gathered.at[index], recv_sems.at[k, index]).wait()

            guarded(valid, body)
            for on, start in todo:
                guarded(on, start)

        steps.append((times[block], step))
        other = place.index(at, 1 - place.core, whole)

        def arrived(other=other):
            for k, (_, gathered) in enumerate(pairs):
                pltpu.make_async_copy(gathered.at[other], gathered.at[other], recv_sems.at[k, other]).wait()

        ends.append((valid, arrived))
    return steps, ends, counter[0]


def arrival_times(dims):
    times = {(): 0}
    for _, spread in dims:
        earlier = sorted(times, key=lambda block: times[block])
        found = {block + (0,): times[block] for block in earlier}
        for shift in spread:
            for i, block in enumerate(earlier):
                if shift:
                    far = abs(shift)
                    found[block + (shift,)] = max(times[block] + far, (far - 1) * len(earlier) + i + 1)
        times = found
    return times


def count_gather_sends(dims):
    total = 0
    for block in relative_blocks(dims):
        last = max([k for k, shift in enumerate(block) if shift], default=-1)
        for k, (_, spread) in enumerate(dims):
            if k > last:
                total += len(ways(spread))
            elif k == last and onward(spread, block[k]):
                total += 1
        total += 1
    return total


def exchange_copies(place, blocks, others, send_sems, recv_sems):
    copies = []
    for s in range(1, place.nt):
        back = blocks[0].shape == others[0].shape
        there = lax.rem(place.t + (s if back else place.nt - s), place.nt)
        target = place.device({"t": there}, place.core)
        for k, (block, other) in enumerate(zip(blocks, others)):
            copies.append(
                pltpu.make_async_remote_copy(
                    src_ref=block.at[s - 1] if back else block,
                    dst_ref=other.at[s - 1],
                    send_sem=send_sems.at[k, s - 1],
                    recv_sem=recv_sems.at[k, s - 1],
                    device_id=target,
                    device_id_type=MESH,
                )
            )
    return copies


def gather_kernel(ep_count, tp_count, groups, *refs):
    count = sum(n for _, n, _ in groups)
    blocks, gathered, scratch = refs[:count], refs[count : 2 * count], refs[2 * count :]
    place = Place(ep_count, tp_count)
    greet(place, longest([group[:2] for group in groups]))
    steps, ends, first = [], [], 0
    local, swaps = [], []
    for order, n, patience in groups:
        mine_in, mine_out = blocks[first : first + n], gathered[first : first + n]
        first += n
        if order == "t":
            swaps += exchange_copies(place, mine_in, mine_out, scratch[0], scratch[1])
            scratch = scratch[2:]
            continue
        send_sems, recv_sems, own_sems = scratch[:3]
        scratch = scratch[3:]
        pairs = list(zip(mine_in, mine_out))
        more, finish = [], []
        for lines, only in by_core(place, order):
            found = gather_events(place, lines, only, pairs, send_sems, recv_sems)
            more += found[0]
            finish += found[1]
        lines = by_core(place, order)[0][0]
        size = sum(block.shape[0] * block.shape[1] * (4 if block.dtype == jnp.float32 else 2) for block in mine_in)
        steps += [(key * size * patience, len(steps) + i, step) for i, (key, step) in enumerate(more)]
        ends += finish
        here = {name: place.own(name) for name, _ in place.dims(lines)}
        mine = place.index(here, place.core, len(lines) > 2)
        for k, (block, out) in enumerate(pairs):
            local.append(pltpu.make_async_copy(block, out.at[mine], own_sems.at[k]))
    steps.sort(key=lambda entry: entry[:2])
    lead = sum(1 for key, _, _ in steps if key == 0)
    for _, _, step in steps[:lead]:
        step()
    for copy in swaps + local:
        copy.start()
    for _, _, step in steps[lead:]:
        step()
    for on, finish in ends:
        guarded(on, finish)
    for copy in swaps + local:
        copy.wait()


def gather(ep_count, tp_count, collective_id, name, groups):
    arrays, shapes, scratch = [], [], []
    place = Place(ep_count, tp_count)
    for order, blocks, _ in groups:
        lines = [line for line, _ in by_core(place, order)]
        total = ep_count * tp_count if len(lines[0]) > 2 else ep_count if order != "t" else tp_count - 1
        for block in blocks:
            arrays.append(block)
            shapes.append(jax.ShapeDtypeStruct((total,) + block.shape, block.dtype))
        if order == "t":
            scratch += [pltpu.SemaphoreType.DMA((len(blocks), total))] * 2
            continue
        sends = max(count_gather_sends(place.dims(line)) for line in lines)
        scratch += [
            pltpu.SemaphoreType.DMA((len(blocks), sends)),
            pltpu.SemaphoreType.DMA((len(blocks), total)),
            pltpu.SemaphoreType.DMA((len(blocks),)),
        ]
    return pl.pallas_call(
        functools.partial(
            gather_kernel,
            ep_count,
            tp_count,
            tuple((order, len(blocks), patience) for order, blocks, patience in groups),
        ),
        out_shape=tuple(shapes),
        in_specs=[pl.BlockSpec(memory_space=pl.ANY)] * len(arrays),
        out_specs=tuple([pl.BlockSpec(memory_space=pl.ANY)] * len(arrays)),
        scratch_shapes=scratch,
        compiler_params=pltpu.CompilerParams(collective_id=collective_id, has_side_effects=True),
        name=name,
    )(*arrays)


def add_into(target, sources, dtype):
    rows, columns = target.shape
    piece = 128
    while columns % (piece * 2) == 0 and rows * piece * 2 <= 40 * 1024:
        piece *= 2

    def body(i, carry):
        window = pl.ds(pl.multiple_of(i * piece, piece), piece)
        total = sources[0][:, window].astype(jnp.float32)
        for source in sources[1:]:
            total = total + source[:, window].astype(jnp.float32)
        target[:, window] = total.astype(dtype)
        return carry

    lax.fori_loop(0, columns // piece, body, 0)


def norm_kernel(ep_count, tp_count, count, *refs):
    parts, extra, out = refs[:count], refs[count], refs[count + 1]
    tile, tiles, send, recv = refs[count + 2 :]
    devices = ep_count * tp_count
    me = lax.axis_index("ep") * tp_count + lax.axis_index("tp")

    def place(i):
        other = lax.rem(me + i, devices)
        return other, (other // tp_count, lax.rem(other, tp_count))

    barrier = pltpu.get_barrier_semaphore()

    def signal(i, carry):
        pl.semaphore_signal(barrier, inc=1, device_id=place(i)[1], device_id_type=MESH)
        return carry

    lax.fori_loop(1, devices, signal, 0)
    tile[...] = jnp.zeros_like(tile)
    for first in range(0, extra.shape[1], 128):
        tile[0:1, :] += extra[:, first : first + 128]
    for part in parts:

        def add(i, carry, part=part):
            piece = part[:, pl.ds(pl.multiple_of(i * 128, 128), 128)]
            tile[0:1, :] += jnp.sum(piece * piece, axis=0, keepdims=True)
            return carry

        lax.fori_loop(0, part.shape[1] // 128, add, 0)
    pl.semaphore_wait(barrier, devices - 1)

    def share(i, carry):
        pltpu.make_async_remote_copy(
            src_ref=tile,
            dst_ref=tiles.at[me],
            send_sem=send.at[i],
            recv_sem=recv.at[me],
            device_id=place(i)[1],
            device_id_type=MESH,
        ).start()
        return carry

    lax.fori_loop(1, devices, share, 0)
    out[...] = tile[...]

    def collect(i, carry):
        other = place(i)[0]
        pltpu.make_async_copy(tiles.at[other], tiles.at[other], recv.at[other]).wait()
        out[...] += tiles[other]
        return carry

    lax.fori_loop(1, devices, collect, 0)

    def sent(i, carry):
        pltpu.make_async_copy(tile, tile, send.at[i]).wait()
        return carry

    lax.fori_loop(1, devices, sent, 0)


def sum_of_squares(ep_count, tp_count, collective_id, parts, extra):
    devices = ep_count * tp_count
    inside = pl.BlockSpec(memory_space=pltpu.VMEM)
    total = pl.pallas_call(
        functools.partial(norm_kernel, ep_count, tp_count, len(parts)),
        out_shape=jax.ShapeDtypeStruct((8, 128), jnp.float32),
        in_specs=[inside] * (len(parts) + 1),
        out_specs=inside,
        scratch_shapes=[
            pltpu.VMEM((8, 128), jnp.float32),
            pltpu.VMEM((devices, 8, 128), jnp.float32),
            pltpu.SemaphoreType.DMA((devices,)),
            pltpu.SemaphoreType.DMA((devices,)),
        ],
        compiler_params=pltpu.CompilerParams(collective_id=collective_id, has_side_effects=True),
        name="sum_of_squares",
    )(*parts, extra)
    return jnp.sum(total)


def scatter_order(dims):
    blocks = sorted(relative_blocks(dims), key=lambda block: -sum(abs(s) for s in block))
    return sorted(blocks, key=lambda block: -max([k for k, s in enumerate(block) if s], default=-1))


def scatter_events(place, order, only, partials, outs, refs):
    count = len(partials)
    dims = place.dims(order)
    whole = len(dims) > 2
    here = {name: place.own(name) for name, _ in dims}
    owns, sibs = refs[:count], refs[count : 2 * count]
    lands = [refs[(2 + k) * count : (3 + k) * count] for k in range(len(dims))]
    sems = refs[(2 + len(dims)) * count :]
    own_sem, sib_send, sib_recv, line_send = sems[:4]
    line_recv = sems[4:]
    blocks = scatter_order(dims)
    info = {}
    starts, steps, ends = [], [], []
    for block in blocks:
        at, valid = dict(here), only
        for (name, _), shift in zip(dims, block):
            at[name], on = place.moved(name, shift)
            valid = both(valid, on)
        slot = place.slot(at, whole)
        local = [
            pltpu.make_async_copy(
                partials[k].at[place.index(at, place.core, whole)], owns[k].at[slot], own_sem.at[k, slot]
            )
            for k in range(count)
        ]
        across = [
            pltpu.make_async_remote_copy(
                src_ref=partials[k].at[place.index(at, 1 - place.core, whole)],
                dst_ref=sibs[k].at[slot],
                send_sem=sib_send.at[k, slot],
                recv_sem=sib_recv.at[k, slot],
                device_id=place.device(here, 1 - place.core),
                device_id_type=MESH,
            )
            for k in range(count)
        ]

        def start(local=local, across=across):
            for copy in across + local:
                copy.start()

        def finish(across=across):
            for copy in across:
                copy.wait_send()

        starts.append((valid, start))
        ends.append((valid, finish))
        info[block] = (at, valid, slot, local, across)

    def land_slot(level, at, shift, side):
        inner, wide = 0, 1
        for name, _ in dims[:level]:
            inner = inner * place.extent(name) + at[name]
            wide = wide * place.extent(name)
        return landings(dims[level][1]).index((shift, side)) * wide + inner

    number = 0
    for block in blocks:
        at, valid, slot, local, across = info[block]
        todo = []
        last = max([k for k, shift in enumerate(block) if shift], default=-1)
        extra_refs = []
        for level in range(len(dims) - 1, max(last, 0) - 1, -1):
            name, spread = dims[level]
            for shift, side in landings(spread):
                if shift == block[level]:
                    _, on = place.moved(name, side)
                    extra_refs.append((level, land_slot(level, at, shift, side), on))

        def arrive(local=local, across=across):
            for copy in local:
                copy.wait()
            for copy in across:
                copy.wait_recv()

        todo.append((valid, arrive))
        for k in range(count):
            sure = [owns[k].at[slot], sibs[k].at[slot]]
            maybe = []
            for level, spot, on in extra_refs:
                ref = lands[level][k].at[spot]

                def wait(ref=ref, k=k, level=level, spot=spot):
                    pltpu.make_async_copy(ref, ref, line_recv[level].at[k, spot]).wait()

                todo.append((both(valid, on), wait))
                if on is None:
                    sure.append(ref)
                else:
                    maybe.append((ref, on))
            if last >= 0:
                target, dtype = owns[k].at[slot], owns[k].dtype
            else:
                target, dtype = outs[k], outs[k].dtype

            def add(sure=sure, maybe=maybe, target=target, dtype=dtype):
                if not maybe:
                    add_into(target, sure, dtype)
                elif len(maybe) == 1:
                    ((ref, on),) = maybe
                    pl.when(on)(lambda: add_into(target, sure + [ref], dtype))
                    pl.when(jnp.logical_not(on))(lambda: add_into(target, sure, dtype))
                else:
                    (low, on_low), (high, on_high) = maybe
                    pl.when(on_low & on_high)(lambda: add_into(target, sure + [low, high], dtype))
                    pl.when(on_low & jnp.logical_not(on_high))(lambda: add_into(target, sure + [low], dtype))
                    pl.when(on_high & jnp.logical_not(on_low))(lambda: add_into(target, sure + [high], dtype))

            todo.append((valid, add))
        if last >= 0:
            name, spread = dims[last]
            way = 1 if block[last] > 0 else -1
            there, _ = place.moved(name, way)
            spot = land_slot(last, at, block[last] - way, -way if len(spread) > 2 else 1)
            made = [
                pltpu.make_async_remote_copy(
                    src_ref=owns[k].at[slot],
                    dst_ref=lands[last][k].at[spot],
                    send_sem=line_send.at[k, number],
                    recv_sem=line_recv[last].at[k, spot],
                    device_id=place.device({**here, name: there}, place.core),
                    device_id_type=MESH,
                )
                for k in range(count)
            ]
            number += 1

            def start(made=made):
                for copy in made:
                    copy.start()

            def finish(made=made):
                for copy in made:
                    copy.wait_send()

            todo.append((valid, start))
            ends.append((valid, finish))
        steps.append(todo)
    return starts, steps, ends


def scatter_sizes(place, order):
    found = []
    for line, _ in by_core(place, order):
        dims = place.dims(line)
        slots, lands = 1, []
        for name, spread in dims:
            lands.append(len(landings(spread)) * slots)
            slots *= place.extent(name)
        found.append((slots, lands, sum(1 for block in relative_blocks(dims) if any(block))))
    lands = [max(wide) for wide in zip(*[entry[1] for entry in found])]
    return found[0][0], lands, max(entry[2] for entry in found)


def scatter_scratch(place, order, partials):
    slots, lands, sends = scatter_sizes(place, order)
    count, dma = len(partials), pltpu.SemaphoreType.DMA
    scratch = []
    for wide in [slots, slots] + lands:
        scratch += [pltpu.VMEM((wide,) + p.shape[1:], p.dtype) for p in partials]
    return scratch + [dma((count, slots))] * 3 + [dma((count, sends))] + [dma((count, wide)) for wide in lands]


def greet_all(ep_count, tp_count):
    devices = ep_count * tp_count
    me = lax.axis_index("ep") * tp_count + lax.axis_index("tp")
    barrier = pltpu.get_barrier_semaphore()

    def signal(i, carry):
        other = lax.rem(me + i, devices)
        target = (other // tp_count, lax.rem(other, tp_count))
        pl.semaphore_signal(barrier, inc=1, device_id=target, device_id_type=MESH)
        return carry

    lax.fori_loop(1, devices, signal, 0)
    pl.semaphore_wait(barrier, devices - 1)


def add_squares(total, ref):
    def add(i, carry):
        piece = ref[:, pl.ds(pl.multiple_of(i * 128, 128), 128)]
        total[0:1, :] += jnp.sum(piece * piece, axis=0, keepdims=True)
        return carry

    lax.fori_loop(0, ref.shape[1] // 128, add, 0)


def exchanged_pieces(own, others, summed, total, held, come, load_sems, save_sem):
    pieces, parts = own.shape[0], others.shape[0]

    def loads(q):
        found = [pltpu.make_async_copy(own.at[q], held.at[q % 2], load_sems.at[q % 2, 0])]
        for s in range(parts):
            found.append(pltpu.make_async_copy(others.at[s, q], come.at[q % 2, s], load_sems.at[q % 2, s + 1]))
        return found

    def save(q):
        return pltpu.make_async_copy(held.at[q % 2], summed.at[q], save_sem.at[q % 2])

    def load(q):
        if q >= 2:
            save(q - 2).wait()
        for copy in loads(q):
            copy.start()

    def piece(q):
        for copy in loads(q):
            copy.wait()
        arrived = [come.at[q % 2, s] for s in range(parts)]
        add_into(held.at[q % 2], [held.at[q % 2]] + arrived, jnp.float32)
        add_squares(total, held.at[q % 2])
        save(q).start()
        if q + 2 < pieces:
            load(q + 2)

    def finish():
        for q in range(max(0, pieces - 2), pieces):
            save(q).wait()

    for q in range(min(2, pieces)):
        load(q)
    return [functools.partial(piece, q) for q in range(pieces)] + [finish]


def share_total(ep_count, tp_count, total, totals, send, recv, norm):
    devices = ep_count * tp_count
    me = lax.axis_index("ep") * tp_count + lax.axis_index("tp")

    def share(i, carry):
        other = lax.rem(me + i, devices)
        pltpu.make_async_remote_copy(
            src_ref=total,
            dst_ref=totals.at[me],
            send_sem=send.at[i],
            recv_sem=recv.at[me],
            device_id=(other // tp_count, lax.rem(other, tp_count)),
            device_id_type=MESH,
        ).start()
        return carry

    lax.fori_loop(1, devices, share, 0)
    norm[...] = total[...]

    def collect(i, carry):
        other = lax.rem(me + i, devices)
        pltpu.make_async_copy(totals.at[other], totals.at[other], recv.at[other]).wait()
        norm[...] += totals[other]
        return carry

    lax.fori_loop(1, devices, collect, 0)
    norm[...] = jnp.broadcast_to(jnp.sqrt(jnp.sum(norm[...], keepdims=True)), norm.shape)

    def sent(i, carry):
        pltpu.make_async_copy(total, total, send.at[i]).wait()
        return carry

    lax.fori_loop(1, devices, sent, 0)


def scatter_kernel(ep_count, tp_count, groups, normed, *refs):
    count = sum(n for _, n in groups)
    partials, refs = refs[:count], refs[count:]
    if normed:
        own, others, refs = refs[0], refs[1], refs[2:]
    outs, refs = refs[:count], refs[count:]
    if normed:
        summed, norm, refs = refs[0], refs[1], refs[2:]
        total, totals, held, come, load_sems, save_sem, send, recv = refs[:8]
        refs = refs[8:]
    place = Place(ep_count, tp_count)
    if normed:
        greet_all(ep_count, tp_count)
    else:
        greet(place, longest(groups))
    starts, steps, ends, swaps, first = [], [], [], [], 0
    for order, n in groups:
        mine_in, mine_out = partials[first : first + n], outs[first : first + n]
        first += n
        if order == "t":
            swaps += exchange_copies(place, mine_in, mine_out, refs[0], refs[1])
            refs = refs[2:]
            continue
        lines = by_core(place, order)
        used = n * (2 + len(lines[0][0])) + 4 + len(lines[0][0])
        for line, only in lines:
            more, done, finish = scatter_events(place, line, only, mine_in, mine_out, refs[:used])
            starts += [(i / len(more), len(starts) + i, entry) for i, entry in enumerate(more)]
            steps += [(i / len(done), len(steps) + i, todo) for i, todo in enumerate(done)]
            ends += finish
        refs = refs[used:]
    for copy in swaps:
        copy.start()
    for _, _, (on, start) in sorted(starts, key=lambda entry: entry[:2]):
        guarded(on, start)
    steps = [todo for _, _, todo in sorted(steps, key=lambda entry: entry[:2])]
    if normed:
        total[...] = jnp.zeros_like(total)
        extras = exchanged_pieces(own, others, summed, total, held, come, load_sems, save_sem)
        for i, act in enumerate(extras):
            steps.insert((4 + i) * len(steps) // (5 + len(extras)), [(None, act)])
    for todo in steps:
        for on, act in todo:
            guarded(on, act)
    if normed:
        for out in outs:
            add_squares(total, out)
        share_total(ep_count, tp_count, total, totals, send, recv, norm)
    for on, finish in ends:
        guarded(on, finish)
    for copy in swaps:
        copy.wait()


def landings(spread):
    if len(spread) == 2:
        return [(0, 1)]
    return [(shift, way) for shift in spread for way in (-1, 1) if shift - way in spread and shift * way <= 0]


def scatter_add(ep_count, tp_count, collective_id, name, groups, grads=None):
    place = Place(ep_count, tp_count)
    arrays, shapes, scratch, specs = [], [], [], []
    normed = grads is not None
    dma = pltpu.SemaphoreType.DMA
    for order, partials in groups:
        arrays += partials
        count = len(partials)
        if order == "t":
            shapes += [jax.ShapeDtypeStruct(p.shape, p.dtype) for p in partials]
            specs += [pl.BlockSpec(memory_space=pl.ANY)] * count
            scratch += [dma((count, tp_count - 1))] * 2
            continue
        shapes += [jax.ShapeDtypeStruct(p.shape[1:], jnp.float32) for p in partials]
        specs += [pl.BlockSpec(memory_space=pltpu.VMEM)] * count
        scratch += scatter_scratch(place, order, partials)
    if normed:
        own, others = grads
        arrays += [own, others]
        devices, parts = ep_count * tp_count, others.shape[0]
        shapes += [jax.ShapeDtypeStruct(own.shape, own.dtype), jax.ShapeDtypeStruct((8, 128), jnp.float32)]
        specs += [pl.BlockSpec(memory_space=pl.ANY), pl.BlockSpec(memory_space=pltpu.VMEM)]
        scratch = [
            pltpu.VMEM((8, 128), jnp.float32),
            pltpu.VMEM((devices, 8, 128), jnp.float32),
            pltpu.VMEM((2,) + own.shape[1:], own.dtype),
            pltpu.VMEM((2, parts) + own.shape[1:], others.dtype),
            dma((2, parts + 1)),
            dma((2,)),
            dma((devices,)),
            dma((devices,)),
        ] + scratch
    return pl.pallas_call(
        functools.partial(
            scatter_kernel,
            ep_count,
            tp_count,
            tuple((order, len(partials)) for order, partials in groups),
            normed,
        ),
        out_shape=tuple(shapes),
        in_specs=[pl.BlockSpec(memory_space=pl.ANY)] * len(arrays),
        out_specs=tuple(specs),
        scratch_shapes=scratch,
        compiler_params=pltpu.CompilerParams(
            collective_id=collective_id, has_side_effects=True, vmem_limit_bytes=VMEM_MOST
        ),
        name=name,
    )(*arrays)


def scatter_room(place, order, partials):
    slots, lands, _ = scatter_sizes(place, order)
    rows = [(p.shape[1] + 15) // 16 * 16 for p in partials]
    sizes = [r * p.shape[2] * p.dtype.itemsize for r, p in zip(rows, partials)]
    return (2 * slots + sum(lands)) * sum(sizes)


def scatter_all(ep_count, tp_count, collective_ids, name, groups):
    place = Place(ep_count, tp_count)
    calls, room = [[]], 0
    for order, partials in groups:
        need = 0 if order == "t" else scatter_room(place, order, partials)
        if calls[-1] and room + need > VMEM_MOST * 19 // 20:
            calls.append([])
            room = 0
        calls[-1].append((order, partials))
        room += need
    found = []
    for i, call in enumerate(calls):
        found += scatter_add(ep_count, tp_count, collective_ids[i], "%s_%d" % (name, i), call)
    return found

OVER_LAST = (((1,), (1,)), ((), ()))
OVER_FIRST = (((0,), (0,)), ((), ()))
STRAIGHT = (((1,), (0,)), ((), ()))


def mul(left, right, dims=STRAIGHT):
    return lax.dot_general(left, right, dims, preferred_element_type=jnp.float32)


def rope_rows(length):
    places = np.arange(length, dtype=np.float32)
    frequencies = ROPE_BASE ** (-np.arange(HDIM // 2, dtype=np.float32) * np.float32(2.0 / HDIM))
    angles = places[:, None] * frequencies.astype(np.float32)[None, :]
    cosine, sine = np.cos(angles), np.sin(angles)
    return (
        np.concatenate([cosine, cosine], axis=1).astype(np.float32),
        np.concatenate([-sine, sine], axis=1).astype(np.float32),
    )


def unit_of(values):
    factor = lax.rsqrt(jnp.mean(values * values, axis=-1, keepdims=True) + NORM_EPS)
    return values * factor, factor


def masked_probs(queries, keys, allowed):
    raw = mul(queries, keys, OVER_LAST) * HDIM ** (-0.5)
    scores = jnp.where(allowed, raw, NEG_BIG)
    weights = jnp.exp(scores - jnp.max(scores, axis=-1, keepdims=True))
    return weights * (1.0 / jnp.sum(weights, axis=-1, keepdims=True))


def allowed_pairs(seg_row, seg_column):
    length = seg_row.shape[1]
    later = lax.broadcasted_iota(jnp.int32, (length, length), 0)
    earlier = lax.broadcasted_iota(jnp.int32, (length, length), 1)
    return (later >= earlier) & (seg_column[:, 0:1] == seg_row[0:1, :])


def forward_kernel(tokens, seg_row, seg_column, gains, cosine, sine, wq, wk, wv, wo,
                   qkv_out, attended, hidden, normed_two, normed):
    pair = pl.program_id(0)
    width = tokens.shape[1]
    wide = 2 * HDIM

    @pl.when(pair == 0)
    def _():
        values = tokens[...].astype(jnp.float32)
        normed[...] = (unit_of(values)[0] * gains[0:1, :]).astype(jnp.bfloat16)
        hidden[...] = values

    allowed = allowed_pairs(seg_row, seg_column)
    window = pl.ds(pl.multiple_of(pair * wide, wide), wide)
    made = []
    for part, weight in enumerate((wq, wk, wv)):
        projected = mul(normed[...], weight[...])
        heads = []
        for j in range(2):
            head = projected[:, j * HDIM : (j + 1) * HDIM]
            if part < 2:
                head = head * cosine[...] + pltpu.roll(head, HDIM // 2, 1) * sine[...]
            heads.append(head.astype(jnp.bfloat16))
            qkv_out[:, pl.ds(pl.multiple_of(part * width + pair * wide + j * HDIM, HDIM), HDIM)] = heads[j]
        made.append(heads)
    for j in range(2):
        probs = masked_probs(made[0][j], made[1][j], allowed).astype(jnp.bfloat16)
        attended[:, pl.ds(pl.multiple_of(pair * wide + j * HDIM, HDIM), HDIM)] = mul(
            probs, made[2][j]
        ).astype(jnp.bfloat16)
    hidden[...] += mul(attended[:, window], wo[...])

    @pl.when(pair == pl.num_programs(0) - 1)
    def _():
        normed_two[...] = (unit_of(hidden[...])[0] * gains[1:2, :]).astype(jnp.bfloat16)


def attention_forward(tokens, segments, gains, qkv_low, out_low):
    length, width = tokens.shape
    wide, pairs = 2 * HDIM, HEADS // 2
    cosine, sine = rope_rows(length)
    seg_row = jnp.broadcast_to(segments, (8, length))
    seg_column = jnp.broadcast_to(segments.T, (length, 128))
    low = jnp.bfloat16

    def whole(*shape):
        return pl.BlockSpec(shape, lambda i: (0,) * len(shape))

    def columns(part):
        return pl.BlockSpec((width, wide), lambda i: (0, part * pairs + i))

    return pl.pallas_call(
        forward_kernel,
        grid=(pairs,),
        in_specs=[
            whole(length, width), whole(8, length), whole(length, 128), whole(8, width),
            whole(length, HDIM), whole(length, HDIM), columns(0), columns(1), columns(2),
            pl.BlockSpec((wide, width), lambda i: (i, 0)),
        ],
        out_specs=[whole(length, 3 * width), whole(length, width), whole(length, width), whole(length, width)],
        out_shape=[
            jax.ShapeDtypeStruct((length, 3 * width), low),
            jax.ShapeDtypeStruct((length, width), low),
            jax.ShapeDtypeStruct((length, width), jnp.float32),
            jax.ShapeDtypeStruct((length, width), low),
        ],
        scratch_shapes=[pltpu.VMEM((length, width), low)],
        compiler_params=pltpu.CompilerParams(
            dimension_semantics=("arbitrary",), vmem_limit_bytes=VMEM_MOST
        ),
        name="attention_forward",
    )(tokens, seg_row, seg_column, gains, jnp.asarray(cosine), jnp.asarray(sine), qkv_low, qkv_low, qkv_low, out_low)


def spread_matrix(units, padded, group, step):
    unit = lax.broadcasted_iota(jnp.int32, (units, padded), 0)
    spot = lax.broadcasted_iota(jnp.int32, (units, padded), 1)
    within = jnp.bitwise_and(spot, step - 1)
    source = (spot - within) // step * group + within
    return jnp.where((unit == source) & (within < group), 1.0, 0.0).astype(jnp.bfloat16)


def backward_kernel(group, step, carried, *refs):
    (tokens, cot, seg_row, seg_column, gains, cosine, sine, qkv_act, attended, hidden, normed_two,
     routed_grad, wq, wk, wv, wo, shin, shout) = refs[:18]
    refs = refs[18:]
    if carried:
        ep_count, tp_count, order = carried
        result_part, sent_grads, refs = refs[0], refs[1], refs[2:]
    base, tokens_grad, gain_grads, qkv_grad, out_grad, shin_grad, shout_grad = refs[:7]
    refs = refs[7:]
    if carried:
        routed, grads_back, refs = refs[0], refs[1], refs[2:]
    (normed, normed_turned, branch, grad_one, pieces, stage, stage_sem) = refs[:7]
    refs = refs[7:]
    at = pl.program_id(0)
    width = tokens.shape[1]
    wide = 2 * HDIM
    low = jnp.bfloat16
    units = shin.shape[1] // 2

    if carried:
        place = Place(ep_count, tp_count)
        starts, lines, ends = scatter_events(place, order, None, [result_part], [routed], refs[:-2])
        swaps = exchange_copies(place, [sent_grads], [grads_back], refs[-2], refs[-1])
        first = sum(1 for block in scatter_order(place.dims(order)) if block[-1])
        turns = {0: lines[:first], 2: lines[first : first + 2], 4: lines[first + 2 : first + 4]}
        turns[5] = lines[first + 4 :]

    def run(entries):
        for on, act in entries:
            guarded(on, act)

    def carry(turn):
        if carried:
            for todo in turns.get(turn, []):
                run(todo)

    def stage_copy(part, pair):
        return pltpu.make_async_copy(
            stage.at[part],
            qkv_grad.at[:, pl.ds(pl.multiple_of(part * width + pair * wide, wide), wide)],
            stage_sem.at[part],
        )

    @pl.when(at == 0)
    def _():
        if carried:
            greet(place, "tab")
            for copy in swaps:
                copy.start()
            run(starts)
        unit_one = unit_of(tokens[...].astype(jnp.float32))[0]
        first = unit_one * gains[0:1, :]
        normed[...] = first.astype(low)
        normed_turned[...] = first.T.astype(low)
        pre_gate = mul(normed_two[...], shin[:, :units])
        pre_up = mul(normed_two[...], shin[:, units:])
        sigmoid = jax.nn.sigmoid(pre_gate)
        act = (pre_gate * sigmoid * pre_up).astype(low)
        spread = spread_matrix(units, shout.shape[0], group, step)
        act_spread = mul(act, spread).astype(low)
        base[...] = hidden[...] + mul(act_spread, shout[...])
        shout_grad[...] = mul(act_spread, cot[...], OVER_FIRST).astype(low)
        carry(0)
        shout_tight = mul(spread, shout[...]).astype(low)
        grad_act = mul(cot[...], shout_tight, OVER_LAST)
        grad_up = (grad_act * pre_gate * sigmoid).astype(low)
        grad_gate = (grad_act * pre_up * sigmoid * (1.0 + pre_gate * (1.0 - sigmoid))).astype(low)
        shin_grad[:, :units] = mul(normed_two[...], grad_gate, OVER_FIRST).astype(low)
        shin_grad[:, units:] = mul(normed_two[...], grad_up, OVER_FIRST).astype(low)
        grad_two = (
            routed_grad[...]
            + mul(grad_gate, shin[:, :units], OVER_LAST)
            + mul(grad_up, shin[:, units:], OVER_LAST)
        )
        unit_two, factor_two = unit_of(hidden[...])
        gain_grads[...] = jnp.zeros_like(gain_grads)
        gain_grads[1:2, :] = jnp.sum(grad_two * unit_two, axis=0, keepdims=True)
        grad_unit = grad_two * gains[1:2, :]
        back = factor_two * (
            grad_unit - unit_two * jnp.mean(grad_unit * unit_two, axis=-1, keepdims=True)
        )
        tokens_grad[...] = cot[...].astype(jnp.float32) + back
        branch[...] = tokens_grad[...].astype(low)
        grad_one[...] = jnp.zeros_like(grad_one)

    @pl.when(at > 0)
    def _():
        pair = at - 1
        allowed = allowed_pairs(seg_row, seg_column)
        window = pl.ds(pl.multiple_of(pair * wide, wide), wide)
        out_grad[...] = mul(attended[:, window], branch[...], OVER_FIRST).astype(low)
        grad_att = mul(branch[...], wo[...], OVER_LAST).astype(low)
        for j in range(2):

            def head(part):
                start = pl.multiple_of(part * width + pair * wide + j * HDIM, HDIM)
                return qkv_act[:, pl.ds(start, HDIM)]

            queries, keys, values = head(0), head(1), head(2)
            own = slice(j * HDIM, (j + 1) * HDIM)
            grad_own = grad_att[:, own]
            probs = masked_probs(queries, keys, allowed)
            grad_probs = mul(grad_own, values, OVER_LAST)
            grad_values = mul(probs.astype(low), grad_own, OVER_FIRST)
            row_dot = jnp.sum(probs * grad_probs, axis=-1, keepdims=True)
            grad_scores = (probs * (grad_probs - row_dot)).astype(low)
            grad_queries = mul(grad_scores, keys) * HDIM ** (-0.5)
            grad_keys = mul(grad_scores, queries, OVER_FIRST) * HDIM ** (-0.5)
            for part, grad in ((0, grad_queries), (1, grad_keys), (2, grad_values)):
                if part < 2:
                    grad = grad * cosine[...] - pltpu.roll(grad, HDIM // 2, 1) * sine[...]
                pieces[part, :, own] = grad.astype(low)
        for part, weight in enumerate((wq, wk, wv)):

            @pl.when(pair > 0)
            def _(part=part):
                stage_copy(part, pair - 1).wait()

            stage[part] = mul(normed_turned[...], pieces[part]).astype(low)
            stage_copy(part, pair).start()
            grad_one[...] += mul(pieces[part], weight[...], OVER_LAST)

        for turn in (2, 4):
            pl.when(at == turn)(functools.partial(carry, turn))

        @pl.when(at == pl.num_programs(0) - 1)
        def _():
            unit_one, factor_one = unit_of(tokens[...].astype(jnp.float32))
            total = grad_one[...]
            gain_grads[0:1, :] = jnp.sum(total * unit_one, axis=0, keepdims=True)
            grad_unit = total * gains[0:1, :]
            back = factor_one * (
                grad_unit - unit_one * jnp.mean(grad_unit * unit_one, axis=-1, keepdims=True)
            )
            tokens_grad[...] += back
            for part in range(3):
                stage_copy(part, pair).wait()
            carry(5)
            if carried:
                run(ends)
                for copy in swaps:
                    copy.wait()


def dense_backward(group, step, tokens, cot, segments, gains, qkv_act, attended, hidden, normed_two,
                   routed_grad, qkv_low, out_low, shin_low, shout_spread, ep_count, tp_count,
                   collective_id, order, result_part, sent_grads):
    length, width = tokens.shape
    wide, pairs = 2 * HDIM, HEADS // 2
    cosine, sine = rope_rows(length)
    seg_row = jnp.broadcast_to(segments, (8, length))
    seg_column = jnp.broadcast_to(segments.T, (length, 128))
    low = jnp.bfloat16
    once = pl.Buffered(1)

    def whole(*shape):
        return pl.BlockSpec(shape, lambda i: (0,) * len(shape), pipeline_mode=once)

    def columns(part):
        return pl.BlockSpec((width, wide), lambda i: (0, part * pairs + jnp.maximum(i - 1, 0)))

    rows = pl.BlockSpec((wide, width), lambda i: (jnp.maximum(i - 1, 0), 0))
    in_specs = [
        whole(length, width), whole(length, width), whole(8, length), whole(length, 128),
        whole(8, width), whole(length, HDIM), whole(length, HDIM), whole(length, 3 * width),
        whole(length, width), whole(length, width), whole(length, width), whole(length, width),
        columns(0), columns(1), columns(2), rows,
        whole(*shin_low.shape), whole(*shout_spread.shape),
    ]
    anywhere = pl.BlockSpec(memory_space=pl.ANY)
    out_specs = [
        whole(length, width), whole(length, width), whole(8, width),
        anywhere, rows, whole(*shin_low.shape), whole(*shout_spread.shape),
    ]
    out_shape = [
        jax.ShapeDtypeStruct((length, width), jnp.float32),
        jax.ShapeDtypeStruct((length, width), jnp.float32),
        jax.ShapeDtypeStruct((8, width), jnp.float32),
        jax.ShapeDtypeStruct((width, 3 * width), low),
        jax.ShapeDtypeStruct((width, width), low),
        jax.ShapeDtypeStruct(shin_low.shape, low),
        jax.ShapeDtypeStruct(shout_spread.shape, low),
    ]
    scratch = [
        pltpu.VMEM((length, width), low), pltpu.VMEM((width, length), low),
        pltpu.VMEM((length, width), low), pltpu.VMEM((length, width), jnp.float32),
        pltpu.VMEM((3, length, wide), low),
        pltpu.VMEM((3, width, wide), low), pltpu.SemaphoreType.DMA((3,)),
    ]
    arguments = [tokens, cot, seg_row, seg_column, gains, jnp.asarray(cosine), jnp.asarray(sine), qkv_act,
                 attended, hidden, normed_two, routed_grad, qkv_low, qkv_low, qkv_low, out_low, shin_low,
                 shout_spread]
    carried, more = None, {}
    if result_part is not None:
        carried, more = (ep_count, tp_count, order), dict(collective_id=collective_id, has_side_effects=True)
        arguments += [result_part, sent_grads]
        in_specs += [anywhere, anywhere]
        out_specs += [whole(length, width), anywhere]
        out_shape += [
            jax.ShapeDtypeStruct((length, width), jnp.float32),
            jax.ShapeDtypeStruct(sent_grads.shape, sent_grads.dtype),
        ]
        scratch += scatter_scratch(Place(ep_count, tp_count), order, [result_part])
        scratch += [pltpu.SemaphoreType.DMA((1, tp_count - 1))] * 2
    return pl.pallas_call(
        functools.partial(backward_kernel, group, step, carried),
        grid=(pairs + 1,),
        in_specs=in_specs,
        out_specs=out_specs,
        out_shape=out_shape,
        scratch_shapes=scratch,
        compiler_params=pltpu.CompilerParams(
            dimension_semantics=("arbitrary",), vmem_limit_bytes=VMEM_MOST, **more
        ),
        name="dense_backward",
    )(*arguments)


def expert_kernel(parts, per_step, cap, *refs):
    normed, cot, info = refs[:3]
    ins, outs_w = refs[3 : 3 + parts], refs[3 + parts : 3 + 2 * parts]
    result_ref, input_ref, own_grad = refs[3 + 2 * parts : 6 + 2 * parts]
    sent = refs[6 + 2 * parts : 5 + 3 * parts]
    scratch = refs[5 + 3 * parts :]
    rows_x, rows_g, gate_col, result_acc, input_acc = scratch[:5]
    sums = (own_grad,) + tuple(scratch[5:])
    step = pl.program_id(0)
    tok = normed.shape[1]
    width = normed.shape[2]
    chunk = 256

    @pl.when(step == 0)
    def _():
        for total in sums:
            total[...] = jnp.zeros_like(total)

    slots = lax.broadcasted_iota(jnp.int32, (cap, tok), 0).astype(jnp.float32)
    for s in range(per_step):
        hit = slots == info[s, 0:1, :]
        picks = jnp.where(hit, 1.0, 0.0).astype(jnp.bfloat16)
        gates = jnp.sum(jnp.where(hit, info[s, 1:2, :], 0.0), axis=1, keepdims=True)
        window = pl.ds(s * cap, cap)
        gate_col[window, :] = jnp.broadcast_to(gates, (cap, 128))
        rows_x[window, :] = jnp.dot(picks, normed[s], preferred_element_type=jnp.float32).astype(
            jnp.bfloat16
        )
        taken = jnp.dot(picks, cot[s], preferred_element_type=jnp.float32)
        rows_g[window, :] = (gates * taken).astype(jnp.bfloat16)
    across = (((1,), (1,)), ((), ()))
    down = (((0,), (0,)), ((), ()))

    def mul(left, right, dims):
        return lax.dot_general(left, right, dims, preferred_element_type=jnp.float32)

    straight = (((1,), (0,)), ((), ()))
    for p in range(parts):
        gate_pre = mul(rows_x[...], ins[p][0], across)
        up_pre = mul(rows_x[...], ins[p][1], across)
        sigmoid = jax.nn.sigmoid(gate_pre)
        active = (gate_pre * sigmoid * up_pre).astype(jnp.bfloat16)
        grad_act = mul(rows_g[...], outs_w[p][...], across)
        grad_up = (grad_act * gate_pre * sigmoid).astype(jnp.bfloat16)
        grad_gate = (grad_act * up_pre * sigmoid * (1.0 + gate_pre * (1.0 - sigmoid))).astype(
            jnp.bfloat16
        )
        for first in range(0, width, chunk):
            window = slice(first, first + chunk)
            result = mul(active, outs_w[p][:, window], straight)
            back = mul(grad_gate, ins[p][0, :, window], straight) + mul(
                grad_up, ins[p][1, :, window], straight
            )
            if p == 0:
                result_acc[:, window] = result
                input_acc[:, window] = back
            else:
                result_acc[:, window] += result
                input_acc[:, window] += back
            sums[p][0, :, window] += mul(grad_gate, rows_x[:, window], down)
            sums[p][1, :, window] += mul(grad_up, rows_x[:, window], down)
            sums[p][2, :, window] += mul(active, rows_g[:, window], down)
    for s in range(per_step):
        hit = slots == info[s, 0:1, :]
        picks = jnp.where(hit, 1.0, 0.0).astype(jnp.bfloat16)
        window = pl.ds(s * cap, cap)
        rounded = result_acc[window, :].astype(jnp.bfloat16).astype(jnp.float32)
        weighted = (gate_col[window, 0:1] * rounded).astype(jnp.bfloat16)
        result_ref[s] = mul(picks, weighted, down).astype(jnp.bfloat16)
        input_ref[s] = mul(picks, input_acc[window, :].astype(jnp.bfloat16), down).astype(
            jnp.bfloat16
        )

    @pl.when(step == pl.num_programs(0) - 1)
    def _():
        for p in range(1, parts):
            sent[p - 1][...] = sums[p][...].astype(jnp.bfloat16)


def expert_pass(normed_all, cot_all, info, ins, outs_w, cap):
    ep_count, tok, width = normed_all.shape
    parts = len(ins)
    hidden = ins[0].shape[1]
    per_step = max(1, min(ep_count, 256 // cap))
    rows = per_step * cap
    token_spec = pl.BlockSpec((per_step, tok, width), lambda i: (i, 0, 0))
    once = pl.Buffered(1)
    in_specs = [token_spec, token_spec, pl.BlockSpec((per_step, 2, tok), lambda i: (i, 0, 0))]
    in_specs += [
        pl.BlockSpec((2, hidden, width), lambda i: (0, 0, 0), pipeline_mode=once)
    ] * parts
    in_specs += [pl.BlockSpec((hidden, width), lambda i: (0, 0), pipeline_mode=once)] * parts
    grad_spec = pl.BlockSpec((3, hidden, width), lambda i: (0, 0, 0), pipeline_mode=once)
    token_shape = jax.ShapeDtypeStruct((ep_count, tok, width), jnp.bfloat16)
    out_shape = [token_shape, token_shape, jax.ShapeDtypeStruct((3, hidden, width), jnp.float32)]
    out_shape += [jax.ShapeDtypeStruct((3, hidden, width), jnp.bfloat16)] * (parts - 1)
    scratch = [
        pltpu.VMEM((rows, width), jnp.bfloat16),
        pltpu.VMEM((rows, width), jnp.bfloat16),
        pltpu.VMEM((rows, 128), jnp.float32),
        pltpu.VMEM((rows, width), jnp.float32),
        pltpu.VMEM((rows, width), jnp.float32),
    ] + [pltpu.VMEM((3, hidden, width), jnp.float32)] * (parts - 1)
    found = pl.pallas_call(
        functools.partial(expert_kernel, parts, per_step, cap),
        grid=(ep_count // per_step,),
        in_specs=in_specs,
        out_specs=[token_spec, token_spec] + [grad_spec] * parts,
        out_shape=out_shape,
        scratch_shapes=scratch,
        compiler_params=pltpu.CompilerParams(
            dimension_semantics=("arbitrary",), vmem_limit_bytes=VMEM_MOST
        ),
        cost_estimate=pl.CostEstimate(
            flops=18 * ep_count * cap * parts * hidden * width,
            bytes_accessed=8 * ep_count * tok * width + 30 * parts * hidden * width,
            transcendentals=ep_count * cap * parts * hidden,
        ),
        name="expert_pass",
    )(normed_all, cot_all, info, *ins, *outs_w)
    return found[0], found[1], found[2], found[3:]


def adam_rows(source, target, grad, clip, rate, decay):
    weight, first, second = source
    clipped = grad * clip
    first_new = BETA_ONE * first + (1.0 - BETA_ONE) * clipped
    second_new = BETA_TWO * second + (1.0 - BETA_TWO) * clipped * clipped
    corr_one = 1.0 - BETA_ONE**STEP
    corr_two = 1.0 - BETA_TWO**STEP
    stepped = first_new * (1.0 / corr_one) / (jnp.sqrt(second_new * (1.0 / corr_two)) + ADAM_EPS)
    weight_new = weight - rate * (stepped + decay * weight)
    refs, window = target
    for ref, value in zip(refs, (weight_new, first_new, second_new, weight_new)):
        ref[window] = value.astype(ref.dtype)


def adam_dense_kernel(count, norm, *refs):
    clip = jnp.minimum(1.0, CLIP_LEVEL / (norm[0:1, 0:1] + 1e-06))
    for k in range(count):
        source, grad = refs[4 * k : 4 * k + 3], refs[4 * k + 3]
        target = refs[4 * (count + k) : 4 * (count + k) + 4]
        rows, width = source[0].shape
        if k == count - 1:
            values = [ref[...] for ref in source]
            window = (slice(None), slice(None))
            adam_rows(values, (target, window), grad[:rows, :width], clip, GAIN_RATE, 0.0)
            continue

        def columns(i, carry, source=source, grad=grad, target=target, rows=rows):
            some = pl.ds(pl.multiple_of(i * 256, 256), 256)
            values = [ref[:, some] for ref in source]
            adam_rows(values, (target, (slice(None), some)), grad[:rows, some], clip, MATRIX_RATE, WEIGHT_DECAY)
            return carry

        lax.fori_loop(0, width // 256, columns, 0)


def adam_dense(norm, dense):
    low, full = jnp.bfloat16, jnp.float32
    more = [array for entry in dense for array in entry]
    out_shape = [jax.ShapeDtypeStruct(e[0].shape, kind) for e in dense for kind in (full, full, full, low)]
    inside = pl.BlockSpec(memory_space=pltpu.VMEM)
    found = pl.pallas_call(
        functools.partial(adam_dense_kernel, len(dense)),
        in_specs=[inside] * (1 + len(more)),
        out_specs=[inside] * len(out_shape),
        out_shape=out_shape,
        compiler_params=pltpu.CompilerParams(vmem_limit_bytes=VMEM_MOST),
        name="adam_dense",
    )(norm, *more)
    return [found[4 * k : 4 * k + 4] for k in range(len(dense))]


FROM_A = {1: (1, 0), 2: (2, 1), 3: (4, 1)}
FROM_B = {0: (0, 2), 1: (2, 1), 2: (4, 1), 3: (6, 0)}
TO_B = {1: (6, 1), 2: (5, 2), 3: (7, 2)}
TO_A = {2: (6, 2)}


def nearest(place):
    count = place.na
    table = [sorted(range(count), key=lambda other: abs(other - own)) for own in range(count)]

    def chip_at(r):
        found = jnp.int32(0)
        for own in range(count):
            for rank in range(count):
                found = found + jnp.where((place.a == own) & (r == rank), table[own][rank], 0)
        return found

    return chip_at


def fused_kernel(parts, ep_count, tp_count, cap, *refs):
    normed, info, cot = refs[:3]
    w_in, w_out = refs[3 : 3 + parts], refs[3 + parts : 3 + 2 * parts]
    refs = refs[3 + 2 * parts :]
    result_ref, routed_ref, own_grad = refs[:3]
    sent = refs[3 : 2 + parts]
    scratch = refs[2 + parts :]
    tok, infos, cots, vin, vout, own, sib, sib_stage, bland, aland, res_stage = scratch[:11]
    rows_x, rows_g, gate_col, result_acc, input_acc, stage = scratch[11:17]
    sums = (own_grad,) + tuple(scratch[17 : 16 + parts])
    (tok_recv, tok_send, local_sem, cot_sem, sib_recv, sib_send, b_recv, b_send, a_recv, a_send,
     res_sem, stage_sem) = scratch[16 + parts :]
    place = Place(ep_count, tp_count)
    na, a, b, core = place.na, place.a, place.b, place.core
    width = normed.shape[1]
    me = (a * 2 + b) * 2 + core
    chip_at = nearest(place)
    chunk = 256

    def device(a_, b_, core_):
        return ((a_ * 2 + b_) * 2 + core_, place.t)

    sibling, across = device(a, b, 1 - core), device(a, 1 - b, core)
    barrier = pltpu.get_barrier_semaphore()
    for target in (sibling, across):
        pl.semaphore_signal(barrier, inc=1, device_id=target, device_id_type=MESH)
    for step in range(1, na):
        pl.semaphore_signal(
            barrier, inc=1, device_id=device(lax.rem(a + step, na), b, core), device_id_type=MESH
        )
    pl.semaphore_wait(barrier, na + 1)

    def hop(index, number, target, first=False):
        return [
            pltpu.make_async_remote_copy(
                src_ref=own_block if first else held.at[index],
                dst_ref=held.at[index],
                send_sem=tok_send.at[k, number],
                recv_sem=tok_recv.at[k, index],
                device_id=target,
                device_id_type=MESH,
            )
            for k, (own_block, held) in enumerate(((normed, tok), (info, infos)))
        ]

    def start(copies):
        for copy in copies:
            copy.start()

    def arrived(index):
        for k, held in enumerate((tok, infos)):
            pltpu.make_async_copy(held.at[index], held.at[index], tok_recv.at[k, index]).wait()

    ends = []

    def launch(on, copies):
        def finish():
            for copy in copies:
                copy.wait_send()

        guarded(on, lambda: start(copies))
        ends.append((on, finish))

    up, down_ok = a + 1 < na, a > 0
    launch(up, hop(me, 0, device(a + 1, b, core), True))
    launch(down_ok, hop(me, 1, device(a - 1, b, core), True))
    launch(None, hop(me, 2, across, True))
    launch(None, hop(me, 3, sibling, True))
    loads = [pltpu.make_async_copy(normed, tok.at[me], local_sem.at[0])]
    loads.append(pltpu.make_async_copy(info, infos.at[me], local_sem.at[1]))
    for p in range(parts):
        loads.append(pltpu.make_async_copy(w_in[p], vin.at[p], local_sem.at[2 + 2 * p]))
        loads.append(pltpu.make_async_copy(w_out[p], vout.at[p], local_sem.at[3 + 2 * p]))
    start(loads)

    def chip_of(k):
        near = (lax.rem(k, 2) == 0) == (k < 2 * na - 2)
        return chip_at(k // 2) * 2 + jnp.where(near, b, 1 - b)

    def cot_copies(k):
        chip, buffer = chip_of(k), lax.rem(k, 2)
        return [
            pltpu.make_async_copy(cot.at[chip * 2 + j], cots.at[buffer, j], cot_sem.at[buffer, j])
            for j in range(2)
        ]

    start(cot_copies(jnp.int32(0)))
    for total in sums:
        total[...] = jnp.zeros_like(total)
    for load in loads:
        load.wait()

    def from_a(r):
        other = chip_at(r)
        index = (other * 2 + b) * 2 + core
        arrived(index)
        first = 4 + 3 * (r - 1)
        beyond = jnp.where(other > a, a - 1, a + 1)
        on = (beyond >= 0) & (beyond < na)
        copies = hop(index, first, device(beyond, b, core))
        pl.when(on)(lambda: start(copies))
        start(hop(index, first + 1, across))
        start(hop(index, first + 2, sibling))

    def from_b(r):
        index = (chip_at(r) * 2 + 1 - b) * 2 + core
        arrived(index)
        start(hop(index, 4 + 3 * (na - 1) + r, sibling))

    def sent_from_a(r):
        other = chip_at(r)
        index = (other * 2 + b) * 2 + core
        first = 4 + 3 * (r - 1)
        beyond = jnp.where(other > a, a - 1, a + 1)
        on = (beyond >= 0) & (beyond < na)

        def finish(number):
            for copy in hop(index, number, sibling):
                copy.wait_send()

        pl.when(on)(lambda: finish(first))
        finish(first + 1)
        finish(first + 2)

    def sib_wait(chip):
        pltpu.make_async_copy(sib.at[chip], sib.at[chip], sib_recv.at[chip]).wait()

    def to_b(r):
        chip = chip_at(r) * 2 + 1 - b
        sib_wait(chip)
        add_into(own.at[chip], [own.at[chip], sib.at[chip]], own.dtype)
        pltpu.make_async_remote_copy(
            src_ref=own.at[chip],
            dst_ref=bland.at[r],
            send_sem=b_send.at[r],
            recv_sem=b_recv.at[r],
            device_id=across,
            device_id_type=MESH,
        ).start()

    def b_wait(r):
        pltpu.make_async_copy(bland.at[r], bland.at[r], b_recv.at[r]).wait()

    def to_a(r):
        other = chip_at(r)
        chip = other * 2 + b
        sib_wait(chip)
        b_wait(r)
        add_into(own.at[chip], [own.at[chip], sib.at[chip], bland.at[r]], own.dtype)
        pltpu.make_async_remote_copy(
            src_ref=own.at[chip],
            dst_ref=aland.at[a],
            send_sem=a_send.at[r],
            recv_sem=a_recv.at[a],
            device_id=device(other, b, core),
            device_id_type=MESH,
        ).start()

    over_last = (((1,), (1,)), ((), ()))
    over_first = (((0,), (0,)), ((), ()))
    straight = (((1,), (0,)), ((), ()))

    def mul(left, right, dims):
        return lax.dot_general(left, right, dims, preferred_element_type=jnp.float32)

    slots = lax.broadcasted_iota(jnp.int32, (cap, normed.shape[0]), 0).astype(jnp.float32)

    def picks_of(source):
        return slots == infos[source, pl.ds(me, 1), :]

    def turn(k, phase):
        for r in range(1, na):
            for far, spot in FROM_A.items():
                if spot[1] == phase and (r + 1) // 2 <= far <= r:
                    on = (k == spot[0]) & (jnp.abs(chip_at(r) - a) == far)
                    pl.when(on)(functools.partial(from_a, r))
        for act, spots in ((from_b, FROM_B), (to_b, TO_B), (to_a, TO_A)):
            for r, spot in spots.items():
                if spot[1] == phase:
                    pl.when(k == spot[0])(functools.partial(act, r))

    def work(k, carry):
        chip, buffer = chip_of(k), lax.rem(k, 2)

        @pl.when(k + 1 < 2 * na)
        def _():
            start(cot_copies(k + 1))

        turn(k, 0)
        arrived(chip * 2 + 1 - core)
        for copy in cot_copies(k):
            copy.wait()
        for j in range(2):
            hit = picks_of(chip * 2 + j)
            picks = jnp.where(hit, 1.0, 0.0).astype(jnp.bfloat16)
            gate_row = infos[chip * 2 + j, pl.ds(ep_count + me, 1), :]
            gates = jnp.sum(jnp.where(hit, gate_row, 0.0), axis=1, keepdims=True)
            window = pl.ds(j * cap, cap)
            gate_col[window, :] = jnp.broadcast_to(gates, (cap, 128))
            rows_x[window, :] = mul(picks, tok[chip * 2 + j], straight).astype(jnp.bfloat16)
            taken = mul(picks, cots[buffer, j], straight)
            rows_g[window, :] = (gates * taken).astype(jnp.bfloat16)
        for p in range(parts):
            gate_pre = mul(rows_x[...], vin[p, 0], over_last)
            up_pre = mul(rows_x[...], vin[p, 1], over_last)
            sigmoid = jax.nn.sigmoid(gate_pre)
            active = (gate_pre * sigmoid * up_pre).astype(jnp.bfloat16)
            grad_act = mul(rows_g[...], vout[p], over_last)
            grad_up = (grad_act * gate_pre * sigmoid).astype(jnp.bfloat16)
            grad_gate = (
                grad_act * up_pre * sigmoid * (1.0 + gate_pre * (1.0 - sigmoid))
            ).astype(jnp.bfloat16)
            for first in range(0, width, chunk):
                window = slice(first, first + chunk)
                result = mul(active, vout[p, :, window], straight)
                back = mul(grad_gate, vin[p, 0, :, window], straight) + mul(
                    grad_up, vin[p, 1, :, window], straight
                )
                if p == 0:
                    result_acc[:, window] = result
                    input_acc[:, window] = back
                else:
                    result_acc[:, window] += result
                    input_acc[:, window] += back
                sums[p][0, :, window] += mul(grad_gate, rows_x[:, window], over_first)
                sums[p][1, :, window] += mul(grad_up, rows_x[:, window], over_first)
                sums[p][2, :, window] += mul(active, rows_g[:, window], over_first)
            if p == 0:
                turn(k, 1)

        @pl.when(k > 0)
        def _():
            pltpu.make_async_copy(sib_stage, sib_stage, sib_send.at[0]).wait()
            for j in range(2):
                pltpu.make_async_copy(res_stage.at[j], res_stage.at[j], res_sem.at[j]).wait()

        for other in range(2):
            j = 1 - core if other == 0 else core
            source = chip * 2 + j
            picks = jnp.where(picks_of(source), 1.0, 0.0).astype(jnp.bfloat16)
            window = pl.ds(pl.multiple_of(j * cap, cap), cap)
            back = mul(picks, input_acc[window, :].astype(jnp.bfloat16), over_first)
            if other == 0:
                sib_stage[...] = back.astype(jnp.bfloat16)
                pltpu.make_async_remote_copy(
                    src_ref=sib_stage,
                    dst_ref=sib.at[chip],
                    send_sem=sib_send.at[0],
                    recv_sem=sib_recv.at[chip],
                    device_id=sibling,
                    device_id_type=MESH,
                ).start()
            else:
                own[chip] = back.astype(jnp.bfloat16)
            rounded = result_acc[window, :].astype(jnp.bfloat16).astype(jnp.float32)
            weighted = (gate_col[window, 0:1] * rounded).astype(jnp.bfloat16)
            res_stage[other] = mul(picks, weighted, over_first).astype(jnp.bfloat16)
            pltpu.make_async_copy(res_stage.at[other], result_ref.at[source], res_sem.at[other]).start()
        turn(k, 2)
        return carry

    lax.fori_loop(0, 2 * na, work, 0)
    to_a(1)
    to_b(0)
    for p in range(1, parts):
        for q in range(3):
            if p > 1 or q > 0:
                pltpu.make_async_copy(stage, stage, stage_sem.at[0]).wait()
            stage[...] = sums[p][q].astype(jnp.bfloat16)
            pltpu.make_async_copy(stage, sent[p - 1].at[q], stage_sem.at[0]).start()
    to_a(3)
    chip = a * 2 + b
    sib_wait(chip)
    b_wait(0)
    add_into(routed_ref, [own.at[chip], sib.at[chip], bland.at[0]], jnp.float32)
    for r in range(1, na):
        other = chip_at(r)
        pltpu.make_async_copy(aland.at[other], aland.at[other], a_recv.at[other]).wait()
        add_into(routed_ref, [routed_ref, aland.at[other]], jnp.float32)
    for on, finish in ends:
        guarded(on, finish)
    for r in range(na):
        if r:
            sent_from_a(r)
            pltpu.make_async_copy(own.at[0], own.at[0], a_send.at[r]).wait()
        for copy in hop(me, 4 + 3 * (na - 1) + r, sibling):
            copy.wait_send()
        pltpu.make_async_copy(own.at[0], own.at[0], b_send.at[r]).wait()
    pltpu.make_async_copy(sib_stage, sib_stage, sib_send.at[0]).wait()
    for j in range(2):
        pltpu.make_async_copy(res_stage.at[j], res_stage.at[j], res_sem.at[j]).wait()
    pltpu.make_async_copy(stage, stage, stage_sem.at[0]).wait()


def fused_experts(ep_count, tp_count, collective_id, normed, info, cot_all, ins, outs_w, cap):
    place = Place(ep_count, tp_count)
    tok, width = normed.shape
    parts = len(ins)
    hidden = ins[0].shape[1]
    na, chips, rows = place.na, 2 * place.na, 2 * cap
    low = jnp.bfloat16
    anywhere = pl.BlockSpec(memory_space=pl.ANY)
    inside = pl.BlockSpec(memory_space=pltpu.VMEM)
    out_shape = [
        jax.ShapeDtypeStruct((ep_count, tok, width), low),
        jax.ShapeDtypeStruct((tok, width), jnp.float32),
        jax.ShapeDtypeStruct((3, hidden, width), jnp.float32),
    ] + [jax.ShapeDtypeStruct((3, hidden, width), low)] * (parts - 1)
    scratch = [
        pltpu.VMEM((ep_count, tok, width), low),
        pltpu.VMEM((ep_count, 2 * ep_count, tok), jnp.float32),
        pltpu.VMEM((2, 2, tok, width), low),
        pltpu.VMEM((parts, 2, hidden, width), low),
        pltpu.VMEM((parts, hidden, width), low),
        pltpu.VMEM((chips, tok, width), low),
        pltpu.VMEM((chips, tok, width), low),
        pltpu.VMEM((tok, width), low),
        pltpu.VMEM((na, tok, width), low),
        pltpu.VMEM((na, tok, width), low),
        pltpu.VMEM((2, tok, width), low),
        pltpu.VMEM((rows, width), low),
        pltpu.VMEM((rows, width), low),
        pltpu.VMEM((rows, 128), jnp.float32),
        pltpu.VMEM((rows, width), jnp.float32),
        pltpu.VMEM((rows, width), jnp.float32),
        pltpu.VMEM((hidden, width), low),
    ] + [pltpu.VMEM((3, hidden, width), jnp.float32)] * (parts - 1)
    dma = pltpu.SemaphoreType.DMA
    scratch += [
        dma((2, ep_count)), dma((2, 4 + 3 * (na - 1) + na)), dma((2 + 2 * parts,)), dma((2, 2)),
        dma((chips,)), dma((1,)), dma((na,)), dma((na,)), dma((na,)), dma((na,)), dma((2,)), dma((1,)),
    ]
    found = pl.pallas_call(
        functools.partial(fused_kernel, parts, ep_count, tp_count, cap),
        in_specs=[anywhere] * (3 + 2 * parts),
        out_specs=[anywhere, inside, inside] + [anywhere] * (parts - 1),
        out_shape=out_shape,
        scratch_shapes=scratch,
        compiler_params=pltpu.CompilerParams(
            collective_id=collective_id, has_side_effects=True, vmem_limit_bytes=VMEM_MOST
        ),
        name="fused_experts",
    )(normed, info, cot_all, *ins, *outs_w)
    return found[0], found[1], found[2], found[3:]


def adam_update(weight, gradient, first, second, clip_scale, rate, decay):
    clipped = gradient * clip_scale
    first_new = BETA_ONE * first + (1.0 - BETA_ONE) * clipped
    second_new = BETA_TWO * second + (1.0 - BETA_TWO) * clipped * clipped
    corr_one = 1.0 - BETA_ONE**STEP
    corr_two = 1.0 - BETA_TWO**STEP
    stepped = first_new / corr_one / (jnp.sqrt(second_new / corr_two) + ADAM_EPS)
    weight_new = weight - rate * (stepped + decay * weight)
    return (weight_new, first_new, second_new, weight_new.astype(jnp.bfloat16))


def per_device(
    tokens,
    cotangent,
    segments,
    routes,
    gates,
    qkv_weight,
    qkv_first,
    qkv_second,
    out_weight,
    out_first,
    out_second,
    shared_in,
    shared_in_first,
    shared_in_second,
    shared_out,
    shared_out_first,
    shared_out_second,
    expert_in,
    expert_in_first,
    expert_in_second,
    expert_out,
    expert_out_first,
    expert_out_second,
    norm_gains,
    gains_first,
    gains_second,
):
    tok_count = tokens.shape[0]
    width = tokens.shape[1]
    ep_count = lax.axis_size("ep")
    tp_count = lax.axis_size("tp")
    devices = ep_count * tp_count
    capacity = tok_count * 8 // ep_count
    low = jnp.bfloat16
    in_own, out_own = expert_in[0].astype(low), expert_out[0].astype(low)
    gain_columns = jnp.pad(norm_gains.T.astype(low), ((0, 0), (0, 126)))
    group = shared_out.shape[0]
    step = 16 * ((group + 15) // 16)
    while step & (step - 1):
        step += 16
    shout_own = jnp.pad(shared_out.astype(low), ((0, step - group), (0, 0)))
    qkv_low, out_low, gains_low, cot_all, in_others, out_others, shin_low, shout_low = gather(
        ep_count,
        tp_count,
        1,
        "gather_weights",
        [
            (("tab", "abt"), [qkv_weight.astype(low), out_weight.astype(low), gain_columns], 1.0),
            (("ab", "ba"), [cotangent], 0.92),
            ("t", [in_own, out_own], 1.0),
            (("tab", "atb"), [shared_in.astype(low), shout_own], 2.9),
        ],
    )
    qkv_low = qkv_low.reshape(width, 3 * width)
    out_low = out_low.reshape(width, width)
    shin_low = shin_low.reshape(width, 2 * FF)
    shout_low = shout_low.reshape(devices * step, width)
    gains = jnp.pad(gains_low.reshape(width, 128)[:, :2].T.astype(jnp.float32), ((0, 6), (0, 0)))
    ins_low = [in_own] + [in_others[s] for s in range(tp_count - 1)]
    outs_low = [out_own] + [out_others[s] for s in range(tp_count - 1)]
    expert_ids = jnp.arange(ep_count, dtype=jnp.int32)
    chosen = routes[:, :, None] == expert_ids[None, None, :]
    onehot = jnp.sum(chosen.astype(jnp.float32), axis=1)
    gate_of = jnp.sum(jnp.where(chosen, gates[:, :, None], 0.0), axis=1)
    earlier = jnp.tril(jnp.ones((tok_count, tok_count), low), -1)
    rank = jnp.dot(earlier, onehot.astype(low), preferred_element_type=jnp.float32)
    slot_of = jnp.where(onehot > 0.0, rank, -1.0)
    info_own = jnp.concatenate([slot_of, gate_of], axis=1).T
    qkv_act, attended, hidden, normed_two = attention_forward(
        tokens, segments, gains, qkv_low, out_low
    )
    chips = ep_count // 2
    held = tok_count * width * 2 * (ep_count + 3 * chips + 12) + 9 * tp_count * expert_in.size
    place = Place(ep_count, tp_count)
    if (place.na, place.nb) == (4, 2) and held <= VMEM_MOST * 9 // 10:
        result_part, routed_grad, own_grad, sent_grads = fused_experts(
            ep_count, tp_count, 3, normed_two, info_own, cot_all, ins_low, outs_low, capacity
        )
    else:
        normed_all, info_all = gather(
            ep_count, tp_count, 2, "gather_tokens", [("ab", [normed_two, info_own], 1.0)]
        )
        info = lax.dynamic_index_in_dim(
            info_all.reshape(ep_count, 2, ep_count, tok_count),
            lax.axis_index("ep"),
            axis=2,
            keepdims=False,
        )
        result_part, input_part, own_grad, sent_grads = expert_pass(
            normed_all, cot_all, info, ins_low, outs_low, capacity
        )
        (routed_grad,) = scatter_add(ep_count, tp_count, 3, "scatter_inputs", [("ab", [input_part])])
    sent = jnp.stack(sent_grads)
    lean = scatter_room(Place(ep_count, tp_count), "ab", [result_part]) <= VMEM_MOST // 3
    base, tokens_grad, gain_grads, qkv_grad, out_grad, shin_grad, shout_grad, *carried = dense_backward(
        group, step, tokens, cotangent, segments, gains, qkv_act, attended, hidden, normed_two,
        routed_grad, qkv_low, out_low, shin_low, shout_low, ep_count, tp_count, 9, "ab",
        result_part if lean else None, sent,
    )
    own_gains = norm_gains.shape[1]
    gain_rows = gain_grads[:2].astype(low).reshape(2, devices, own_gains).transpose(1, 0, 2)
    gain_rows = jnp.pad(gain_rows, ((0, 0), (0, 14), (0, 128 - own_gains)))

    def by_owner(grad):
        return grad.reshape(devices, -1, grad.shape[1])

    scattered = [
        (("abt", "tab"), [by_owner(qkv_grad), by_owner(out_grad), gain_rows]),
        (("abt", "bta"), [by_owner(shin_grad), by_owner(shout_grad)]),
    ]
    if lean:
        routed, others = carried
        qkv_part, out_part, gains_part, shin_part, shout_part, own_grad, norm = scatter_add(
            ep_count, tp_count, 4, "scatter_weights", scattered, (own_grad, others)
        )
    else:
        scattered += [("ab", [result_part]), ("t", [sent])]
        qkv_part, out_part, gains_part, shin_part, shout_part, routed, others = scatter_all(
            ep_count, tp_count, (4, 6, 7, 8), "scatter_weights", scattered
        )
        for shift in range(tp_count - 1):
            own_grad = own_grad + others[shift].astype(jnp.float32)
        extra = jnp.sum(own_grad * own_grad, axis=(0, 1))[None, :]
        norm = sum_of_squares(
            ep_count, tp_count, 5, [qkv_part, out_part, gains_part, shin_part, shout_part], extra
        )
        norm = jnp.broadcast_to(jnp.sqrt(norm), (8, 128))
    grad_norm = norm[0, 0]
    block_out = (base + routed).astype(low)
    clip_scale = jnp.minimum(1.0, CLIP_LEVEL / (grad_norm + 1e-06))
    exin = adam_update(
        expert_in, own_grad[None, :2], expert_in_first, expert_in_second, clip_scale, MATRIX_RATE, WEIGHT_DECAY
    )
    exout = adam_update(
        expert_out, own_grad[2:], expert_out_first, expert_out_second, clip_scale, MATRIX_RATE, WEIGHT_DECAY
    )
    dense = adam_dense(
        norm,
        [
            (qkv_weight, qkv_first, qkv_second, qkv_part),
            (out_weight, out_first, out_second, out_part),
            (shared_in, shared_in_first, shared_in_second, shin_part),
            (shared_out, shared_out_first, shared_out_second, shout_part),
            (norm_gains, gains_first, gains_second, gains_part),
        ],
    )
    qkv_all, out_all, shin_all, shout_all, gains_all = dense
    return (
        block_out, tokens_grad, grad_norm, *qkv_all, *out_all, *shin_all, *shout_all, *exin, *exout, *gains_all
    )


def solution(mesh):
    placed = (
        P(("ep", "tp"), None),
        P(("ep", "tp"), None),
        P(("ep", "tp"), None),
        P(("ep", "tp"), None),
        P(("ep", "tp"), None),
        P(("ep", "tp"), None),
        P(("ep", "tp"), None),
        P(("ep", "tp"), None),
        P(("ep", "tp"), None),
        P(("ep", "tp"), None),
        P(("ep", "tp"), None),
        P(("ep", "tp"), None),
        P(("ep", "tp"), None),
        P(("ep", "tp"), None),
        P(("ep", "tp"), None),
        P(("ep", "tp"), None),
        P(("ep", "tp"), None),
        P("ep", None, "tp", None),
        P("ep", None, "tp", None),
        P("ep", None, "tp", None),
        P("ep", "tp", None),
        P("ep", "tp", None),
        P("ep", "tp", None),
        P(None, ("ep", "tp")),
        P(None, ("ep", "tp")),
        P(None, ("ep", "tp")),
    )
    return jax.shard_map(
        per_device,
        mesh=mesh,
        in_specs=placed,
        out_specs=(
            P(("ep", "tp"), None),
            P(("ep", "tp"), None),
            P(),
            P(("ep", "tp"), None),
            P(("ep", "tp"), None),
            P(("ep", "tp"), None),
            P(("ep", "tp"), None),
            P(("ep", "tp"), None),
            P(("ep", "tp"), None),
            P(("ep", "tp"), None),
            P(("ep", "tp"), None),
            P(("ep", "tp"), None),
            P(("ep", "tp"), None),
            P(("ep", "tp"), None),
            P(("ep", "tp"), None),
            P(("ep", "tp"), None),
            P(("ep", "tp"), None),
            P(("ep", "tp"), None),
            P(("ep", "tp"), None),
            P("ep", None, "tp", None),
            P("ep", None, "tp", None),
            P("ep", None, "tp", None),
            P("ep", None, "tp", None),
            P("ep", "tp", None),
            P("ep", "tp", None),
            P("ep", "tp", None),
            P("ep", "tp", None),
            P(None, ("ep", "tp")),
            P(None, ("ep", "tp")),
            P(None, ("ep", "tp")),
            P(None, ("ep", "tp")),
        ),
        check_vma=False,
    )
```
